32 devices in a mesh: wide: 16 (over z, y, x), narrow: 2 (over core).
Axes of the slice: x: 2, y: 2, z: 4, core: 2. Of those that a mesh axis runs over, the one named last changes fastest.
Arguments:
- particle_position: float32 [3, 256, 128], P(None, ('wide', 'narrow')), may hold values from -6 to 6
- particle_velocity: float32 [3, 256, 128], P(None, ('wide', 'narrow')), may hold values from -6 to 6
- radius: float32 [256, 128], P(('wide', 'narrow')), may hold values from 0.4 to 1
- block_live_count: int32 [256], P(('wide', 'narrow')), may hold values from 64 to 128
- cell_index: int32 [256, 128], P(('wide', 'narrow')), may hold values from 0 to 8191
- block_offset: int32 [256], P(('wide', 'narrow')), may hold values from -2 to 2, as said below
- neighbours: int32 [256, 6], P(('wide', 'narrow')), may hold values from 0 to 7, as said below
- gas_velocity: float32 [3, 128, 16, 128], P(None, 'wide', 'narrow'), may hold values from -6 to 6
- pressure_source: float32 [128, 16, 128], P('wide', 'narrow'), may hold values from -6 to 6
- void_before: float32 [128, 16, 128], P('wide', 'narrow'), may hold values from 0.6 to 1
Outputs:
- pressure: float32 [128, 16, 128], P('wide', 'narrow')
- gas_next: float32 [3, 128, 16, 128], P(None, 'wide', 'narrow')
- updated_particle_velocity: float32 [3, 256, 128], P(None, ('wide', 'narrow'))
The draws below stay inside these ranges and needn't reach their ends.
Inputs may be any that keep to these rules, and one draw needn't show every extreme that they name: For a block held at index w along wide, w + block_offset lies in 0 to 15. At most 3 blocks of one device share one offset, and on every device some offset has exactly 3. `neighbours`: each block lists 6 different blocks of its own device, never itself.
All inputs are finite; a program needn't handle non-finite values.
Results may differ from the reference program's by a relative error of at most 0.0003.
Values sent between devices are 32-bit elements; how exact they have to be, the bound alone decides.
No kernel may reach another device: no remote copies, remote signals or barrier semaphores. Data moves between devices by JAX's collectives and lax.ppermute only.
A program may use at most 128 MiB of HBM per device.

```python
import math
import jax
import jax.numpy as jnp
from jax import lax

NX = 128
CZ = 8
CY = 8
PARTICLE_SLOTS = 128
BLOCKS_PER_CHIPSET = 8
NEIGHBOUR_COUNT = 6
SPREAD = 2
LEVELS = 4
SWEEPS = 2
COARSE_SWEEPS = 4
CAP = 3
NZ = 128
NY = 16
BLOCKS = 256
N_WIDE = 16
N_NARROW = 2


def draw_block_offset(key, part):
    block_groups = N_WIDE * N_NARROW
    choices_total = 2 * SPREAD + 1
    slot_total = choices_total * CAP
    first_key, second_key, third_key = jax.random.split(jax.random.fold_in(key, 11), 3)
    holder = (jnp.arange(block_groups, dtype=jnp.int32) // N_NARROW)[:, None]
    offsets = jnp.arange(choices_total, dtype=jnp.int32) - SPREAD
    allowed = jnp.logical_and(holder + offsets[None, :] >= 0, holder + offsets[None, :] < N_WIDE)
    pick_score = jax.random.randint(first_key, (block_groups, choices_total), 0, 1024) * choices_total + jnp.arange(choices_total, dtype=jnp.int32)[None, :]
    pick_score = jnp.where(allowed, pick_score, 1 << 28)
    filled = jnp.argmin(pick_score, axis=1).astype(jnp.int32)
    slot_group = jnp.arange(slot_total, dtype=jnp.int32) // CAP
    slot_allowed = allowed[:, slot_group]
    priority = jax.random.randint(second_key, (block_groups, slot_total), 0, 1024) * slot_total + jnp.arange(slot_total, dtype=jnp.int32)[None, :] + slot_total
    priority = jnp.where(slot_group[None, :] == filled[:, None], jnp.arange(slot_total, dtype=jnp.int32)[None, :], priority)
    priority = jnp.where(slot_allowed, priority, priority + (1 << 28))
    order = jnp.argsort(priority, axis=1)[:, :BLOCKS_PER_CHIPSET]
    chosen_offset = slot_group[order] - SPREAD
    shuffle_score = jax.random.randint(third_key, (block_groups, BLOCKS_PER_CHIPSET), 0, 1024) * BLOCKS_PER_CHIPSET + jnp.arange(BLOCKS_PER_CHIPSET, dtype=jnp.int32)[None, :]
    shuffle = jnp.argsort(shuffle_score, axis=1)
    return jnp.take_along_axis(chosen_offset, shuffle, axis=1).reshape(-1).astype(jnp.int32)


def draw_neighbours(key, part):
    others = BLOCKS_PER_CHIPSET - 1
    score = jax.random.randint(jax.random.fold_in(key, 23), (BLOCKS, others), 0, 4096) * others + jnp.arange(others, dtype=jnp.int32)[None, :]
    picked = jnp.argsort(score, axis=1)[:, :NEIGHBOUR_COUNT].astype(jnp.int32)
    local_index = (jnp.arange(BLOCKS, dtype=jnp.int32) % BLOCKS_PER_CHIPSET)[:, None]
    return ((local_index + 1 + picked) % BLOCKS_PER_CHIPSET).astype(jnp.int32)


def set_ends(drawn, stream_key, least, top_value):
    dims = drawn.shape
    index_at = [jax.random.randint(jax.random.fold_in(stream_key, axis), (), 0, dims[axis]) for axis in range(len(dims))]
    drawn = drawn.at[tuple(index_at)].set(least)
    longest = dims.index(max(dims))
    index_at[longest] = (index_at[longest] + 1) % dims[longest]
    return drawn.at[tuple(index_at)].set(top_value)


def level_of(stream_key, dims, pieces, low, top_value):
    def one(axis_at, blocks):
        draws = jax.random.uniform(jax.random.fold_in(jax.random.fold_in(stream_key, 6), axis_at), (blocks,), jnp.float32, low / len(pieces), top_value / len(pieces))
        return jnp.repeat(jnp.exp(draws), dims[axis_at] // blocks).reshape((-1,) + (1,) * (len(dims) - axis_at - 1))

    level = one(*pieces[0])
    for cut in pieces[1:]:
        level = level * one(*cut)
    return level


def normal_values(key, dims, spread, bound, cuts=(), kind=jnp.bfloat16):
    loudness = level_of(key, dims, cuts, -0.22, 0.18) if cuts else 1.0
    result = jax.random.normal(key, dims, jnp.float32) * spread * loudness
    return jnp.minimum(jnp.maximum(result, -bound), bound).astype(kind)


def setup_inputs(seed: int = 0) -> dict:
    key_list = jax.random.split(jax.random.key(seed), 11)
    return {
        "particle_position": normal_values(key_list[0], (3, BLOCKS, PARTICLE_SLOTS), 1.0, 6.0, ((1, 32),), jnp.float32),
        "particle_velocity": normal_values(key_list[1], (3, BLOCKS, PARTICLE_SLOTS), 1.0, 6.0, ((1, 32),), jnp.float32),
        "radius": jnp.clip(jnp.exp(math.log(1.0) - 0.9162907 * jax.random.uniform(key_list[2], (BLOCKS, PARTICLE_SLOTS), jnp.float32) ** level_of(key_list[2], (BLOCKS, PARTICLE_SLOTS), ((0, 32),), -0.2, 0.2)), 0.4, 1.0),
        "block_live_count": set_ends(jax.random.randint(key_list[3], (BLOCKS,), PARTICLE_SLOTS // 2, PARTICLE_SLOTS + 1), jax.random.fold_in(key_list[3], 1), PARTICLE_SLOTS // 2, PARTICLE_SLOTS).astype(jnp.int32),
        "cell_index": set_ends(jax.random.randint(key_list[4], (BLOCKS, PARTICLE_SLOTS), 0, CZ * CY * NX), jax.random.fold_in(key_list[4], 1), 0, (CZ * CY * NX) - 1).astype(jnp.int32),
        "block_offset": draw_block_offset(jax.random.fold_in(key_list[10], 71), 0),
        "neighbours": draw_neighbours(jax.random.fold_in(key_list[10], 71), 0),
        "gas_velocity": normal_values(key_list[7], (3, NZ, NY, NX), 1.0, 6.0, ((1, 16), (2, 2)), jnp.float32),
        "pressure_source": normal_values(key_list[8], (NZ, NY, NX), 1.0, 6.0, ((0, 16), (1, 2)), jnp.float32),
        "void_before": jnp.clip(0.6 + 0.39999998 * jax.random.uniform(key_list[9], (NZ, NY, NX), jnp.float32) ** level_of(key_list[9], (NZ, NY, NX), ((0, 16), (1, 2)), -0.2, 0.2), 0.6, 1.0),
    }


relax_weight = 0.8
solid_most = 0.6
void_power = 2.65
drag_base = 0.5
drag_slope = 0.5
stiffness = 16.0
softening = 0.1
particle_density = 2.0
gas_density = 1.0
step_duration = 0.25
gravity = -1.0

def restrict(grid_field):
    depth_cells, lane_cells, width_cells = grid_field.shape
    return grid_field.reshape(depth_cells // 2, 2, lane_cells // 2, 2, width_cells // 2, 2).mean(axis=(1, 3, 5))

def prolong(grid_field):
    return jnp.repeat(jnp.repeat(jnp.repeat(grid_field, 2, axis=0), 2, axis=1), 2, axis=2)

def coefs_from_padded(padded, weight):
    middle = padded[1:-1, 1:-1, 1:-1]
    couplings = (0.5 * weight * (middle + padded[:-2, 1:-1, 1:-1]), 0.5 * weight * (middle + padded[2:, 1:-1, 1:-1]), 0.5 * weight * (middle + padded[1:-1, :-2, 1:-1]), 0.5 * weight * (middle + padded[1:-1, 2:, 1:-1]), 0.5 * weight * (middle + padded[1:-1, 1:-1, :-2]), 0.5 * weight * (middle + padded[1:-1, 1:-1, 2:]))
    diagonal = couplings[0] + couplings[1] + couplings[2] + couplings[3] + couplings[4] + couplings[5]
    return (couplings, diagonal)

def apply_padded(padded, couplings, diagonal):
    middle = padded[1:-1, 1:-1, 1:-1]
    beside = couplings[0] * padded[:-2, 1:-1, 1:-1] + couplings[1] * padded[2:, 1:-1, 1:-1]
    beside = beside + couplings[2] * padded[1:-1, :-2, 1:-1] + couplings[3] * padded[1:-1, 2:, 1:-1]
    beside = beside + couplings[4] * padded[1:-1, 1:-1, :-2] + couplings[5] * padded[1:-1, 1:-1, 2:]
    return diagonal * middle - beside

def pad_plain(grid_field):
    return jnp.pad(grid_field, 1)

def unchanged(grid_field):
    return grid_field

def cycle(right_side, levels, level_index):
    couplings, diagonal, padder, enter_level, leave_level = levels[level_index]
    right_side = enter_level(right_side)
    coarsest = level_index == len(levels) - 1
    sweep_total = COARSE_SWEEPS if coarsest else SWEEPS
    iterate = relax_weight * right_side / diagonal
    for sweep_index in range(sweep_total - 1):
        iterate = iterate + relax_weight * (right_side - apply_padded(padder(iterate), couplings, diagonal)) / diagonal
    if not coarsest:
        residual = right_side - apply_padded(padder(iterate), couplings, diagonal)
        iterate = iterate + prolong(cycle(restrict(residual), levels, level_index + 1))
        for sweep_index in range(SWEEPS):
            iterate = iterate + relax_weight * (right_side - apply_padded(padder(iterate), couplings, diagonal)) / diagonal
    return leave_level(iterate)

def pressure_gradient(padded):
    return jnp.stack([0.5 * (padded[2:, 1:-1, 1:-1] - padded[:-2, 1:-1, 1:-1]), 0.5 * (padded[1:-1, 2:, 1:-1] - padded[1:-1, :-2, 1:-1]), 0.5 * (padded[1:-1, 1:-1, 2:] - padded[1:-1, 1:-1, :-2])])

def pairwise_force(local_positions, local_radii, local_live_mask, there_pos, there_rad, there_live):
    apart_z = local_positions[0][:, :, None] - there_pos[0][:, None, :]
    apart_y = local_positions[1][:, :, None] - there_pos[1][:, None, :]
    apart_x = local_positions[2][:, :, None] - there_pos[2][:, None, :]
    distance = jnp.sqrt(apart_z * apart_z + apart_y * apart_y + apart_x * apart_x + softening * softening)
    intersection = jnp.maximum(local_radii[:, :, None] + there_rad[:, None, :] - distance, 0.0)
    weight = intersection * there_live[:, None, :] / distance
    return local_live_mask[None] * jnp.stack([lax.optimization_barrier(jnp.sum(apart_z * weight, axis=2)), lax.optimization_barrier(jnp.sum(apart_y * weight, axis=2)), lax.optimization_barrier(jnp.sum(apart_x * weight, axis=2))])

def block_contact_forces(slot_positions, slot_radii, live_flags, adjacent_blocks):
    block_count = slot_radii.shape[0]
    batch_extent = math.gcd(block_count, 8)
    factor = stiffness / (slot_radii.shape[1] * (adjacent_blocks.shape[1] + 1))

    def one_batch(batch_index):
        leading_row = batch_index * batch_extent
        local_positions = lax.dynamic_slice_in_dim(slot_positions, leading_row, batch_extent, 1)
        local_radii = lax.dynamic_slice_in_dim(slot_radii, leading_row, batch_extent, 0)
        local_live_mask = lax.dynamic_slice_in_dim(live_flags, leading_row, batch_extent, 0)
        near_list = lax.dynamic_slice_in_dim(adjacent_blocks, leading_row, batch_extent, 0)
        total_force_sum = pairwise_force(local_positions, local_radii, local_live_mask, local_positions, local_radii, local_live_mask)
        for column in range(adjacent_blocks.shape[1]):
            selected_blocks = near_list[:, column]
            total_force_sum = total_force_sum + pairwise_force(local_positions, local_radii, local_live_mask, slot_positions[:, selected_blocks], slot_radii[selected_blocks], live_flags[selected_blocks])
        return total_force_sum * factor
    stacked = lax.map(one_batch, jnp.arange(block_count // batch_extent, dtype=jnp.int32))
    return stacked.transpose(1, 0, 2, 3).reshape(3, block_count, -1)

def reference(particle_position, particle_velocity, radius, block_live_count, cell_index, block_offset, neighbours, gas_velocity, pressure_source, void_before):
    slot_index_list = jnp.arange(PARTICLE_SLOTS, dtype=jnp.int32)
    live_flags = (slot_index_list[None, :] < block_live_count[:, None]).astype(jnp.float32)
    particle_volume = radius * radius * radius
    volume_live_mask = particle_volume * live_flags
    owner_index = jnp.arange(BLOCKS, dtype=jnp.int32) // BLOCKS_PER_CHIPSET
    home_slab = owner_index // N_NARROW + block_offset
    lateral = owner_index % N_NARROW
    height = home_slab[:, None] * CZ + cell_index // (CY * NX)
    across = lateral[:, None] * CY + cell_index // NX % CY
    flat_cell = ((height * NY + across) * NX + cell_index % NX).reshape(-1).astype(jnp.int32)
    total_cells = NZ * NY * NX
    vol_flat = volume_live_mask.reshape(-1)
    solid_sum = jnp.zeros((total_cells,), jnp.float32).at[flat_cell].add(vol_flat)
    voidage = 1.0 - solid_most * solid_sum / (1.0 + solid_sum)
    slip_vel = gas_velocity.reshape(3, -1)[:, flat_cell] - particle_velocity.reshape(3, -1)
    slip_speed = jnp.sqrt(lax.optimization_barrier(jnp.sum(slip_vel * slip_vel, axis=0)))
    drag_force = (vol_flat * (drag_base + drag_slope * slip_speed) * voidage[flat_cell] ** (-void_power))[None] * slip_vel
    reaction = jnp.zeros((3, total_cells), jnp.float32).at[:, flat_cell].add(-drag_force)
    voidage_grid = voidage.reshape(NZ, NY, NX)
    right_side = pressure_source + (void_before - voidage_grid) / step_duration
    levels = []
    coarse = voidage_grid
    for level_index in range(LEVELS):
        if level_index > 0:
            coarse = restrict(coarse)
        couplings, diagonal = coefs_from_padded(pad_plain(coarse), 0.25 ** level_index)
        levels.append((couplings, diagonal, pad_plain, unchanged, unchanged))
    pressure = cycle(right_side, levels, 0)
    gradient = pressure_gradient(pad_plain(pressure))
    gas_next = gas_velocity + step_duration * (reaction.reshape(3, NZ, NY, NX) / (gas_density * voidage_grid)[None] - gradient / gas_density)
    fluid_force = drag_force - vol_flat[None] * gradient.reshape(3, -1)[:, flat_cell]
    block_groups = N_WIDE * N_NARROW
    position_groups = particle_position.reshape(3, block_groups, BLOCKS_PER_CHIPSET, PARTICLE_SLOTS).transpose(1, 0, 2, 3)

    def single_group(inputs):
        return block_contact_forces(inputs[0], inputs[1], inputs[2], inputs[3])
    contact_force = lax.map(single_group, (position_groups, radius.reshape(block_groups, BLOCKS_PER_CHIPSET, PARTICLE_SLOTS), live_flags.reshape(block_groups, BLOCKS_PER_CHIPSET, PARTICLE_SLOTS), neighbours.reshape(block_groups, BLOCKS_PER_CHIPSET, NEIGHBOUR_COUNT)))
    contact_force = contact_force.transpose(1, 0, 2, 3).reshape(3, BLOCKS, PARTICLE_SLOTS)
    downward = jnp.array([gravity, 0.0, 0.0], jnp.float32)[:, None, None]
    particle_acceleration = (contact_force + fluid_force.reshape(3, BLOCKS, PARTICLE_SLOTS)) / (particle_density * particle_volume)[None] + downward
    updated_particle_velocity = live_flags[None] * (particle_velocity + step_duration * particle_acceleration)
    return (pressure, gas_next, updated_particle_velocity)
```

```python
import functools

import jax
import jax.numpy as jnp
from jax import lax
from jax.experimental import pallas as pl
from jax.experimental.pallas import tpu as pltpu
from jax.sharding import PartitionSpec as P

SPREAD = 2
SWEEPS = 2
COARSE_SWEEPS = 4
CAP = 3
GROUPS = 2 * SPREAD + 1
HALO = 5
REACH = 4

relax_weight = 0.8
solid_most = 0.6
void_power = 2.65
drag_base = 0.5
drag_slope = 0.5
stiffness = 16.0
softening = 0.1
particle_density = 2.0
gas_density = 1.0
step_duration = 0.25
gravity = -1.0

F32 = jnp.float32
BF16 = jnp.bfloat16
VMEM = pl.BlockSpec(memory_space=pltpu.VMEM)
SMEM = pl.BlockSpec(memory_space=pltpu.SMEM)
HIGHEST = lax.Precision.HIGHEST
VOL_ROW = 0
CELL_ROW = 3 * CAP
VEL_ROW = 6 * CAP
SOURCE_ROW = 32
VMEM_LIMIT = 60 * 1024 * 1024


def call(kernel, out_shape, in_specs, out_specs, scratch=(), flops=0):
    return pl.pallas_call(
        kernel,
        out_shape=out_shape,
        in_specs=in_specs,
        out_specs=out_specs,
        scratch_shapes=list(scratch),
        compiler_params=pltpu.CompilerParams(vmem_limit_bytes=VMEM_LIMIT),
        cost_estimate=pl.CostEstimate(flops=flops, bytes_accessed=1 << 18, transcendentals=0),
    )


def f32s(*shape):
    return jax.ShapeDtypeStruct(shape, F32)


def iota(shape, dim):
    return lax.broadcasted_iota(jnp.int32, shape, dim)


def back(value, step, axis):
    return pltpu.roll(value, step, axis)


def ahead(value, step, axis):
    return pltpu.roll(value, value.shape[axis] - step, axis)


def ranks(offset_ref, count):
    offsets = [offset_ref[i] for i in range(count)]
    found = []
    for i in range(count):
        rank = jnp.int32(0)
        for j in range(i):
            rank = rank + jnp.where(offsets[j] == offsets[i], 1, 0)
        found.append(rank)
    return offsets, found


def pack_kernel(wide, offset_ref, count_ref, radius_ref, vel_ref, cell_ref, source_ref, before_ref, send_ref, s_ref):
    w = lax.axis_index("wide")
    blocks, slots = radius_ref.shape
    depth, lanes, _ = source_ref.shape
    send_ref[...] = jnp.zeros(send_ref.shape, F32)
    offsets, rank = ranks(offset_ref, blocks)
    slot = iota((1, slots), 1)
    for b in range(blocks):
        radius = radius_ref[b : b + 1, :]
        vol = jnp.where(slot < count_ref[b], radius * radius * radius, 0.0)
        cell = cell_ref[b : b + 1, :].astype(F32)
        for e in (-1, 0, 1):
            target = w + offsets[b] - e

            @pl.when(jnp.logical_and(target >= 0, target < wide))
            def _():
                row = (e + 1) * CAP + rank[b]
                send_ref[target, pl.ds(VOL_ROW + row, 1), :] = vol
                send_ref[target, pl.ds(CELL_ROW + row, 1), :] = cell
                if e == 0:
                    for c in range(3):
                        send_ref[target, pl.ds(VEL_ROW + c * CAP + rank[b], 1), :] = vel_ref[c, b : b + 1, :]

    for z in range(depth):
        s_ref[z] = source_ref[z] + before_ref[z] * (1.0 / step_duration)

    @pl.when(w + 1 < wide)
    def _():
        for z in range(REACH):
            send_ref[w + 1, SOURCE_ROW + z * lanes : SOURCE_ROW + (z + 1) * lanes, :] = s_ref[depth - REACH + z]

    @pl.when(w > 0)
    def _():
        for z in range(REACH):
            send_ref[w - 1, SOURCE_ROW + z * lanes : SOURCE_ROW + (z + 1) * lanes, :] = s_ref[z]


def cell_rows(cell_row):
    cell = cell_row.astype(jnp.int32)
    return cell >> 7, cell & 127


def pieces_of(value):
    high = value.astype(BF16).astype(F32)
    return high, value - high


def contract(lhs, rhs):
    return lax.dot_general(lhs, rhs, (((1,), (1,)), ((), ())), preferred_element_type=F32)


def solid_of(vols, cells, first, rows):
    total = jnp.zeros((2 * rows, 128), F32)
    place = iota((rows, 128), 0) + first
    column = iota((128, 128), 0)
    for pair in range(0, len(vols), 2):
        left, right = [], []
        for k in range(pair, min(pair + 2, len(vols))):
            zy, x = cell_rows(cells[k])
            here = place == zy
            high, low = pieces_of(vols[k])
            left.append(
                jnp.concatenate([jnp.where(here, high, 0.0), jnp.where(here, low, 0.0)], axis=0).astype(BF16)
            )
            right.append(jnp.where(column == x, 1.0, 0.0).astype(BF16))
        total = total + contract(jnp.concatenate(left, axis=1), jnp.concatenate(right, axis=1))
    return total[:rows] + total[rows:]


def void_kernel(wide, recv_ref, s_ref, window_ref, rows_ref):
    w = lax.axis_index("wide")
    depth, lanes, _ = s_ref.shape
    cells = depth * lanes
    rows_ref[...] = jnp.zeros(rows_ref.shape, F32)
    for e in (-1, 0, 1):
        vols, codes = [], []
        for g in range(GROUPS):
            source = w + e - (g - SPREAD)
            inside = jnp.logical_and(source >= 0, source < wide)
            source = jnp.clip(source, 0, wide - 1)
            row = (e + 1) * CAP
            for r in range(CAP):
                k = g * CAP + r
                vol = jnp.where(inside, recv_ref[source, VOL_ROW + row + r : VOL_ROW + row + r + 1, :], 0.0)
                code = recv_ref[source, CELL_ROW + row + r : CELL_ROW + row + r + 1, :]
                vols.append(vol)
                codes.append(code)
                if e == 0:
                    rows_ref[0, k : k + 1, :] = vol
                    rows_ref[1, k : k + 1, :] = code
                    for c in range(3):
                        at = VEL_ROW + c * CAP + r
                        rows_ref[2 + c, k : k + 1, :] = recv_ref[source, at : at + 1, :]
        low = depth - HALO if e < 0 else 0
        layers = depth if e == 0 else HALO
        first = 0 if e >= 0 else (low * lanes) // 16 * 16
        count = cells if e == 0 else -(-(layers * lanes + (low * lanes - first)) // 16) * 16
        solid = solid_of(vols, codes, first, count)
        void = 1.0 - solid_most * solid / (1.0 + solid)
        exists = jnp.logical_and(w + e >= 0, w + e < wide)
        void = jnp.where(exists, void, 0.0)
        base = HALO + (e * HALO if e < 0 else e * depth)
        for z in range(layers):
            start = (low + z) * lanes - first
            window_ref[base + z] = void[start : start + lanes]
    voids = depth + 2 * HALO
    for z in range(depth):
        window_ref[voids + REACH + z] = s_ref[z]
    for e in (-1, 1):
        beside = w + e
        exists = jnp.logical_and(beside >= 0, beside < wide)
        beside = jnp.clip(beside, 0, wide - 1)
        for z in range(REACH):
            part = recv_ref[beside, SOURCE_ROW + z * lanes : SOURCE_ROW + (z + 1) * lanes, :]
            at = voids + (z if e < 0 else REACH + depth + z)
            window_ref[at] = jnp.where(exists, part, 0.0)


def gather_cells(refs, zy, x, rows):
    found = [jnp.zeros(zy.shape, F32) for _ in refs]
    for row in range(rows):
        here = zy == row
        for i, ref in enumerate(refs):
            source = jnp.broadcast_to(ref(row), zy.shape)
            found[i] = jnp.where(here, jnp.take_along_axis(source, x, axis=1), found[i])
    return found


def drag_kernel(window_ref, rows_ref, gas_ref, drag_ref, base_ref):
    _, depth, lanes, _ = gas_ref.shape
    cells = depth * lanes
    vol = rows_ref[0]
    zy, x = cell_rows(rows_ref[1])

    def table(c):
        return lambda row: gas_ref[c, row // lanes, row % lanes : row % lanes + 1, :]

    def voids(row):
        return window_ref[HALO + row // lanes, row % lanes : row % lanes + 1, :]

    gas_z, gas_y, gas_x, void = gather_cells([table(0), table(1), table(2), voids], zy, x, cells)
    slips = [gas_z - rows_ref[2], gas_y - rows_ref[3], gas_x - rows_ref[4]]
    speed = jnp.sqrt(slips[0] * slips[0] + slips[1] * slips[1] + slips[2] * slips[2])
    scale = vol * (drag_base + drag_slope * speed) * jnp.exp(-void_power * jnp.log(void))
    drags = [scale * slip for slip in slips]
    for c in range(3):
        drag_ref[c] = drags[c]
    split = []
    for c in range(3):
        split += list(pieces_of(drags[c]))
    total = jnp.zeros((6 * cells, 128), F32)
    place = iota((cells, 128), 0)
    column = iota((128, 128), 0)
    for pair in range(0, vol.shape[0], 2):
        left, right = [], []
        for k in range(pair, pair + 2):
            here = place == zy[k : k + 1]
            left.append(
                jnp.concatenate([jnp.where(here, part[k : k + 1], 0.0) for part in split], axis=0).astype(BF16)
            )
            right.append(jnp.where(column == x[k : k + 1], 1.0, 0.0).astype(BF16))
        total = total + contract(jnp.concatenate(left, axis=1), jnp.concatenate(right, axis=1))
    for z in range(depth):
        per_void = step_duration / (gas_density * window_ref[HALO + z])
        for c in range(3):
            start = 2 * c * cells + z * lanes
            given = total[start : start + lanes] + total[start + cells : start + cells + lanes]
            base_ref[c, z] = gas_ref[c, z] - per_void * given


def fill_window(pieces, spots, lanes, void_ref, source_ref):
    voids = void_ref.shape[0]
    for piece, spot in zip(pieces, spots):
        at = pl.ds(spot * lanes if isinstance(spot, int) else pl.multiple_of(spot * lanes, lanes), lanes)
        for z in range(voids):
            void_ref[z, at, :] = piece[z]
        for z in range(source_ref.shape[0]):
            source_ref[z, at, :] = piece[voids + z]


def side_masks(lanes, width):
    y, x = iota((lanes, width), 0), iota((lanes, width), 1)
    return (y >= 1, y < lanes - 1, x >= 1, x < width - 1)


def sides(value, masks, step_y, step_x):
    return (
        jnp.where(masks[0], back(value, step_y, 0), 0.0),
        jnp.where(masks[1], ahead(value, step_y, 0), 0.0),
        jnp.where(masks[2], back(value, step_x, 1), 0.0),
        jnp.where(masks[3], ahead(value, step_x, 1), 0.0),
    )


def fine_start(void_ref, source_ref, coef_ref, diag_ref, first_ref):
    layers, lanes, width = source_ref.shape
    masks = side_masks(lanes, width)
    for i in range(layers):
        p = void_ref[i + 1]
        around = (void_ref[i], void_ref[i + 2]) + sides(p, masks, 1, 1)
        sums = [p + q for q in around]
        diag = sums[0] + sums[1] + sums[2] + sums[3] + sums[4] + sums[5]
        inside = p > 0.0
        inverse = jnp.where(inside, relax_weight / jnp.where(inside, diag, 1.0), 0.0)
        for k in range(6):
            coef = sums[k] * inverse
            if k >= 2:
                coef = jnp.where(masks[k - 2], coef, 0.0)
            coef_ref[k, i] = coef
        if diag_ref is not None:
            diag_ref[i] = diag * (0.5 / relax_weight)
        first_ref[i] = (source_ref[i] - p * (1.0 / step_duration)) * inverse * 2.0


def pull(coef_ref, i, below, here, above, step_y=1, step_x=1):
    total = coef_ref[0, i] * below + coef_ref[1, i] * above
    total = total + coef_ref[2, i] * back(here, step_y, 0) + coef_ref[3, i] * ahead(here, step_y, 0)
    return total + coef_ref[4, i] * back(here, step_x, 1) + coef_ref[5, i] * ahead(here, step_x, 1)


def fine_sweep(coef_ref, first_ref, old_ref, new_ref, start, stop):
    for i in range(start, stop):
        here = old_ref[i]
        new_ref[i] = (
            (1.0 - relax_weight) * here
            + first_ref[i]
            + pull(coef_ref, i, old_ref[i - 1], here, old_ref[i + 1])
        )


def spread_matrix(rows, columns, shift):
    return jnp.where(iota((rows, columns), 1) // 2 + shift == iota((rows, columns), 0), 1.0, 0.0)


def mean_matrix(width, shift):
    return jnp.where(iota((width, width), 0) // 2 + shift == iota((width, width), 1), 0.125, 0.0)


def coarsen_kernel(wide, *refs):
    *pieces, send_ref, void_ref, source_ref, coef_ref, diag_ref, first_ref, next_ref, fold_ref = refs
    narrow = len(pieces)
    lanes = pieces[0].shape[1]
    n = lax.axis_index("narrow")
    spots = [n, 1 - n] if narrow == 2 else list(range(narrow))
    fill_window(pieces, spots, lanes, void_ref, source_ref)
    fine_start(void_ref, source_ref, coef_ref, diag_ref, first_ref)
    layers, width_y, width = source_ref.shape
    depth = layers - 2 * REACH
    fine_sweep(coef_ref, first_ref, first_ref, next_ref, REACH - 1, layers - REACH + 1)
    half = depth // 2
    rows = half * width_y
    for k in range(half):
        total = jnp.zeros((width_y, width), F32)
        for i in (REACH + 2 * k, REACH + 2 * k + 1):
            here = next_ref[i]
            total = total + diag_ref[i] * (
                first_ref[i]
                - relax_weight * here
                + pull(coef_ref, i, next_ref[i - 1], here, next_ref[i + 1])
            )
        fold_ref[0, k * width_y : (k + 1) * width_y, :] = total
        fold_ref[1, k * width_y : (k + 1) * width_y, :] = void_ref[HALO + 2 * k] + void_ref[HALO + 2 * k + 1]
    right = fold_ref[0, pl.ds(0, rows // 2, stride=2), :] + fold_ref[0, pl.ds(1, rows // 2, stride=2), :]
    porous = fold_ref[1, pl.ds(0, rows // 2, stride=2), :] + fold_ref[1, pl.ds(1, rows // 2, stride=2), :]
    coarse = jnp.dot(right, mean_matrix(width, 0), precision=HIGHEST, preferred_element_type=F32)
    coarse = coarse + jnp.dot(porous, mean_matrix(width, width // 2), precision=HIGHEST, preferred_element_type=F32)
    for t in range(wide):
        send_ref[t] = coarse


def loop(count, body, unroll=4):
    while count % unroll:
        unroll //= 2

    def step(i, _):
        for j in range(unroll):
            body(i * unroll + j)
        return 0

    lax.fori_loop(0, count // unroll, step, 0)


def close_halves(ref, first_half):
    last = ref.shape[0] - 2
    half = ref.shape[2] // 2
    ref[0] = jnp.where(first_half, 0.0, pltpu.roll(ref[last], half, 1))
    ref[last + 1] = jnp.where(first_half, pltpu.roll(ref[1], half, 1), 0.0)


class Level:
    def __init__(self, index, refs):
        self.index = index
        self.step = 2 ** (index - 1)
        self.porous, self.right, self.coef, self.diag, self.first, self.one, self.two = refs
        self.layers, lanes, width = self.right.shape
        half = width // 2
        y, x = iota((lanes, width), 0), iota((lanes, width), 1) % half
        self.first_half = iota((lanes, width), 1) < half
        self.masks = (y >= self.step, y < lanes - self.step, x >= self.step, x < half - self.step)

    def start(self):
        weight = 0.5 * 0.25**self.index
        close_halves(self.porous, self.first_half)

        def body(i):
            p = self.porous[i + 1]
            around = (self.porous[i], self.porous[i + 2]) + sides(p, self.masks, self.step, self.step)
            sums = [p + q for q in around]
            diag = sums[0] + sums[1] + sums[2] + sums[3] + sums[4] + sums[5]
            inverse = relax_weight / diag
            for k in range(6):
                coef = sums[k] * inverse
                if k >= 2:
                    coef = jnp.where(self.masks[k - 2], coef, 0.0)
                self.coef[k, i] = coef
            self.diag[i] = diag * (weight / relax_weight)

        loop(self.layers, body)

    def begin(self):
        weight = 0.5 * 0.25**self.index

        def body(i):
            value = self.right[i] / self.diag[i]
            self.first[i] = value
            self.one[i + 1] = value

        loop(self.layers, body)

    def sweep(self):
        close_halves(self.one, self.first_half)

        def body(i):
            here = self.one[i + 1]
            self.two[i + 1] = (
                (1.0 - relax_weight) * here
                + self.first[i]
                + pull(self.coef, i, self.one[i], here, self.one[i + 2], self.step, self.step)
            )

        loop(self.layers, body)
        self.one, self.two = self.two, self.one

    def residual(self, i):
        here = self.one[i + 1]
        return self.diag[i] * (
            self.first[i]
            - relax_weight * here
            + pull(self.coef, i, self.one[i], here, self.one[i + 2], self.step, self.step)
        )

    def mean(self, value):
        y, x = iota(value.shape, 0), iota(value.shape, 1)
        value = value + jnp.where(
            (y & self.step) == 0, ahead(value, self.step, 0), back(value, self.step, 0)
        )
        value = value + jnp.where(
            (x & self.step) == 0, ahead(value, self.step, 1), back(value, self.step, 1)
        )
        return value * 0.125


def coarse_cycle(levels, index):
    level = levels[index]
    level.begin()
    last = index == len(levels) - 1
    for _ in range((COARSE_SWEEPS if last else SWEEPS) - 1):
        level.sweep()
    if not last:
        under = levels[index + 1]
        close_halves(level.one, level.first_half)

        def body(i):
            under.right[i] = level.mean(level.residual(2 * i) + level.residual(2 * i + 1))

        loop(under.layers, body)
        coarse_cycle(levels, index + 1)

        def add(i):
            correction = under.one[i + 1]
            level.one[2 * i + 1] = level.one[2 * i + 1] + correction
            level.one[2 * i + 2] = level.one[2 * i + 2] + correction

        loop(under.layers, add)
        for _ in range(SWEEPS):
            level.sweep()


def solve_kernel(wide, recv_ref, rows_ref, drag_ref, base_ref, *refs):
    pieces, refs = refs[: len(refs) - 33], refs[len(refs) - 33 :]
    pressure_ref, gas_ref, send_ref = refs[:3]
    level_refs = [refs[3 + 7 * i : 10 + 7 * i] for i in range(3)]
    void_ref, source_ref, coef_ref, first_ref, one_ref, two_ref, coarse_ref, fold_ref, slope_ref = refs[24:33]
    narrow = len(pieces)
    lanes = pieces[0].shape[1]
    n = lax.axis_index("narrow")
    w = lax.axis_index("wide")
    spots = [n, 1 - n] if narrow == 2 else list(range(narrow))
    fill_window(pieces, spots, lanes, void_ref, source_ref)
    layers, width_y, width = source_ref.shape
    depth = layers - 2 * REACH
    half, coarse_y = depth // 2, width_y // 2
    levels = [Level(i + 1, level_refs[i]) for i in range(3)]
    top = levels[0]
    middle = width // 2

    def unpack(t):
        for z in range(half):
            low = recv_ref[t, pl.ds(z * coarse_y, coarse_y), :]
            high = recv_ref[t + wide // 2, pl.ds(z * coarse_y, coarse_y), :]
            top.right[t * half + z] = jnp.where(top.first_half, low, pltpu.roll(high, middle, 1))
            top.porous[t * half + z + 1] = jnp.where(top.first_half, pltpu.roll(low, middle, 1), high)

    loop(wide // 2, unpack)
    for upper, lower in ((levels[0], levels[1]), (levels[1], levels[2])):

        def narrow_down(i):
            lower.porous[i + 1] = upper.mean(upper.porous[2 * i + 1] + upper.porous[2 * i + 2])

        loop(lower.layers, narrow_down)
    for level in levels:
        level.start()
    coarse_cycle(levels, 0)

    fine_start(void_ref, source_ref, coef_ref, None, first_ref)
    fine_sweep(coef_ref, first_ref, first_ref, one_ref, 1, layers - 1)
    total = top.layers
    spans = layers // 2
    for k in range(spans):
        z = w * half - REACH // 2 + k
        inside = jnp.logical_and(z >= 0, z < 2 * total)
        z = jnp.clip(z, 0, 2 * total - 1)
        upper = z >= total
        value = top.one[jnp.where(upper, z - total, z) + 1]
        value = jnp.where(upper, pltpu.roll(value, middle, 1), value)
        coarse_ref[k * coarse_y : (k + 1) * coarse_y, :] = jnp.where(inside, value, 0.0)
    wider = jnp.dot(coarse_ref[...], spread_matrix(width, width, 0), precision=HIGHEST, preferred_element_type=F32)
    count = spans * coarse_y
    fold_ref[pl.ds(0, count, stride=2), :] = wider
    fold_ref[pl.ds(1, count, stride=2), :] = wider
    for i in range(1, layers - 1):
        k = i // 2
        correction = fold_ref[k * width_y : (k + 1) * width_y, :]
        one_ref[i] = one_ref[i] + jnp.where(void_ref[i + 1] > 0.0, correction, 0.0)
    fine_sweep(coef_ref, first_ref, one_ref, two_ref, 2, layers - 2)
    fine_sweep(coef_ref, first_ref, two_ref, one_ref, 3, layers - 3)

    masks = side_masks(width_y, width)
    own = pl.ds(pl.multiple_of(n * lanes, lanes), lanes)
    for z in range(depth):
        i = REACH + z
        here = one_ref[i]
        before_y, after_y, before_x, after_x = sides(here, masks, 1, 1)
        slope_ref[0, z] = 0.5 * (one_ref[i + 1] - one_ref[i - 1])
        slope_ref[1, z] = 0.5 * (after_y - before_y)
        slope_ref[2, z] = 0.5 * (after_x - before_x)
        pressure_ref[z] = one_ref[i, own, :]
        for c in range(3):
            gas_ref[c, z] = base_ref[c, z] - (step_duration / gas_density) * slope_ref[c, z, own, :]

    zy, x = cell_rows(rows_ref[1])

    def table(c):
        return lambda row: slope_ref[c, row // lanes, pl.ds(n * lanes + row % lanes, 1), :]

    slopes = gather_cells([table(0), table(1), table(2)], zy, x, depth * lanes)
    forces = [drag_ref[c] - rows_ref[0] * slopes[c] for c in range(3)]
    for g in range(GROUPS):
        target = w - (g - SPREAD)

        @pl.when(jnp.logical_and(target >= 0, target < wide))
        def _():
            for c in range(3):
                send_ref[target, c * CAP : (c + 1) * CAP, :] = forces[c][g * CAP : (g + 1) * CAP]


def contact_kernel(near_ref, count_ref, pos_ref, radius_ref, force_ref, across_ref):
    blocks, slots = radius_ref.shape
    neighbours = near_ref.shape[1]
    slot = iota((1, slots), 1)
    for b in range(blocks):
        radius = jnp.where(slot < count_ref[b], radius_ref[b : b + 1, :], -100.0)
        for q in range(4):
            row = pos_ref[q, b : b + 1, :] if q < 3 else radius
            across_ref[q, b] = jnp.broadcast_to(row, (slots, slots)).T

    factor = stiffness / (slots * (neighbours + 1))
    for b in range(blocks):
        mine = [jnp.broadcast_to(pos_ref[c, b : b + 1, :], (8, slots)) for c in range(3)]
        mine_radius = jnp.broadcast_to(radius_ref[b : b + 1, :], (8, slots))

        def one(k, sums):
            j = jnp.where(k < neighbours, near_ref[b, jnp.minimum(k, neighbours - 1)], b)
            sums = list(sums)
            for row in range(0, slots, 8):
                apart = [mine[c] - across_ref[c, j, row : row + 8, :] for c in range(3)]
                square = apart[0] * apart[0] + apart[1] * apart[1] + (apart[2] * apart[2] + softening * softening)
                inverse = lax.rsqrt(square)
                overlap = jnp.maximum(mine_radius + across_ref[3, j, row : row + 8, :] - square * inverse, 0.0)
                weight = overlap * inverse
                for c in range(3):
                    sums[c] = sums[c] + apart[c] * weight
            return tuple(sums)

        sums = lax.fori_loop(0, neighbours + 1, one, tuple(jnp.zeros((8, slots), F32) for _ in range(3)))
        for c in range(3):
            force_ref[c, b : b + 1, :] = jnp.sum(sums[c], axis=0, keepdims=True) * factor


def move_kernel(wide, offset_ref, count_ref, recv_ref, contact_ref, radius_ref, vel_ref, out_ref):
    w = lax.axis_index("wide")
    blocks, slots = radius_ref.shape
    offsets, rank = ranks(offset_ref, blocks)
    slot = iota((1, slots), 1)
    for b in range(blocks):
        home = jnp.clip(w + offsets[b], 0, wide - 1)
        live = jnp.where(slot < count_ref[b], 1.0, 0.0)
        radius = radius_ref[b : b + 1, :]
        inverse = 1.0 / (particle_density * (radius * radius * radius))
        for c in range(3):
            fluid = recv_ref[home, pl.ds(c * CAP + rank[b], 1), :]
            push = (contact_ref[c, b : b + 1, :] + fluid) * inverse
            if c == 0:
                push = push + gravity
            out_ref[c, b : b + 1, :] = live * (vel_ref[c, b : b + 1, :] + step_duration * push)


def local(
    particle_position,
    particle_velocity,
    radius,
    block_live_count,
    cell_index,
    block_offset,
    neighbours,
    gas_velocity,
    pressure_source,
    void_before,
):
    wide, narrow = lax.axis_size("wide"), lax.axis_size("narrow")
    blocks, slots = radius.shape
    depth, lanes, width = pressure_source.shape
    width_y = lanes * narrow
    voids, layers = depth + 2 * HALO, depth + 2 * REACH
    half, coarse_y = depth // 2, width_y // 2
    slot_rows = -(-GROUPS * CAP // 8) * 8

    send, source = call(
        functools.partial(pack_kernel, wide),
        (f32s(wide, SOURCE_ROW + REACH * lanes, width), f32s(depth, lanes, width)),
        [SMEM, SMEM] + [VMEM] * 5,
        (VMEM, VMEM),
    )(block_offset, block_live_count, radius, particle_velocity, cell_index, pressure_source, void_before)
    recv = lax.all_to_all(send, "wide", 0, 0)

    contact = call(
        contact_kernel,
        f32s(3, blocks, slots),
        [SMEM, SMEM, VMEM, VMEM],
        VMEM,
        [pltpu.VMEM((4, blocks, slots, slots), F32)],
        flops=56 * 128 * 128 * 20,
    )(neighbours, block_live_count, particle_position, radius)

    window, rows = call(
        functools.partial(void_kernel, wide),
        (f32s(voids + layers, lanes, width), f32s(5, slot_rows, slots)),
        [VMEM] * 2,
        (VMEM, VMEM),
    )(recv, source)
    if narrow == 2:
        pieces = [window, lax.ppermute(window, "narrow", [(0, 1), (1, 0)])]
    else:
        every = lax.all_gather(window, "narrow")
        pieces = [every[i] for i in range(narrow)]

    fine = [
        pltpu.VMEM((voids, width_y, width), F32),
        pltpu.VMEM((layers, width_y, width), F32),
        pltpu.VMEM((6, layers, width_y, width), F32),
    ]
    plane = pltpu.VMEM((layers, width_y, width), F32)
    coarse = call(
        functools.partial(coarsen_kernel, wide),
        f32s(wide, half * coarse_y, width),
        [VMEM] * len(pieces),
        VMEM,
        fine + [plane, plane, plane, pltpu.VMEM((2, half * width_y, width), F32)],
    )(*pieces)
    gathered = lax.all_to_all(coarse, "wide", 0, 0)

    drag, base = call(
        drag_kernel,
        (f32s(3, slot_rows, slots), f32s(3, depth, lanes, width)),
        [VMEM] * 3,
        (VMEM, VMEM),
        flops=10_000_000,
    )(window, rows, gas_velocity)

    level_scratch = []
    for index in range(3):
        count = wide * half // 2 >> index
        body = pltpu.VMEM((count, coarse_y, width), F32)
        edged = pltpu.VMEM((count + 2, coarse_y, width), F32)
        level_scratch += [edged, body, pltpu.VMEM((6, count, coarse_y, width), F32), body, body, edged, edged]
    pressure, gas_next, returning = call(
        functools.partial(solve_kernel, wide),
        (f32s(depth, lanes, width), f32s(3, depth, lanes, width), f32s(wide, slot_rows, slots)),
        [VMEM] * (4 + len(pieces)),
        (VMEM, VMEM, VMEM),
        level_scratch
        + fine
        + [plane, plane, plane]
        + [
            pltpu.VMEM((layers // 2 * coarse_y, width), F32),
            pltpu.VMEM((layers // 2 * width_y, width), F32),
            pltpu.VMEM((3, depth, width_y, width), F32),
        ],
    )(gathered, rows, drag, base, *pieces)
    returned = lax.all_to_all(returning, "wide", 0, 0)

    updated = call(
        functools.partial(move_kernel, wide),
        f32s(3, blocks, slots),
        [SMEM, SMEM] + [VMEM] * 4,
        VMEM,
    )(block_offset, block_live_count, returned, contact, radius, particle_velocity)
    return (pressure, gas_next, updated)


def solution(mesh):
    placed = (
        P(None, ("wide", "narrow"), None),
        P(None, ("wide", "narrow"), None),
        P(("wide", "narrow"), None),
        P(("wide", "narrow")),
        P(("wide", "narrow"), None),
        P(("wide", "narrow")),
        P(("wide", "narrow"), None),
        P(None, "wide", "narrow", None),
        P("wide", "narrow", None),
        P("wide", "narrow", None),
    )
    return jax.shard_map(
        local,
        mesh=mesh,
        in_specs=placed,
        out_specs=(
            P("wide", "narrow", None),
            P(None, "wide", "narrow", None),
            P(None, ("wide", "narrow"), None),
        ),
        check_vma=False,
    )
```

```python
import functools
import math

import jax
import jax.numpy as jnp
from jax import lax
from jax.experimental import pallas as pl
from jax.experimental.pallas import tpu as pltpu
from jax.sharding import PartitionSpec as P

SPREAD = 2
SWEEPS = 2
COARSE_SWEEPS = 4
CAP = 3
GROUPS = 2 * SPREAD + 1
HALO = 5
REACH = 4

relax_weight = 0.8
solid_most = 0.6
void_power = 2.65
drag_base = 0.5
drag_slope = 0.5
stiffness = 16.0
softening = 0.1
particle_density = 2.0
gas_density = 1.0
step_duration = 0.25
gravity = -1.0

F32 = jnp.float32
BF16 = jnp.bfloat16
VMEM = pl.BlockSpec(memory_space=pltpu.VMEM)
SMEM = pl.BlockSpec(memory_space=pltpu.SMEM)
HIGHEST = lax.Precision.HIGHEST
VOL_ROW = 0
CELL_ROW = 3 * CAP
VEL_ROW = 6 * CAP
SEND_ROWS = -(-9 * CAP // 8) * 8
UNROLL = 32
VMEM_SPARE = 4 * 1024 * 1024
VMEM_MOST = 60 * 1024 * 1024


def call(kernel, out_shape, in_specs, out_specs, scratch=(), flops=0, spare=VMEM_SPARE):
    def run(*args):
        held = [*args, *jax.tree.leaves(out_shape), *scratch]
        need = sum(4 * math.prod(array.shape) for array in held)
        return pl.pallas_call(
            kernel,
            out_shape=out_shape,
            in_specs=in_specs,
            out_specs=out_specs,
            scratch_shapes=list(scratch),
            compiler_params=pltpu.CompilerParams(vmem_limit_bytes=min(2 * need + spare, VMEM_MOST)),
            cost_estimate=pl.CostEstimate(flops=flops, bytes_accessed=1 << 18, transcendentals=0),
        )(*args)

    return run


def f32s(*shape):
    return jax.ShapeDtypeStruct(shape, F32)


def iota(shape, dim):
    return lax.broadcasted_iota(jnp.int32, shape, dim)


def back(value, step, axis):
    return pltpu.roll(value, step, axis)


def ahead(value, step, axis):
    return pltpu.roll(value, value.shape[axis] - step, axis)


def ranks(offset_ref, count):
    offsets = [offset_ref[i] for i in range(count)]
    found = []
    for i in range(count):
        rank = jnp.int32(0)
        for j in range(i):
            rank = rank + jnp.where(offsets[j] == offsets[i], 1, 0)
        found.append(rank)
    return offsets, found


def pack_kernel(wide, offset_ref, count_ref, radius_ref, vel_ref, cell_ref, source_ref, before_ref, send_ref, s_ref, edge_ref, other_edge_ref):
    w = lax.axis_index("wide")
    blocks, slots = radius_ref.shape
    depth, lanes, _ = source_ref.shape
    send_ref[...] = jnp.zeros(send_ref.shape, F32)
    offsets, rank = ranks(offset_ref, blocks)
    slot = iota((1, slots), 1)
    for b in range(blocks):
        radius = radius_ref[b : b + 1, :]
        vol = jnp.where(slot < count_ref[b], radius * radius * radius, 0.0)
        cell = cell_ref[b : b + 1, :].astype(F32)
        for e in (-1, 0, 1):
            target = w + offsets[b] - e

            @pl.when(jnp.logical_and(target >= 0, target < wide))
            def _():
                row = (e + 1) * CAP + rank[b]
                send_ref[target, pl.ds(VOL_ROW + row, 1), :] = vol
                send_ref[target, pl.ds(CELL_ROW + row, 1), :] = cell
                if e == 0:
                    for c in range(3):
                        send_ref[target, pl.ds(VEL_ROW + c * CAP + rank[b], 1), :] = vel_ref[c, b : b + 1, :]

    for z in range(depth):
        s_ref[z] = source_ref[z] + before_ref[z] * (1.0 / step_duration)

    for turn, ref in enumerate((edge_ref, other_edge_ref)):
        upward = w % 2 == turn
        for z in range(REACH):
            ref[z] = jnp.where(upward, s_ref[depth - REACH + z], s_ref[z])


def cell_rows(cell_row):
    cell = cell_row.astype(jnp.int32)
    return cell >> 7, cell & 127


def pieces_of(value):
    high = value.astype(BF16).astype(F32)
    return high, value - high


def contract(lhs, rhs):
    return lax.dot_general(lhs, rhs, (((1,), (1,)), ((), ())), preferred_element_type=F32)


def solid_of(vols, cells, first, rows):
    total = jnp.zeros((2 * rows, 128), F32)
    place = iota((rows, 128), 0) + first
    column = iota((128, 128), 0)
    for pair in range(0, len(vols), 2):
        left, right = [], []
        for k in range(pair, min(pair + 2, len(vols))):
            zy, x = cell_rows(cells[k])
            here = place == zy
            high, low = pieces_of(vols[k])
            left.append(
                jnp.concatenate([jnp.where(here, high, 0.0), jnp.where(here, low, 0.0)], axis=0).astype(BF16)
            )
            right.append(jnp.where(column == x, 1.0, 0.0).astype(BF16))
        total = total + contract(jnp.concatenate(left, axis=1), jnp.concatenate(right, axis=1))
    return total[:rows] + total[rows:]


def void_kernel(wide, recv_ref, edge_ref, other_edge_ref, s_ref, window_ref, rows_ref):
    w = lax.axis_index("wide")
    depth, lanes, _ = s_ref.shape
    cells = depth * lanes
    rows_ref[...] = jnp.zeros(rows_ref.shape, F32)
    for e in (-1, 0, 1):
        vols, codes = [], []
        for g in range(GROUPS):
            source = w + e - (g - SPREAD)
            inside = jnp.logical_and(source >= 0, source < wide)
            source = jnp.clip(source, 0, wide - 1)
            row = (e + 1) * CAP
            for r in range(CAP):
                k = g * CAP + r
                vol = jnp.where(inside, recv_ref[source, VOL_ROW + row + r : VOL_ROW + row + r + 1, :], 0.0)
                code = recv_ref[source, CELL_ROW + row + r : CELL_ROW + row + r + 1, :]
                vols.append(vol)
                codes.append(code)
                if e == 0:
                    rows_ref[0, k : k + 1, :] = vol
                    rows_ref[1, k : k + 1, :] = code
                    for c in range(3):
                        at = VEL_ROW + c * CAP + r
                        rows_ref[2 + c, k : k + 1, :] = recv_ref[source, at : at + 1, :]
        low = depth - HALO if e < 0 else 0
        layers = depth if e == 0 else HALO
        first = 0 if e >= 0 else (low * lanes) // 16 * 16
        count = cells if e == 0 else -(-(layers * lanes + (low * lanes - first)) // 16) * 16
        solid = solid_of(vols, codes, first, count)
        void = 1.0 - solid_most * solid / (1.0 + solid)
        exists = jnp.logical_and(w + e >= 0, w + e < wide)
        void = jnp.where(exists, void, 0.0)
        base = HALO + (e * HALO if e < 0 else e * depth)
        for z in range(layers):
            start = (low + z) * lanes - first
            window_ref[base + z] = void[start : start + lanes]
    voids = depth + 2 * HALO
    for z in range(depth):
        window_ref[voids + REACH + z] = s_ref[z]
    for e in (-1, 1):
        beside = w + e
        exists = jnp.logical_and(beside >= 0, beside < wide)
        turn = w % 2 == (0 if e > 0 else 1)
        for z in range(REACH):
            part = jnp.where(turn, edge_ref[z], other_edge_ref[z])
            at = voids + (z if e < 0 else REACH + depth + z)
            window_ref[at] = jnp.where(exists, part, 0.0)


def gather_cells(refs, zy, x, rows):
    found = [jnp.zeros(zy.shape, F32) for _ in refs]
    for row in range(rows):
        here = zy == row
        for i, ref in enumerate(refs):
            source = jnp.broadcast_to(ref(row), zy.shape)
            found[i] = jnp.where(here, jnp.take_along_axis(source, x, axis=1), found[i])
    return found


def drag_kernel(window_ref, rows_ref, gas_ref, drag_ref, base_ref):
    _, depth, lanes, _ = gas_ref.shape
    cells = depth * lanes
    vol = rows_ref[0]
    zy, x = cell_rows(rows_ref[1])

    def table(c):
        return lambda row: gas_ref[c, row // lanes, row % lanes : row % lanes + 1, :]

    def voids(row):
        return window_ref[HALO + row // lanes, row % lanes : row % lanes + 1, :]

    gas_z, gas_y, gas_x, void = gather_cells([table(0), table(1), table(2), voids], zy, x, cells)
    slips = [gas_z - rows_ref[2], gas_y - rows_ref[3], gas_x - rows_ref[4]]
    speed = jnp.sqrt(slips[0] * slips[0] + slips[1] * slips[1] + slips[2] * slips[2])
    scale = vol * (drag_base + drag_slope * speed) * jnp.exp(-void_power * jnp.log(void))
    drags = [scale * slip for slip in slips]
    for c in range(3):
        drag_ref[c] = drags[c]
    split = []
    for c in range(3):
        split += list(pieces_of(drags[c]))
    total = jnp.zeros((6 * cells, 128), F32)
    place = iota((cells, 128), 0)
    column = iota((128, 128), 0)
    for pair in range(0, vol.shape[0], 2):
        left, right = [], []
        for k in range(pair, pair + 2):
            here = place == zy[k : k + 1]
            left.append(
                jnp.concatenate([jnp.where(here, part[k : k + 1], 0.0) for part in split], axis=0).astype(BF16)
            )
            right.append(jnp.where(column == x[k : k + 1], 1.0, 0.0).astype(BF16))
        total = total + contract(jnp.concatenate(left, axis=1), jnp.concatenate(right, axis=1))
    for z in range(depth):
        per_void = step_duration / (gas_density * window_ref[HALO + z])
        for c in range(3):
            start = 2 * c * cells + z * lanes
            given = total[start : start + lanes] + total[start + cells : start + cells + lanes]
            base_ref[c, z] = gas_ref[c, z] - per_void * given


def fill_window(pieces, spots, lanes, void_ref, source_ref):
    voids = void_ref.shape[0]
    for piece, spot in zip(pieces, spots):
        at = pl.ds(spot * lanes if isinstance(spot, int) else pl.multiple_of(spot * lanes, lanes), lanes)
        for z in range(voids):
            void_ref[z, at, :] = piece[z]
        for z in range(source_ref.shape[0]):
            source_ref[z, at, :] = piece[voids + z]


def side_masks(lanes, width):
    y, x = iota((lanes, width), 0), iota((lanes, width), 1)
    return (y >= 1, y < lanes - 1, x >= 1, x < width - 1)


def sides(value, masks, step_y, step_x):
    return (
        jnp.where(masks[0], back(value, step_y, 0), 0.0),
        jnp.where(masks[1], ahead(value, step_y, 0), 0.0),
        jnp.where(masks[2], back(value, step_x, 1), 0.0),
        jnp.where(masks[3], ahead(value, step_x, 1), 0.0),
    )


def fine_start(void_ref, source_ref, coef_ref, diag_ref, first_ref):
    layers, lanes, width = source_ref.shape
    masks = side_masks(lanes, width)
    for i in range(layers):
        p = void_ref[i + 1]
        around = (void_ref[i], void_ref[i + 2]) + sides(p, masks, 1, 1)
        sums = [p + q for q in around]
        diag = sums[0] + sums[1] + sums[2] + sums[3] + sums[4] + sums[5]
        inside = p > 0.0
        inverse = jnp.where(inside, relax_weight / jnp.where(inside, diag, 1.0), 0.0)
        for k in range(6):
            coef = sums[k] * inverse
            if k >= 2:
                coef = jnp.where(masks[k - 2], coef, 0.0)
            coef_ref[k, i] = coef
        if diag_ref is not None:
            diag_ref[i] = diag * (0.5 / relax_weight)
        first_ref[i] = (source_ref[i] - p * (1.0 / step_duration)) * inverse * 2.0


def pull(coef_ref, i, below, here, above, step_y=1, step_x=1):
    total = coef_ref[0, i] * below + coef_ref[1, i] * above
    total = total + coef_ref[2, i] * back(here, step_y, 0) + coef_ref[3, i] * ahead(here, step_y, 0)
    return total + coef_ref[4, i] * back(here, step_x, 1) + coef_ref[5, i] * ahead(here, step_x, 1)


def fine_sweep(coef_ref, first_ref, old_ref, new_ref, start, stop):
    for i in range(start, stop):
        here = old_ref[i]
        new_ref[i] = (
            (1.0 - relax_weight) * here
            + first_ref[i]
            + pull(coef_ref, i, old_ref[i - 1], here, old_ref[i + 1])
        )


def spread_matrix(rows, columns, shift):
    return jnp.where(iota((rows, columns), 1) // 2 + shift == iota((rows, columns), 0), 1.0, 0.0)


def mean_matrix(width, shift):
    return jnp.where(iota((width, width), 0) // 2 + shift == iota((width, width), 1), 0.125, 0.0)


def coarsen_kernel(wide, *refs):
    *pieces, send_ref, void_ref, source_ref, coef_ref, diag_ref, first_ref, next_ref, fold_ref = refs
    narrow = len(pieces)
    lanes = pieces[0].shape[1]
    n = lax.axis_index("narrow")
    spots = [n, 1 - n] if narrow == 2 else list(range(narrow))
    fill_window(pieces, spots, lanes, void_ref, source_ref)
    fine_start(void_ref, source_ref, coef_ref, diag_ref, first_ref)
    layers, width_y, width = source_ref.shape
    depth = layers - 2 * REACH
    fine_sweep(coef_ref, first_ref, first_ref, next_ref, REACH - 1, layers - REACH + 1)
    half = depth // 2
    rows = half * width_y
    for k in range(half):
        total = jnp.zeros((width_y, width), F32)
        for i in (REACH + 2 * k, REACH + 2 * k + 1):
            here = next_ref[i]
            total = total + diag_ref[i] * (
                first_ref[i]
                - relax_weight * here
                + pull(coef_ref, i, next_ref[i - 1], here, next_ref[i + 1])
            )
        fold_ref[0, k * width_y : (k + 1) * width_y, :] = total
        fold_ref[1, k * width_y : (k + 1) * width_y, :] = void_ref[HALO + 2 * k] + void_ref[HALO + 2 * k + 1]
    right = fold_ref[0, pl.ds(0, rows // 2, stride=2), :] + fold_ref[0, pl.ds(1, rows // 2, stride=2), :]
    porous = fold_ref[1, pl.ds(0, rows // 2, stride=2), :] + fold_ref[1, pl.ds(1, rows // 2, stride=2), :]
    coarse = jnp.dot(right, mean_matrix(width, 0), precision=HIGHEST, preferred_element_type=F32)
    coarse = coarse + jnp.dot(porous, mean_matrix(width, width // 2), precision=HIGHEST, preferred_element_type=F32)
    for t in range(wide):
        send_ref[t] = coarse


def loop(count, body, size=1):
    unroll = max(1, UNROLL // size)
    if count <= unroll:
        for i in range(count):
            body(i)
        return
    while count % unroll:
        unroll //= 2

    def step(i, _):
        for j in range(unroll):
            body(i * unroll + j)
        return 0

    lax.fori_loop(0, count // unroll, step, 0)


def close_halves(ref, first_half):
    last = ref.shape[0] - 2
    half = ref.shape[2] // 2
    ref[0] = jnp.where(first_half, 0.0, pltpu.roll(ref[last], half, 1))
    ref[last + 1] = jnp.where(first_half, pltpu.roll(ref[1], half, 1), 0.0)


class Level:
    def __init__(self, index, refs):
        self.index = index
        self.step = 2 ** (index - 1)
        self.porous, self.right, self.coef, self.diag, self.scale, self.first, self.one, self.two = refs
        self.layers, lanes, width = self.right.shape
        half = width // 2
        self.size = -(-lanes // 8)
        y, x = iota((lanes, width), 0), iota((lanes, width), 1) % half
        self.first_half = iota((lanes, width), 1) < half
        self.masks = (y >= self.step, y < lanes - self.step, x >= self.step, x < half - self.step)

    def start(self):
        weight = 0.5 * 0.25**self.index
        close_halves(self.porous, self.first_half)

        def body(i):
            p = self.porous[i + 1]
            around = (self.porous[i], self.porous[i + 2]) + sides(p, self.masks, self.step, self.step)
            sums = [p + q for q in around]
            diag = sums[0] + sums[1] + sums[2] + sums[3] + sums[4] + sums[5]
            inverse = relax_weight / diag
            for k in range(6):
                coef = sums[k] * inverse
                if k >= 2:
                    coef = jnp.where(self.masks[k - 2], coef, 0.0)
                self.coef[k, i] = coef
            self.diag[i] = diag * (weight / relax_weight)
            self.scale[i] = inverse * (1.0 / weight)

        loop(self.layers, body, self.size)

    def begin(self):
        def body(i):
            value = self.right[i] * self.scale[i]
            self.first[i] = value
            self.one[i + 1] = value

        loop(self.layers, body, self.size)

    def sweep(self):
        close_halves(self.one, self.first_half)

        def body(i):
            here = self.one[i + 1]
            self.two[i + 1] = (
                (1.0 - relax_weight) * here
                + self.first[i]
                + pull(self.coef, i, self.one[i], here, self.one[i + 2], self.step, self.step)
            )

        loop(self.layers, body, self.size)
        self.one, self.two = self.two, self.one

    def residual(self, i):
        here = self.one[i + 1]
        return self.diag[i] * (
            self.first[i]
            - relax_weight * here
            + pull(self.coef, i, self.one[i], here, self.one[i + 2], self.step, self.step)
        )

    def mean(self, value):
        y, x = iota(value.shape, 0), iota(value.shape, 1)
        value = value + jnp.where(
            (y & self.step) == 0, ahead(value, self.step, 0), back(value, self.step, 0)
        )
        value = value + jnp.where(
            (x & self.step) == 0, ahead(value, self.step, 1), back(value, self.step, 1)
        )
        return value * 0.125


def coarse_cycle(levels, index):
    level = levels[index]
    level.begin()
    last = index == len(levels) - 1
    for _ in range((COARSE_SWEEPS if last else SWEEPS) - 1):
        level.sweep()
    if not last:
        under = levels[index + 1]
        close_halves(level.one, level.first_half)

        def body(i):
            under.right[i] = level.mean(level.residual(2 * i) + level.residual(2 * i + 1))

        loop(under.layers, body, level.size)
        coarse_cycle(levels, index + 1)

        def add(i):
            correction = under.one[i + 1]
            level.one[2 * i + 1] = level.one[2 * i + 1] + correction
            level.one[2 * i + 2] = level.one[2 * i + 2] + correction

        loop(under.layers, add, level.size)
        for _ in range(SWEEPS):
            level.sweep()


def solve_kernel(wide, recv_ref, rows_ref, drag_ref, base_ref, *refs):
    pieces, refs = refs[: len(refs) - 36], refs[len(refs) - 36 :]
    pressure_ref, gas_ref, send_ref = refs[:3]
    level_refs = [refs[3 + 8 * i : 11 + 8 * i] for i in range(3)]
    void_ref, source_ref, coef_ref, first_ref, one_ref, two_ref, coarse_ref, fold_ref, slope_ref = refs[27:36]
    narrow = len(pieces)
    lanes = pieces[0].shape[1]
    n = lax.axis_index("narrow")
    w = lax.axis_index("wide")
    spots = [n, 1 - n] if narrow == 2 else list(range(narrow))
    fill_window(pieces, spots, lanes, void_ref, source_ref)
    layers, width_y, width = source_ref.shape
    depth = layers - 2 * REACH
    half, coarse_y = depth // 2, width_y // 2
    levels = [Level(i + 1, level_refs[i]) for i in range(3)]
    top = levels[0]
    middle = width // 2

    def unpack(t):
        for z in range(half):
            low = recv_ref[t, pl.ds(z * coarse_y, coarse_y), :]
            high = recv_ref[t + wide // 2, pl.ds(z * coarse_y, coarse_y), :]
            top.right[t * half + z] = jnp.where(top.first_half, low, pltpu.roll(high, middle, 1))
            top.porous[t * half + z + 1] = jnp.where(top.first_half, pltpu.roll(low, middle, 1), high)

    loop(wide // 2, unpack, half * top.size)
    for upper, lower in ((levels[0], levels[1]), (levels[1], levels[2])):

        def narrow_down(i):
            lower.porous[i + 1] = upper.mean(upper.porous[2 * i + 1] + upper.porous[2 * i + 2])

        loop(lower.layers, narrow_down, upper.size)
    for level in levels:
        level.start()
    coarse_cycle(levels, 0)

    fine_start(void_ref, source_ref, coef_ref, None, first_ref)
    fine_sweep(coef_ref, first_ref, first_ref, one_ref, 1, layers - 1)
    total = top.layers
    spans = layers // 2
    for k in range(spans):
        z = w * half - REACH // 2 + k
        inside = jnp.logical_and(z >= 0, z < 2 * total)
        z = jnp.clip(z, 0, 2 * total - 1)
        upper = z >= total
        value = top.one[jnp.where(upper, z - total, z) + 1]
        value = jnp.where(upper, pltpu.roll(value, middle, 1), value)
        coarse_ref[k * coarse_y : (k + 1) * coarse_y, :] = jnp.where(inside, value, 0.0)
    wider = jnp.dot(coarse_ref[...], spread_matrix(width, width, 0), precision=HIGHEST, preferred_element_type=F32)
    count = spans * coarse_y
    fold_ref[pl.ds(0, count, stride=2), :] = wider
    fold_ref[pl.ds(1, count, stride=2), :] = wider
    for i in range(1, layers - 1):
        k = i // 2
        correction = fold_ref[k * width_y : (k + 1) * width_y, :]
        one_ref[i] = one_ref[i] + jnp.where(void_ref[i + 1] > 0.0, correction, 0.0)
    fine_sweep(coef_ref, first_ref, one_ref, two_ref, 2, layers - 2)
    fine_sweep(coef_ref, first_ref, two_ref, one_ref, 3, layers - 3)

    masks = side_masks(width_y, width)
    own = pl.ds(pl.multiple_of(n * lanes, lanes), lanes)
    for z in range(depth):
        i = REACH + z
        here = one_ref[i]
        before_y, after_y, before_x, after_x = sides(here, masks, 1, 1)
        slope_ref[0, z] = 0.5 * (one_ref[i + 1] - one_ref[i - 1])
        slope_ref[1, z] = 0.5 * (after_y - before_y)
        slope_ref[2, z] = 0.5 * (after_x - before_x)
        pressure_ref[z] = one_ref[i, own, :]
        for c in range(3):
            gas_ref[c, z] = base_ref[c, z] - (step_duration / gas_density) * slope_ref[c, z, own, :]

    zy, x = cell_rows(rows_ref[1])

    def table(c):
        return lambda row: slope_ref[c, row // lanes, pl.ds(n * lanes + row % lanes, 1), :]

    slopes = gather_cells([table(0), table(1), table(2)], zy, x, depth * lanes)
    forces = [drag_ref[c] - rows_ref[0] * slopes[c] for c in range(3)]
    for g in range(GROUPS):
        target = w - (g - SPREAD)

        @pl.when(jnp.logical_and(target >= 0, target < wide))
        def _():
            for c in range(3):
                send_ref[target, c * CAP : (c + 1) * CAP, :] = forces[c][g * CAP : (g + 1) * CAP]


def contact_kernel(near_ref, count_ref, pos_ref, radius_ref, force_ref, across_ref):
    blocks, slots = radius_ref.shape
    neighbours = near_ref.shape[1]
    slot = iota((1, slots), 1)
    for b in range(blocks):
        radius = jnp.where(slot < count_ref[b], radius_ref[b : b + 1, :], -100.0)
        for q in range(4):
            row = pos_ref[q, b : b + 1, :] if q < 3 else radius
            across_ref[q, b] = jnp.broadcast_to(row, (slots, slots)).T

    factor = stiffness / (slots * (neighbours + 1))
    for b in range(blocks):
        mine = [jnp.broadcast_to(pos_ref[c, b : b + 1, :], (8, slots)) for c in range(3)]
        mine_radius = jnp.broadcast_to(radius_ref[b : b + 1, :], (8, slots))

        def one(k, sums):
            j = jnp.where(k < neighbours, near_ref[b, jnp.minimum(k, neighbours - 1)], b)
            sums = list(sums)
            for row in range(0, slots, 8):
                apart = [mine[c] - across_ref[c, j, row : row + 8, :] for c in range(3)]
                square = apart[0] * apart[0] + apart[1] * apart[1] + (apart[2] * apart[2] + softening * softening)
                inverse = lax.rsqrt(square)
                overlap = jnp.maximum(mine_radius + across_ref[3, j, row : row + 8, :] - square * inverse, 0.0)
                weight = overlap * inverse
                for c in range(3):
                    sums[c] = sums[c] + apart[c] * weight
            return tuple(sums)

        sums = lax.fori_loop(0, neighbours + 1, one, tuple(jnp.zeros((8, slots), F32) for _ in range(3)))
        for c in range(3):
            force_ref[c, b : b + 1, :] = jnp.sum(sums[c], axis=0, keepdims=True) * factor


def move_kernel(wide, offset_ref, count_ref, recv_ref, contact_ref, radius_ref, vel_ref, out_ref):
    w = lax.axis_index("wide")
    blocks, slots = radius_ref.shape
    offsets, rank = ranks(offset_ref, blocks)
    slot = iota((1, slots), 1)
    for b in range(blocks):
        home = jnp.clip(w + offsets[b], 0, wide - 1)
        live = jnp.where(slot < count_ref[b], 1.0, 0.0)
        radius = radius_ref[b : b + 1, :]
        inverse = 1.0 / (particle_density * (radius * radius * radius))
        for c in range(3):
            fluid = recv_ref[home, pl.ds(c * CAP + rank[b], 1), :]
            push = (contact_ref[c, b : b + 1, :] + fluid) * inverse
            if c == 0:
                push = push + gravity
            out_ref[c, b : b + 1, :] = live * (vel_ref[c, b : b + 1, :] + step_duration * push)


def pairs_of(count, turn):
    lower = range(turn, count - 1, 2)
    return [(i, i + 1) for i in lower] + [(i + 1, i) for i in lower]


def local(
    particle_position,
    particle_velocity,
    radius,
    block_live_count,
    cell_index,
    block_offset,
    neighbours,
    gas_velocity,
    pressure_source,
    void_before,
):
    wide, narrow = lax.axis_size("wide"), lax.axis_size("narrow")
    blocks, slots = radius.shape
    depth, lanes, width = pressure_source.shape
    width_y = lanes * narrow
    voids, layers = depth + 2 * HALO, depth + 2 * REACH
    half, coarse_y = depth // 2, width_y // 2
    slot_rows = -(-GROUPS * CAP // 8) * 8

    send, source, edge, other_edge = call(
        functools.partial(pack_kernel, wide),
        (f32s(wide, SEND_ROWS, width), f32s(depth, lanes, width), f32s(REACH, lanes, width), f32s(REACH, lanes, width)),
        [SMEM, SMEM] + [VMEM] * 5,
        (VMEM,) * 4,
        spare=VMEM_MOST,
    )(block_offset, block_live_count, radius, particle_velocity, cell_index, pressure_source, void_before)
    recv = lax.all_to_all(send, "wide", 0, 0)
    edges = [lax.ppermute(part, "wide", pairs_of(wide, turn)) for turn, part in enumerate((edge, other_edge))]

    contact = call(
        contact_kernel,
        f32s(3, blocks, slots),
        [SMEM, SMEM, VMEM, VMEM],
        VMEM,
        [pltpu.VMEM((4, blocks, slots, slots), F32)],
        flops=56 * 128 * 128 * 20,
    )(neighbours, block_live_count, particle_position, radius)

    window, rows = call(
        functools.partial(void_kernel, wide),
        (f32s(voids + layers, lanes, width), f32s(5, slot_rows, slots)),
        [VMEM] * 4,
        (VMEM, VMEM),
    )(recv, *edges, source)
    if narrow == 2:
        pieces = [window, lax.ppermute(window, "narrow", [(0, 1), (1, 0)])]
    else:
        every = lax.all_gather(window, "narrow")
        pieces = [every[i] for i in range(narrow)]

    fine = [
        pltpu.VMEM((voids, width_y, width), F32),
        pltpu.VMEM((layers, width_y, width), F32),
        pltpu.VMEM((6, layers, width_y, width), F32),
    ]
    plane = pltpu.VMEM((layers, width_y, width), F32)
    coarse = call(
        functools.partial(coarsen_kernel, wide),
        f32s(wide, half * coarse_y, width),
        [VMEM] * len(pieces),
        VMEM,
        fine + [plane, plane, plane, pltpu.VMEM((2, half * width_y, width), F32)],
    )(*pieces)
    gathered = lax.all_to_all(coarse, "wide", 0, 0)

    drag, base = call(
        drag_kernel,
        (f32s(3, slot_rows, slots), f32s(3, depth, lanes, width)),
        [VMEM] * 3,
        (VMEM, VMEM),
        flops=10_000_000,
    )(window, rows, gas_velocity)

    level_scratch = []
    for index in range(3):
        count = wide * half // 2 >> index
        body = pltpu.VMEM((count, coarse_y, width), F32)
        edged = pltpu.VMEM((count + 2, coarse_y, width), F32)
        level_scratch += [edged, body, pltpu.VMEM((6, count, coarse_y, width), F32), body, body, body, edged, edged]
    gathered, contact = lax.optimization_barrier((gathered, contact))
    pressure, gas_next, returning = call(
        functools.partial(solve_kernel, wide),
        (f32s(depth, lanes, width), f32s(3, depth, lanes, width), f32s(wide, slot_rows, slots)),
        [VMEM] * (4 + len(pieces)),
        (VMEM, VMEM, VMEM),
        level_scratch
        + fine
        + [plane, plane, plane]
        + [
            pltpu.VMEM((layers // 2 * coarse_y, width), F32),
            pltpu.VMEM((layers // 2 * width_y, width), F32),
            pltpu.VMEM((3, depth, width_y, width), F32),
        ],
    )(gathered, rows, drag, base, *pieces)
    returned = lax.all_to_all(returning, "wide", 0, 0)

    updated = call(
        functools.partial(move_kernel, wide),
        f32s(3, blocks, slots),
        [SMEM, SMEM] + [VMEM] * 4,
        VMEM,
    )(block_offset, block_live_count, returned, contact, radius, particle_velocity)
    return (pressure, gas_next, updated)


def solution(mesh):
    placed = (
        P(None, ("wide", "narrow"), None),
        P(None, ("wide", "narrow"), None),
        P(("wide", "narrow"), None),
        P(("wide", "narrow")),
        P(("wide", "narrow"), None),
        P(("wide", "narrow")),
        P(("wide", "narrow"), None),
        P(None, "wide", "narrow", None),
        P("wide", "narrow", None),
        P("wide", "narrow", None),
    )
    return jax.shard_map(
        local,
        mesh=mesh,
        in_specs=placed,
        out_specs=(
            P("wide", "narrow", None),
            P(None, "wide", "narrow", None),
            P(None, ("wide", "narrow"), None),
        ),
        check_vma=False,
    )
```

```python
import functools
import math

import jax
import jax.numpy as jnp
from jax import lax
from jax.experimental import pallas as pl
from jax.experimental.pallas import tpu as pltpu
from jax.sharding import PartitionSpec as P

SPREAD = 2
SWEEPS = 2
COARSE_SWEEPS = 4
CAP = 3
GROUPS = 2 * SPREAD + 1
HALO = 5
REACH = 4

relax_weight = 0.8
solid_most = 0.6
void_power = 2.65
drag_base = 0.5
drag_slope = 0.5
stiffness = 16.0
softening = 0.1
particle_density = 2.0
gas_density = 1.0
step_duration = 0.25
gravity = -1.0

F32 = jnp.float32
BF16 = jnp.bfloat16
VMEM = pl.BlockSpec(memory_space=pltpu.VMEM)
SMEM = pl.BlockSpec(memory_space=pltpu.SMEM)
HIGHEST = lax.Precision.HIGHEST
VOL_ROW = 0
CELL_ROW = 3 * CAP
VEL_ROW = 6 * CAP
SEND_ROWS = -(-9 * CAP // 8) * 8
UNROLL = 32
VMEM_SPARE = 4 * 1024 * 1024
VMEM_MOST = 60 * 1024 * 1024


def call(kernel, out_shape, in_specs, out_specs, scratch=(), flops=0, spare=VMEM_SPARE):
    def run(*args):
        held = [*args, *jax.tree.leaves(out_shape), *scratch]
        need = sum(4 * math.prod(array.shape) for array in held)
        return pl.pallas_call(
            kernel,
            out_shape=out_shape,
            in_specs=in_specs,
            out_specs=out_specs,
            scratch_shapes=list(scratch),
            compiler_params=pltpu.CompilerParams(vmem_limit_bytes=min(2 * need + spare, VMEM_MOST)),
            cost_estimate=pl.CostEstimate(flops=flops, bytes_accessed=1 << 18, transcendentals=0),
        )(*args)

    return run


def f32s(*shape):
    return jax.ShapeDtypeStruct(shape, F32)


def iota(shape, dim):
    return lax.broadcasted_iota(jnp.int32, shape, dim)


def back(value, step, axis):
    return pltpu.roll(value, step, axis)


def ahead(value, step, axis):
    return pltpu.roll(value, value.shape[axis] - step, axis)


def ranks(offset_ref, count):
    offsets = [offset_ref[i] for i in range(count)]
    found = []
    for i in range(count):
        rank = jnp.int32(0)
        for j in range(i):
            rank = rank + jnp.where(offsets[j] == offsets[i], 1, 0)
        found.append(rank)
    return offsets, found


def pack_kernel(wide, offset_ref, count_ref, radius_ref, vel_ref, cell_ref, source_ref, before_ref, send_ref, s_ref, edge_ref, other_edge_ref):
    w = lax.axis_index("wide")
    blocks, slots = radius_ref.shape
    depth, lanes, _ = source_ref.shape
    send_ref[...] = jnp.zeros(send_ref.shape, F32)
    offsets, rank = ranks(offset_ref, blocks)
    slot = iota((1, slots), 1)
    for b in range(blocks):
        radius = radius_ref[b : b + 1, :]
        vol = jnp.where(slot < count_ref[b], radius * radius * radius, 0.0)
        cell = cell_ref[b : b + 1, :].astype(F32)
        for e in (-1, 0, 1):
            target = w + offsets[b] - e

            @pl.when(jnp.logical_and(target >= 0, target < wide))
            def _():
                row = (e + 1) * CAP + rank[b]
                send_ref[target, pl.ds(VOL_ROW + row, 1), :] = vol
                send_ref[target, pl.ds(CELL_ROW + row, 1), :] = cell
                if e == 0:
                    for c in range(3):
                        send_ref[target, pl.ds(VEL_ROW + c * CAP + rank[b], 1), :] = vel_ref[c, b : b + 1, :]

    for z in range(depth):
        s_ref[z] = source_ref[z] + before_ref[z] * (1.0 / step_duration)

    for turn, ref in enumerate((edge_ref, other_edge_ref)):
        upward = w % 2 == turn
        for z in range(REACH):
            ref[z] = jnp.where(upward, s_ref[depth - REACH + z], s_ref[z])


def cell_rows(cell_row):
    cell = cell_row.astype(jnp.int32)
    return cell >> 7, cell & 127


def pieces_of(value):
    high = value.astype(BF16).astype(F32)
    return high, value - high


def contract(lhs, rhs):
    return lax.dot_general(lhs, rhs, (((1,), (1,)), ((), ())), preferred_element_type=F32)


def solid_of(vols, cells, first, rows):
    total = jnp.zeros((2 * rows, 128), F32)
    place = iota((rows, 128), 0) + first
    column = iota((128, 128), 0)
    for pair in range(0, len(vols), 2):
        left, right = [], []
        for k in range(pair, min(pair + 2, len(vols))):
            zy, x = cell_rows(cells[k])
            here = place == zy
            high, low = pieces_of(vols[k])
            left.append(
                jnp.concatenate([jnp.where(here, high, 0.0), jnp.where(here, low, 0.0)], axis=0).astype(BF16)
            )
            right.append(jnp.where(column == x, 1.0, 0.0).astype(BF16))
        total = total + contract(jnp.concatenate(left, axis=1), jnp.concatenate(right, axis=1))
    return total[:rows] + total[rows:]


def void_kernel(wide, recv_ref, edge_ref, other_edge_ref, s_ref, window_ref, rows_ref):
    w = lax.axis_index("wide")
    depth, lanes, _ = s_ref.shape
    cells = depth * lanes
    rows_ref[...] = jnp.zeros(rows_ref.shape, F32)
    for e in (-1, 0, 1):
        vols, codes = [], []
        for g in range(GROUPS):
            source = w + e - (g - SPREAD)
            inside = jnp.logical_and(source >= 0, source < wide)
            source = jnp.clip(source, 0, wide - 1)
            row = (e + 1) * CAP
            for r in range(CAP):
                k = g * CAP + r
                vol = jnp.where(inside, recv_ref[source, VOL_ROW + row + r : VOL_ROW + row + r + 1, :], 0.0)
                code = recv_ref[source, CELL_ROW + row + r : CELL_ROW + row + r + 1, :]
                vols.append(vol)
                codes.append(code)
                if e == 0:
                    rows_ref[0, k : k + 1, :] = vol
                    rows_ref[1, k : k + 1, :] = code
                    for c in range(3):
                        at = VEL_ROW + c * CAP + r
                        rows_ref[2 + c, k : k + 1, :] = recv_ref[source, at : at + 1, :]
        low = depth - HALO if e < 0 else 0
        layers = depth if e == 0 else HALO
        first = 0 if e >= 0 else (low * lanes) // 16 * 16
        count = cells if e == 0 else -(-(layers * lanes + (low * lanes - first)) // 16) * 16
        solid = solid_of(vols, codes, first, count)
        void = 1.0 - solid_most * solid / (1.0 + solid)
        exists = jnp.logical_and(w + e >= 0, w + e < wide)
        void = jnp.where(exists, void, 0.0)
        base = HALO + (e * HALO if e < 0 else e * depth)
        for z in range(layers):
            start = (low + z) * lanes - first
            window_ref[base + z] = void[start : start + lanes]
    voids = depth + 2 * HALO
    for z in range(depth):
        window_ref[voids + REACH + z] = s_ref[z]
    for e in (-1, 1):
        beside = w + e
        exists = jnp.logical_and(beside >= 0, beside < wide)
        turn = w % 2 == (0 if e > 0 else 1)
        for z in range(REACH):
            part = jnp.where(turn, edge_ref[z], other_edge_ref[z])
            at = voids + (z if e < 0 else REACH + depth + z)
            window_ref[at] = jnp.where(exists, part, 0.0)


def gather_cells(refs, zy, x, rows):
    found = [jnp.zeros(zy.shape, F32) for _ in refs]
    for row in range(rows):
        here = zy == row
        for i, ref in enumerate(refs):
            source = jnp.broadcast_to(ref(row), zy.shape)
            found[i] = jnp.where(here, jnp.take_along_axis(source, x, axis=1), found[i])
    return found


def drag_kernel(window_ref, rows_ref, gas_ref, drag_ref, base_ref):
    _, depth, lanes, _ = gas_ref.shape
    cells = depth * lanes
    vol = rows_ref[0]
    zy, x = cell_rows(rows_ref[1])

    def table(c):
        return lambda row: gas_ref[c, row // lanes, row % lanes : row % lanes + 1, :]

    def voids(row):
        return window_ref[HALO + row // lanes, row % lanes : row % lanes + 1, :]

    gas_z, gas_y, gas_x, void = gather_cells([table(0), table(1), table(2), voids], zy, x, cells)
    slips = [gas_z - rows_ref[2], gas_y - rows_ref[3], gas_x - rows_ref[4]]
    speed = jnp.sqrt(slips[0] * slips[0] + slips[1] * slips[1] + slips[2] * slips[2])
    scale = vol * (drag_base + drag_slope * speed) * jnp.exp(-void_power * jnp.log(void))
    drags = [scale * slip for slip in slips]
    for c in range(3):
        drag_ref[c] = drags[c]
    split = []
    for c in range(3):
        split += list(pieces_of(drags[c]))
    total = jnp.zeros((6 * cells, 128), F32)
    place = iota((cells, 128), 0)
    column = iota((128, 128), 0)
    for pair in range(0, vol.shape[0], 2):
        left, right = [], []
        for k in range(pair, pair + 2):
            here = place == zy[k : k + 1]
            left.append(
                jnp.concatenate([jnp.where(here, part[k : k + 1], 0.0) for part in split], axis=0).astype(BF16)
            )
            right.append(jnp.where(column == x[k : k + 1], 1.0, 0.0).astype(BF16))
        total = total + contract(jnp.concatenate(left, axis=1), jnp.concatenate(right, axis=1))
    for z in range(depth):
        per_void = step_duration / (gas_density * window_ref[HALO + z])
        for c in range(3):
            start = 2 * c * cells + z * lanes
            given = total[start : start + lanes] + total[start + cells : start + cells + lanes]
            base_ref[c, z] = gas_ref[c, z] - per_void * given


def fill_window(pieces, spots, lanes, void_ref, source_ref):
    voids = void_ref.shape[0]
    for piece, spot in zip(pieces, spots):
        at = pl.ds(spot * lanes if isinstance(spot, int) else pl.multiple_of(spot * lanes, lanes), lanes)
        for z in range(voids):
            void_ref[z, at, :] = piece[z]
        for z in range(source_ref.shape[0]):
            source_ref[z, at, :] = piece[voids + z]


def side_masks(lanes, width):
    y, x = iota((lanes, width), 0), iota((lanes, width), 1)
    return (y >= 1, y < lanes - 1, x >= 1, x < width - 1)


def sides(value, masks, step_y, step_x):
    return (
        jnp.where(masks[0], back(value, step_y, 0), 0.0),
        jnp.where(masks[1], ahead(value, step_y, 0), 0.0),
        jnp.where(masks[2], back(value, step_x, 1), 0.0),
        jnp.where(masks[3], ahead(value, step_x, 1), 0.0),
    )


def fine_start(void_ref, source_ref, coef_ref, diag_ref, first_ref):
    layers, lanes, width = source_ref.shape
    masks = side_masks(lanes, width)
    for i in range(layers):
        p = void_ref[i + 1]
        around = (void_ref[i], void_ref[i + 2]) + sides(p, masks, 1, 1)
        sums = [p + q for q in around]
        diag = sums[0] + sums[1] + sums[2] + sums[3] + sums[4] + sums[5]
        inside = p > 0.0
        inverse = jnp.where(inside, relax_weight / jnp.where(inside, diag, 1.0), 0.0)
        for k in range(6):
            coef = sums[k] * inverse
            if k >= 2:
                coef = jnp.where(masks[k - 2], coef, 0.0)
            coef_ref[k, i] = coef
        diag_ref[i] = diag * (0.5 / relax_weight)
        first_ref[i] = (source_ref[i] - p * (1.0 / step_duration)) * inverse * 2.0


def pull(coef_ref, i, below, here, above, step_y=1, step_x=1):
    total = coef_ref[0, i] * below + coef_ref[1, i] * above
    total = total + coef_ref[2, i] * back(here, step_y, 0) + coef_ref[3, i] * ahead(here, step_y, 0)
    return total + coef_ref[4, i] * back(here, step_x, 1) + coef_ref[5, i] * ahead(here, step_x, 1)


def fine_sweep(coef_ref, first_ref, old_ref, new_ref, start, stop):
    for i in range(start, stop):
        here = old_ref[i]
        new_ref[i] = (
            (1.0 - relax_weight) * here
            + first_ref[i]
            + pull(coef_ref, i, old_ref[i - 1], here, old_ref[i + 1])
        )


def spread_matrix(rows, columns, shift):
    return jnp.where(iota((rows, columns), 1) // 2 + shift == iota((rows, columns), 0), 1.0, 0.0)


def mean_matrix(width, shift):
    return jnp.where(iota((width, width), 0) // 2 + shift == iota((width, width), 1), 0.125, 0.0)


def coarsen_kernel(wide, *refs):
    *pieces, send_ref, coef_ref, first_ref, next_ref, void_ref, source_ref, diag_ref, fold_ref = refs
    narrow = len(pieces)
    lanes = pieces[0].shape[1]
    n = lax.axis_index("narrow")
    spots = [n, 1 - n] if narrow == 2 else list(range(narrow))
    fill_window(pieces, spots, lanes, void_ref, source_ref)
    fine_start(void_ref, source_ref, coef_ref, diag_ref, first_ref)
    layers, width_y, width = source_ref.shape
    depth = layers - 2 * REACH
    fine_sweep(coef_ref, first_ref, first_ref, next_ref, 1, layers - 1)
    half = depth // 2
    rows = half * width_y
    for k in range(half):
        total = jnp.zeros((width_y, width), F32)
        for i in (REACH + 2 * k, REACH + 2 * k + 1):
            here = next_ref[i]
            total = total + diag_ref[i] * (
                first_ref[i]
                - relax_weight * here
                + pull(coef_ref, i, next_ref[i - 1], here, next_ref[i + 1])
            )
        fold_ref[0, k * width_y : (k + 1) * width_y, :] = total
        fold_ref[1, k * width_y : (k + 1) * width_y, :] = void_ref[HALO + 2 * k] + void_ref[HALO + 2 * k + 1]
    right = fold_ref[0, pl.ds(0, rows // 2, stride=2), :] + fold_ref[0, pl.ds(1, rows // 2, stride=2), :]
    porous = fold_ref[1, pl.ds(0, rows // 2, stride=2), :] + fold_ref[1, pl.ds(1, rows // 2, stride=2), :]
    coarse = jnp.dot(right, mean_matrix(width, 0), precision=HIGHEST, preferred_element_type=F32)
    coarse = coarse + jnp.dot(porous, mean_matrix(width, width // 2), precision=HIGHEST, preferred_element_type=F32)
    for t in range(wide):
        send_ref[t] = coarse


def loop(count, body, size=1):
    unroll = max(1, UNROLL // size)
    if count <= unroll:
        for i in range(count):
            body(i)
        return
    while count % unroll:
        unroll //= 2

    def step(i, _):
        for j in range(unroll):
            body(i * unroll + j)
        return 0

    lax.fori_loop(0, count // unroll, step, 0)


def close_halves(ref, first_half):
    last = ref.shape[0] - 2
    half = ref.shape[2] // 2
    ref[0] = jnp.where(first_half, 0.0, pltpu.roll(ref[last], half, 1))
    ref[last + 1] = jnp.where(first_half, pltpu.roll(ref[1], half, 1), 0.0)


class Level:
    def __init__(self, index, refs):
        self.index = index
        self.step = 2 ** (index - 1)
        self.porous, self.right, self.coef, self.diag, self.scale, self.first, self.one, self.two = refs
        self.layers, lanes, width = self.right.shape
        half = width // 2
        self.size = -(-lanes // 8)
        y, x = iota((lanes, width), 0), iota((lanes, width), 1) % half
        self.first_half = iota((lanes, width), 1) < half
        self.masks = (y >= self.step, y < lanes - self.step, x >= self.step, x < half - self.step)

    def start(self):
        weight = 0.5 * 0.25**self.index
        close_halves(self.porous, self.first_half)

        def body(i):
            p = self.porous[i + 1]
            around = (self.porous[i], self.porous[i + 2]) + sides(p, self.masks, self.step, self.step)
            sums = [p + q for q in around]
            diag = sums[0] + sums[1] + sums[2] + sums[3] + sums[4] + sums[5]
            inverse = relax_weight / diag
            for k in range(6):
                coef = sums[k] * inverse
                if k >= 2:
                    coef = jnp.where(self.masks[k - 2], coef, 0.0)
                self.coef[k, i] = coef
            self.diag[i] = diag * (weight / relax_weight)
            self.scale[i] = inverse * (1.0 / weight)

        loop(self.layers, body, self.size)

    def begin(self):
        def body(i):
            value = self.right[i] * self.scale[i]
            self.first[i] = value
            self.one[i + 1] = value

        loop(self.layers, body, self.size)

    def sweep(self):
        close_halves(self.one, self.first_half)

        def body(i):
            here = self.one[i + 1]
            self.two[i + 1] = (
                (1.0 - relax_weight) * here
                + self.first[i]
                + pull(self.coef, i, self.one[i], here, self.one[i + 2], self.step, self.step)
            )

        loop(self.layers, body, self.size)
        self.one, self.two = self.two, self.one

    def residual(self, i):
        here = self.one[i + 1]
        return self.diag[i] * (
            self.first[i]
            - relax_weight * here
            + pull(self.coef, i, self.one[i], here, self.one[i + 2], self.step, self.step)
        )

    def mean(self, value):
        y, x = iota(value.shape, 0), iota(value.shape, 1)
        value = value + jnp.where(
            (y & self.step) == 0, ahead(value, self.step, 0), back(value, self.step, 0)
        )
        value = value + jnp.where(
            (x & self.step) == 0, ahead(value, self.step, 1), back(value, self.step, 1)
        )
        return value * 0.125


def coarse_cycle(levels, index):
    level = levels[index]
    level.begin()
    last = index == len(levels) - 1
    for _ in range((COARSE_SWEEPS if last else SWEEPS) - 1):
        level.sweep()
    if not last:
        under = levels[index + 1]
        close_halves(level.one, level.first_half)

        def body(i):
            under.right[i] = level.mean(level.residual(2 * i) + level.residual(2 * i + 1))

        loop(under.layers, body, level.size)
        coarse_cycle(levels, index + 1)

        def add(i):
            correction = under.one[i + 1]
            level.one[2 * i + 1] = level.one[2 * i + 1] + correction
            level.one[2 * i + 2] = level.one[2 * i + 2] + correction

        loop(under.layers, add, level.size)
        for _ in range(SWEEPS):
            level.sweep()


def solve_kernel(wide, recv_ref, coef_ref, first_ref, start_ref, *refs):
    pressure_ref, slope_ref = refs[:2]
    level_refs = [refs[2 + 8 * i : 10 + 8 * i] for i in range(3)]
    one_ref, two_ref, coarse_ref, fold_ref, tilt_ref = refs[26:]
    n = lax.axis_index("narrow")
    w = lax.axis_index("wide")
    lanes = pressure_ref.shape[1]
    layers, width_y, width = first_ref.shape
    depth = layers - 2 * REACH
    half, coarse_y = depth // 2, width_y // 2
    levels = [Level(i + 1, level_refs[i]) for i in range(3)]
    top = levels[0]
    middle = width // 2

    def unpack(t):
        for z in range(half):
            low = recv_ref[t, pl.ds(z * coarse_y, coarse_y), :]
            high = recv_ref[t + wide // 2, pl.ds(z * coarse_y, coarse_y), :]
            top.right[t * half + z] = jnp.where(top.first_half, low, pltpu.roll(high, middle, 1))
            top.porous[t * half + z + 1] = jnp.where(top.first_half, pltpu.roll(low, middle, 1), high)

    loop(wide // 2, unpack, half * top.size)
    for upper, lower in ((levels[0], levels[1]), (levels[1], levels[2])):

        def narrow_down(i):
            lower.porous[i + 1] = upper.mean(upper.porous[2 * i + 1] + upper.porous[2 * i + 2])

        loop(lower.layers, narrow_down, upper.size)
    for level in levels:
        level.start()
    coarse_cycle(levels, 0)

    total = top.layers
    spans = layers // 2
    for k in range(spans):
        z = w * half - REACH // 2 + k
        inside = jnp.logical_and(z >= 0, z < 2 * total)
        z = jnp.clip(z, 0, 2 * total - 1)
        upper = z >= total
        value = top.one[jnp.where(upper, z - total, z) + 1]
        value = jnp.where(upper, pltpu.roll(value, middle, 1), value)
        coarse_ref[k * coarse_y : (k + 1) * coarse_y, :] = jnp.where(inside, value, 0.0)
    wider = jnp.dot(coarse_ref[...], spread_matrix(width, width, 0), precision=HIGHEST, preferred_element_type=F32)
    count = spans * coarse_y
    fold_ref[pl.ds(0, count, stride=2), :] = wider
    fold_ref[pl.ds(1, count, stride=2), :] = wider
    for i in range(1, layers - 1):
        k = i // 2
        correction = fold_ref[k * width_y : (k + 1) * width_y, :]
        one_ref[i] = start_ref[i] + correction
    fine_sweep(coef_ref, first_ref, one_ref, two_ref, 2, layers - 2)
    fine_sweep(coef_ref, first_ref, two_ref, one_ref, 3, layers - 3)

    masks = side_masks(width_y, width)
    own = pl.ds(pl.multiple_of(n * lanes, lanes), lanes)
    for z in range(depth):
        i = REACH + z
        here = one_ref[i]
        before_y, after_y, before_x, after_x = sides(here, masks, 1, 1)
        tilt_ref[0, z] = 0.5 * (one_ref[i + 1] - one_ref[i - 1])
        tilt_ref[1, z] = 0.5 * (after_y - before_y)
        tilt_ref[2, z] = 0.5 * (after_x - before_x)
        pressure_ref[z] = one_ref[i, own, :]
        for c in range(3):
            slope_ref[c, z] = tilt_ref[c, z, own, :]


def force_kernel(wide, rows_ref, drag_ref, slope_ref, send_ref):
    w = lax.axis_index("wide")
    _, depth, lanes, _ = slope_ref.shape
    zy, x = cell_rows(rows_ref[1])

    def table(c):
        return lambda row: slope_ref[c, row // lanes, row % lanes : row % lanes + 1, :]

    slopes = gather_cells([table(0), table(1), table(2)], zy, x, depth * lanes)
    forces = [drag_ref[c] - rows_ref[0] * slopes[c] for c in range(3)]
    for g in range(GROUPS):
        target = w - (g - SPREAD)

        @pl.when(jnp.logical_and(target >= 0, target < wide))
        def _():
            for c in range(3):
                for r in range(CAP):
                    at = (c * CAP + r) * 128
                    send_ref[target, :, at : at + 128] = forces[c][g * CAP + r : g * CAP + r + 1]


def finish_kernel(base_ref, pressure_ref, slope_ref, pressure_out_ref, gas_ref):
    pressure_out_ref[...] = pressure_ref[...]
    gas_ref[...] = base_ref[...] - (step_duration / gas_density) * slope_ref[...]


def contact_kernel(wide, near_ref, count_ref, offset_ref, pos_ref, radius_ref, vel_ref, still_ref, push_ref, seat_ref, across_ref):
    w = lax.axis_index("wide")
    blocks, slots = radius_ref.shape
    neighbours = near_ref.shape[1]
    slot = iota((1, slots), 1)
    for b in range(blocks):
        radius = jnp.where(slot < count_ref[b], radius_ref[b : b + 1, :], -100.0)
        for q in range(4):
            row = pos_ref[q, b : b + 1, :] if q < 3 else radius
            across_ref[q, b] = jnp.broadcast_to(row, (slots, slots)).T

    offsets, rank = ranks(offset_ref, blocks)
    factor = stiffness / (slots * (neighbours + 1))
    for b in range(blocks):
        mine = [jnp.broadcast_to(pos_ref[c, b : b + 1, :], (8, slots)) for c in range(3)]
        mine_radius = jnp.broadcast_to(radius_ref[b : b + 1, :], (8, slots))

        def one(k, sums):
            j = jnp.where(k < neighbours, near_ref[b, jnp.minimum(k, neighbours - 1)], b)
            sums = list(sums)
            for row in range(0, slots, 8):
                apart = [mine[c] - across_ref[c, j, row : row + 8, :] for c in range(3)]
                square = apart[0] * apart[0] + apart[1] * apart[1] + (apart[2] * apart[2] + softening * softening)
                inverse = lax.rsqrt(square)
                overlap = jnp.maximum(mine_radius + across_ref[3, j, row : row + 8, :] - square * inverse, 0.0)
                weight = overlap * inverse
                for c in range(3):
                    sums[c] = sums[c] + apart[c] * weight
            return tuple(sums)

        live = jnp.where(slot < count_ref[b], 1.0, 0.0)
        radius = radius_ref[b : b + 1, :]
        inverse = 1.0 / (particle_density * (radius * radius * radius))
        sums = lax.fori_loop(0, neighbours + 1, one, tuple(jnp.zeros((8, slots), F32) for _ in range(3)))
        for c in range(3):
            force = jnp.sum(sums[c], axis=0, keepdims=True) * factor
            push = force * inverse
            if c == 0:
                push = push + gravity
            still_ref[c, b : b + 1, :] = live * (vel_ref[c, b : b + 1, :] + step_duration * push)
        push_ref[b : b + 1, :] = live * (step_duration * inverse)
        seat_ref[0, b] = jnp.clip(w + offsets[b], 0, wide - 1)
        seat_ref[1, b] = rank[b]


def move_kernel(seat_ref, recv_ref, still_ref, push_ref, out_ref):
    for b in range(push_ref.shape[0]):
        for c in range(3):
            start = pl.multiple_of((c * CAP + seat_ref[1, b]) * 128, 128)
            fluid = recv_ref[seat_ref[0, b], :, pl.ds(start, 128)]
            out_ref[c, b : b + 1, :] = still_ref[c, b : b + 1, :] + push_ref[b : b + 1, :] * fluid


def pairs_of(count, turn):
    lower = range(turn, count - 1, 2)
    return [(i, i + 1) for i in lower] + [(i + 1, i) for i in lower]


def local(
    particle_position,
    particle_velocity,
    radius,
    block_live_count,
    cell_index,
    block_offset,
    neighbours,
    gas_velocity,
    pressure_source,
    void_before,
):
    wide, narrow = lax.axis_size("wide"), lax.axis_size("narrow")
    blocks, slots = radius.shape
    depth, lanes, width = pressure_source.shape
    width_y = lanes * narrow
    voids, layers = depth + 2 * HALO, depth + 2 * REACH
    half, coarse_y = depth // 2, width_y // 2
    slot_rows = -(-GROUPS * CAP // 8) * 8

    send, source, edge, other_edge = call(
        functools.partial(pack_kernel, wide),
        (f32s(wide, SEND_ROWS, width), f32s(depth, lanes, width), f32s(REACH, lanes, width), f32s(REACH, lanes, width)),
        [SMEM, SMEM] + [VMEM] * 5,
        (VMEM,) * 4,
        spare=VMEM_MOST,
    )(block_offset, block_live_count, radius, particle_velocity, cell_index, pressure_source, void_before)
    recv = lax.all_to_all(send, "wide", 0, 0)
    edges = [lax.ppermute(part, "wide", pairs_of(wide, turn)) for turn, part in enumerate((edge, other_edge))]

    still, push, seat = call(
        functools.partial(contact_kernel, wide),
        (f32s(3, blocks, slots), f32s(blocks, slots), jax.ShapeDtypeStruct((2, blocks), jnp.int32)),
        [SMEM, SMEM, SMEM, VMEM, VMEM, VMEM],
        (VMEM, VMEM, SMEM),
        [pltpu.VMEM((4, blocks, slots, slots), F32)],
        flops=56 * 128 * 128 * 20,
    )(neighbours, block_live_count, block_offset, particle_position, radius, particle_velocity)

    window, rows = call(
        functools.partial(void_kernel, wide),
        (f32s(voids + layers, lanes, width), f32s(5, slot_rows, slots)),
        [VMEM] * 4,
        (VMEM, VMEM),
    )(recv, *edges, source)
    if narrow == 2:
        pieces = [window, lax.ppermute(window, "narrow", [(0, 1), (1, 0)])]
    else:
        every = lax.all_gather(window, "narrow")
        pieces = [every[i] for i in range(narrow)]

    plane = (layers, width_y, width)
    coarse, coefs, first, iterate = call(
        functools.partial(coarsen_kernel, wide),
        (f32s(wide, half * coarse_y, width), f32s(6, *plane), f32s(*plane), f32s(*plane)),
        [VMEM] * len(pieces),
        (VMEM,) * 4,
        [
            pltpu.VMEM((voids, width_y, width), F32),
            pltpu.VMEM(plane, F32),
            pltpu.VMEM(plane, F32),
            pltpu.VMEM((2, half * width_y, width), F32),
        ],
    )(*pieces)
    gathered = lax.all_to_all(coarse, "wide", 0, 0)

    drag, base = call(
        drag_kernel,
        (f32s(3, slot_rows, slots), f32s(3, depth, lanes, width)),
        [VMEM] * 3,
        (VMEM, VMEM),
        flops=10_000_000,
    )(window, rows, gas_velocity)

    level_scratch = []
    for index in range(3):
        count = wide * half // 2 >> index
        body = pltpu.VMEM((count, coarse_y, width), F32)
        edged = pltpu.VMEM((count + 2, coarse_y, width), F32)
        level_scratch += [edged, body, pltpu.VMEM((6, count, coarse_y, width), F32), body, body, body, edged, edged]
    gathered, still, push, seat = lax.optimization_barrier((gathered, still, push, seat))
    pressure, slope = call(
        functools.partial(solve_kernel, wide),
        (f32s(depth, lanes, width), f32s(3, depth, lanes, width)),
        [VMEM] * 4,
        (VMEM,) * 2,
        level_scratch
        + [pltpu.VMEM(plane, F32), pltpu.VMEM(plane, F32)]
        + [
            pltpu.VMEM((layers // 2 * coarse_y, width), F32),
            pltpu.VMEM((layers // 2 * width_y, width), F32),
            pltpu.VMEM((3, depth, width_y, width), F32),
        ],
    )(gathered, coefs, first, iterate)
    returning = call(
        functools.partial(force_kernel, wide),
        f32s(wide, 1, 3 * CAP * slots),
        [VMEM] * 3,
        VMEM,
    )(rows, drag, slope)
    returned = lax.all_to_all(returning, "wide", 0, 0)
    pressure, gas_next = call(
        finish_kernel,
        (f32s(depth, lanes, width), f32s(3, depth, lanes, width)),
        [VMEM] * 3,
        (VMEM,) * 2,
        flops=5_000_000,
    )(base, pressure, slope)
    returned, pressure, gas_next = lax.optimization_barrier((returned, pressure, gas_next))

    updated = call(
        move_kernel,
        f32s(3, blocks, slots),
        [SMEM] + [VMEM] * 3,
        VMEM,
    )(seat, returned, still, push)
    return (pressure, gas_next, updated)


def solution(mesh):
    placed = (
        P(None, ("wide", "narrow"), None),
        P(None, ("wide", "narrow"), None),
        P(("wide", "narrow"), None),
        P(("wide", "narrow")),
        P(("wide", "narrow"), None),
        P(("wide", "narrow")),
        P(("wide", "narrow"), None),
        P(None, "wide", "narrow", None),
        P("wide", "narrow", None),
        P("wide", "narrow", None),
    )
    return jax.shard_map(
        local,
        mesh=mesh,
        in_specs=placed,
        out_specs=(
            P("wide", "narrow", None),
            P(None, "wide", "narrow", None),
            P(None, ("wide", "narrow"), None),
        ),
        check_vma=False,
    )
```

```python
import functools
import math

import jax
import jax.numpy as jnp
from jax import lax
from jax.experimental import pallas as pl
from jax.experimental.pallas import tpu as pltpu
from jax.sharding import PartitionSpec as P

SPREAD = 2
SWEEPS = 2
COARSE_SWEEPS = 4
CAP = 3
GROUPS = 2 * SPREAD + 1
HALO = 5
REACH = 4

relax_weight = 0.8
solid_most = 0.6
void_power = 2.65
drag_base = 0.5
drag_slope = 0.5
stiffness = 16.0
softening = 0.1
particle_density = 2.0
gas_density = 1.0
step_duration = 0.25
gravity = -1.0

F32 = jnp.float32
BF16 = jnp.bfloat16
VMEM = pl.BlockSpec(memory_space=pltpu.VMEM)
SMEM = pl.BlockSpec(memory_space=pltpu.SMEM)
HIGHEST = lax.Precision.HIGHEST
VOL_ROW = 0
CELL_ROW = 3 * CAP
VEL_ROW = 6 * CAP
SEND_ROWS = -(-9 * CAP // 8) * 8
UNROLL = 32
VMEM_SPARE = 4 * 1024 * 1024
VMEM_MOST = 60 * 1024 * 1024


def call(kernel, out_shape, in_specs, out_specs, scratch=(), flops=0, spare=VMEM_SPARE):
    def run(*args):
        held = [*args, *jax.tree.leaves(out_shape), *scratch]
        need = sum(4 * math.prod(array.shape) for array in held)
        return pl.pallas_call(
            kernel,
            out_shape=out_shape,
            in_specs=in_specs,
            out_specs=out_specs,
            scratch_shapes=list(scratch),
            compiler_params=pltpu.CompilerParams(vmem_limit_bytes=min(2 * need + spare, VMEM_MOST)),
            cost_estimate=pl.CostEstimate(flops=flops, bytes_accessed=1 << 18, transcendentals=0),
        )(*args)

    return run


def f32s(*shape):
    return jax.ShapeDtypeStruct(shape, F32)


def iota(shape, dim):
    return lax.broadcasted_iota(jnp.int32, shape, dim)


def back(value, step, axis):
    return pltpu.roll(value, step, axis)


def ahead(value, step, axis):
    return pltpu.roll(value, value.shape[axis] - step, axis)


def ranks(offset_ref, count):
    offsets = [offset_ref[i] for i in range(count)]
    found = []
    for i in range(count):
        rank = jnp.int32(0)
        for j in range(i):
            rank = rank + jnp.where(offsets[j] == offsets[i], 1, 0)
        found.append(rank)
    return offsets, found


def pack_kernel(wide, offset_ref, count_ref, radius_ref, vel_ref, cell_ref, source_ref, before_ref, send_ref, s_ref, edge_ref, other_edge_ref):
    w = lax.axis_index("wide")
    blocks, slots = radius_ref.shape
    depth, lanes, _ = source_ref.shape
    send_ref[...] = jnp.zeros(send_ref.shape, F32)
    offsets, rank = ranks(offset_ref, blocks)
    slot = iota((1, slots), 1)
    for b in range(blocks):
        radius = radius_ref[b : b + 1, :]
        vol = jnp.where(slot < count_ref[b], radius * radius * radius, 0.0)
        cell = cell_ref[b : b + 1, :].astype(F32)
        for e in (-1, 0, 1):
            target = w + offsets[b] - e

            @pl.when(jnp.logical_and(target >= 0, target < wide))
            def _():
                row = (e + 1) * CAP + rank[b]
                send_ref[target, pl.ds(VOL_ROW + row, 1), :] = vol
                send_ref[target, pl.ds(CELL_ROW + row, 1), :] = cell
                if e == 0:
                    for c in range(3):
                        send_ref[target, pl.ds(VEL_ROW + c * CAP + rank[b], 1), :] = vel_ref[c, b : b + 1, :]

    for z in range(depth):
        s_ref[z] = source_ref[z] + before_ref[z] * (1.0 / step_duration)

    for turn, ref in enumerate((edge_ref, other_edge_ref)):
        upward = w % 2 == turn
        for z in range(REACH):
            ref[z] = jnp.where(upward, s_ref[depth - REACH + z], s_ref[z])


def cell_rows(cell_row):
    cell = cell_row.astype(jnp.int32)
    return cell >> 7, cell & 127


def pieces_of(value):
    high = value.astype(BF16).astype(F32)
    return high, value - high


def contract(lhs, rhs):
    return lax.dot_general(lhs, rhs, (((1,), (1,)), ((), ())), preferred_element_type=F32)


def solid_of(vols, cells, first, rows):
    total = jnp.zeros((2 * rows, 128), F32)
    place = iota((rows, 128), 0) + first
    column = iota((128, 128), 0)
    for pair in range(0, len(vols), 2):
        left, right = [], []
        for k in range(pair, min(pair + 2, len(vols))):
            zy, x = cell_rows(cells[k])
            here = place == zy
            high, low = pieces_of(vols[k])
            left.append(
                jnp.concatenate([jnp.where(here, high, 0.0), jnp.where(here, low, 0.0)], axis=0).astype(BF16)
            )
            right.append(jnp.where(column == x, 1.0, 0.0).astype(BF16))
        total = total + contract(jnp.concatenate(left, axis=1), jnp.concatenate(right, axis=1))
    return total[:rows] + total[rows:]


def void_kernel(wide, recv_ref, edge_ref, other_edge_ref, s_ref, window_ref, rows_ref):
    w = lax.axis_index("wide")
    depth, lanes, _ = s_ref.shape
    cells = depth * lanes
    rows_ref[...] = jnp.zeros(rows_ref.shape, F32)
    for e in (-1, 0, 1):
        vols, codes = [], []
        for g in range(GROUPS):
            source = w + e - (g - SPREAD)
            inside = jnp.logical_and(source >= 0, source < wide)
            source = jnp.clip(source, 0, wide - 1)
            row = (e + 1) * CAP
            for r in range(CAP):
                k = g * CAP + r
                vol = jnp.where(inside, recv_ref[source, VOL_ROW + row + r : VOL_ROW + row + r + 1, :], 0.0)
                code = recv_ref[source, CELL_ROW + row + r : CELL_ROW + row + r + 1, :]
                vols.append(vol)
                codes.append(code)
                if e == 0:
                    rows_ref[0, k : k + 1, :] = vol
                    rows_ref[1, k : k + 1, :] = code
                    for c in range(3):
                        at = VEL_ROW + c * CAP + r
                        rows_ref[2 + c, k : k + 1, :] = recv_ref[source, at : at + 1, :]
        low = depth - HALO if e < 0 else 0
        layers = depth if e == 0 else HALO
        first = 0 if e >= 0 else (low * lanes) // 16 * 16
        count = cells if e == 0 else -(-(layers * lanes + (low * lanes - first)) // 16) * 16
        solid = solid_of(vols, codes, first, count)
        void = 1.0 - solid_most * solid / (1.0 + solid)
        exists = jnp.logical_and(w + e >= 0, w + e < wide)
        void = jnp.where(exists, void, 0.0)
        base = HALO + (e * HALO if e < 0 else e * depth)
        for z in range(layers):
            start = (low + z) * lanes - first
            window_ref[base + z] = void[start : start + lanes]
    voids = depth + 2 * HALO
    for z in range(depth):
        window_ref[voids + REACH + z] = s_ref[z]
    for e in (-1, 1):
        beside = w + e
        exists = jnp.logical_and(beside >= 0, beside < wide)
        turn = w % 2 == (0 if e > 0 else 1)
        for z in range(REACH):
            part = jnp.where(turn, edge_ref[z], other_edge_ref[z])
            at = voids + (z if e < 0 else REACH + depth + z)
            window_ref[at] = jnp.where(exists, part, 0.0)


def gather_cells(refs, zy, x, rows):
    found = [jnp.zeros(zy.shape, F32) for _ in refs]
    for row in range(rows):
        here = zy == row
        for i, ref in enumerate(refs):
            source = jnp.broadcast_to(ref(row), zy.shape)
            found[i] = jnp.where(here, jnp.take_along_axis(source, x, axis=1), found[i])
    return found


def drag_kernel(window_ref, rows_ref, gas_ref, drag_ref, base_ref):
    _, depth, lanes, _ = gas_ref.shape
    cells = depth * lanes
    vol = rows_ref[0]
    zy, x = cell_rows(rows_ref[1])

    def table(c):
        return lambda row: gas_ref[c, row // lanes, row % lanes : row % lanes + 1, :]

    def voids(row):
        return window_ref[HALO + row // lanes, row % lanes : row % lanes + 1, :]

    gas_z, gas_y, gas_x, void = gather_cells([table(0), table(1), table(2), voids], zy, x, cells)
    slips = [gas_z - rows_ref[2], gas_y - rows_ref[3], gas_x - rows_ref[4]]
    speed = jnp.sqrt(slips[0] * slips[0] + slips[1] * slips[1] + slips[2] * slips[2])
    scale = vol * (drag_base + drag_slope * speed) * jnp.exp(-void_power * jnp.log(void))
    drags = [scale * slip for slip in slips]
    for c in range(3):
        drag_ref[c] = drags[c]
    split = []
    for c in range(3):
        split += list(pieces_of(drags[c]))
    total = jnp.zeros((6 * cells, 128), F32)
    place = iota((cells, 128), 0)
    column = iota((128, 128), 0)
    for pair in range(0, vol.shape[0], 2):
        left, right = [], []
        for k in range(pair, pair + 2):
            here = place == zy[k : k + 1]
            left.append(
                jnp.concatenate([jnp.where(here, part[k : k + 1], 0.0) for part in split], axis=0).astype(BF16)
            )
            right.append(jnp.where(column == x[k : k + 1], 1.0, 0.0).astype(BF16))
        total = total + contract(jnp.concatenate(left, axis=1), jnp.concatenate(right, axis=1))
    for z in range(depth):
        per_void = step_duration / (gas_density * window_ref[HALO + z])
        for c in range(3):
            start = 2 * c * cells + z * lanes
            given = total[start : start + lanes] + total[start + cells : start + cells + lanes]
            base_ref[c, z] = gas_ref[c, z] - per_void * given


def fill_window(pieces, spots, lanes, void_ref, source_ref):
    voids = void_ref.shape[0]
    for piece, spot in zip(pieces, spots):
        at = pl.ds(spot * lanes if isinstance(spot, int) else pl.multiple_of(spot * lanes, lanes), lanes)
        for z in range(voids):
            void_ref[z, at, :] = piece[z]
        for z in range(source_ref.shape[0]):
            source_ref[z, at, :] = piece[voids + z]


def side_masks(lanes, width):
    y, x = iota((lanes, width), 0), iota((lanes, width), 1)
    return (y >= 1, y < lanes - 1, x >= 1, x < width - 1)


def sides(value, masks, step_y, step_x):
    return (
        jnp.where(masks[0], back(value, step_y, 0), 0.0),
        jnp.where(masks[1], ahead(value, step_y, 0), 0.0),
        jnp.where(masks[2], back(value, step_x, 1), 0.0),
        jnp.where(masks[3], ahead(value, step_x, 1), 0.0),
    )


def fine_start(void_ref, source_ref, coef_ref, diag_ref, first_ref):
    layers, lanes, width = source_ref.shape
    masks = side_masks(lanes, width)
    for i in range(layers):
        p = void_ref[i + 1]
        around = (void_ref[i], void_ref[i + 2]) + sides(p, masks, 1, 1)
        sums = [p + q for q in around]
        diag = sums[0] + sums[1] + sums[2] + sums[3] + sums[4] + sums[5]
        inside = p > 0.0
        inverse = jnp.where(inside, relax_weight / jnp.where(inside, diag, 1.0), 0.0)
        for k in range(6):
            coef = sums[k] * inverse
            if k >= 2:
                coef = jnp.where(masks[k - 2], coef, 0.0)
            coef_ref[k, i] = coef
        diag_ref[i] = diag * (0.5 / relax_weight)
        first_ref[i] = (source_ref[i] - p * (1.0 / step_duration)) * inverse * 2.0


def pull(coef_ref, i, below, here, above, step_y=1, step_x=1):
    total = coef_ref[0, i] * below + coef_ref[1, i] * above
    total = total + coef_ref[2, i] * back(here, step_y, 0) + coef_ref[3, i] * ahead(here, step_y, 0)
    return total + coef_ref[4, i] * back(here, step_x, 1) + coef_ref[5, i] * ahead(here, step_x, 1)


def fine_sweep(coef_ref, first_ref, old_ref, new_ref, start, stop):
    for i in range(start, stop):
        here = old_ref[i]
        new_ref[i] = (
            (1.0 - relax_weight) * here
            + first_ref[i]
            + pull(coef_ref, i, old_ref[i - 1], here, old_ref[i + 1])
        )


def spread_matrix(rows, columns, shift):
    return jnp.where(iota((rows, columns), 1) // 2 + shift == iota((rows, columns), 0), 1.0, 0.0)


def mean_matrix(width, shift):
    return jnp.where(iota((width, width), 0) // 2 + shift == iota((width, width), 1), 0.125, 0.0)


def coarsen_kernel(wide, *refs):
    *pieces, send_ref, coef_ref, first_ref, next_ref, void_ref, source_ref, diag_ref, fold_ref = refs
    narrow = len(pieces)
    lanes = pieces[0].shape[1]
    n = lax.axis_index("narrow")
    spots = [n, 1 - n] if narrow == 2 else list(range(narrow))
    fill_window(pieces, spots, lanes, void_ref, source_ref)
    fine_start(void_ref, source_ref, coef_ref, diag_ref, first_ref)
    layers, width_y, width = source_ref.shape
    depth = layers - 2 * REACH
    fine_sweep(coef_ref, first_ref, first_ref, next_ref, 1, layers - 1)
    half = depth // 2
    rows = half * width_y
    for k in range(half):
        total = jnp.zeros((width_y, width), F32)
        for i in (REACH + 2 * k, REACH + 2 * k + 1):
            here = next_ref[i]
            total = total + diag_ref[i] * (
                first_ref[i]
                - relax_weight * here
                + pull(coef_ref, i, next_ref[i - 1], here, next_ref[i + 1])
            )
        fold_ref[0, k * width_y : (k + 1) * width_y, :] = total
        fold_ref[1, k * width_y : (k + 1) * width_y, :] = void_ref[HALO + 2 * k] + void_ref[HALO + 2 * k + 1]
    right = fold_ref[0, pl.ds(0, rows // 2, stride=2), :] + fold_ref[0, pl.ds(1, rows // 2, stride=2), :]
    porous = fold_ref[1, pl.ds(0, rows // 2, stride=2), :] + fold_ref[1, pl.ds(1, rows // 2, stride=2), :]
    coarse = jnp.dot(right, mean_matrix(width, 0), precision=HIGHEST, preferred_element_type=F32)
    coarse = coarse + jnp.dot(porous, mean_matrix(width, width // 2), precision=HIGHEST, preferred_element_type=F32)
    coarse_y, part_y = width_y // 2, lanes // 2
    for k in range(half):
        part = coarse[k * coarse_y : k * coarse_y + part_y]
        for i in range(1, narrow):
            start = k * coarse_y + i * part_y
            part = jnp.where(n == i, coarse[start : start + part_y], part)
        for t in range(wide):
            send_ref[t, k * part_y : (k + 1) * part_y, :] = part


def loop(count, body, size=1):
    unroll = max(1, UNROLL // size)
    if count <= unroll:
        for i in range(count):
            body(i)
        return
    while count % unroll:
        unroll //= 2

    def step(i, _):
        for j in range(unroll):
            body(i * unroll + j)
        return 0

    lax.fori_loop(0, count // unroll, step, 0)


def close_halves(ref, first_half):
    last = ref.shape[0] - 2
    half = ref.shape[2] // 2
    ref[0] = jnp.where(first_half, 0.0, pltpu.roll(ref[last], half, 1))
    ref[last + 1] = jnp.where(first_half, pltpu.roll(ref[1], half, 1), 0.0)


class Level:
    def __init__(self, index, refs):
        self.index = index
        self.step = 2 ** (index - 1)
        self.porous, self.right, self.coef, self.diag, self.scale, self.first, self.one, self.two = refs
        self.layers, lanes, width = self.right.shape
        half = width // 2
        self.size = -(-lanes // 8)
        y, x = iota((lanes, width), 0), iota((lanes, width), 1) % half
        self.first_half = iota((lanes, width), 1) < half
        self.masks = (y >= self.step, y < lanes - self.step, x >= self.step, x < half - self.step)

    def start(self):
        weight = 0.5 * 0.25**self.index
        close_halves(self.porous, self.first_half)

        def body(i):
            p = self.porous[i + 1]
            around = (self.porous[i], self.porous[i + 2]) + sides(p, self.masks, self.step, self.step)
            sums = [p + q for q in around]
            diag = sums[0] + sums[1] + sums[2] + sums[3] + sums[4] + sums[5]
            inverse = relax_weight / diag
            for k in range(6):
                coef = sums[k] * inverse
                if k >= 2:
                    coef = jnp.where(self.masks[k - 2], coef, 0.0)
                self.coef[k, i] = coef
            self.diag[i] = diag * (weight / relax_weight)
            self.scale[i] = inverse * (1.0 / weight)

        loop(self.layers, body, self.size)

    def begin(self):
        def body(i):
            value = self.right[i] * self.scale[i]
            self.first[i] = value
            self.one[i + 1] = value

        loop(self.layers, body, self.size)

    def sweep(self):
        close_halves(self.one, self.first_half)

        def body(i):
            here = self.one[i + 1]
            self.two[i + 1] = (
                (1.0 - relax_weight) * here
                + self.first[i]
                + pull(self.coef, i, self.one[i], here, self.one[i + 2], self.step, self.step)
            )

        loop(self.layers, body, self.size)
        self.one, self.two = self.two, self.one

    def residual(self, i):
        here = self.one[i + 1]
        return self.diag[i] * (
            self.first[i]
            - relax_weight * here
            + pull(self.coef, i, self.one[i], here, self.one[i + 2], self.step, self.step)
        )

    def mean(self, value):
        y, x = iota(value.shape, 0), iota(value.shape, 1)
        value = value + jnp.where(
            (y & self.step) == 0, ahead(value, self.step, 0), back(value, self.step, 0)
        )
        value = value + jnp.where(
            (x & self.step) == 0, ahead(value, self.step, 1), back(value, self.step, 1)
        )
        return value * 0.125


def coarse_cycle(levels, index):
    level = levels[index]
    level.begin()
    last = index == len(levels) - 1
    for _ in range((COARSE_SWEEPS if last else SWEEPS) - 1):
        level.sweep()
    if not last:
        under = levels[index + 1]
        close_halves(level.one, level.first_half)

        def body(i):
            under.right[i] = level.mean(level.residual(2 * i) + level.residual(2 * i + 1))

        loop(under.layers, body, level.size)
        coarse_cycle(levels, index + 1)

        def add(i):
            correction = under.one[i + 1]
            level.one[2 * i + 1] = level.one[2 * i + 1] + correction
            level.one[2 * i + 2] = level.one[2 * i + 2] + correction

        loop(under.layers, add, level.size)
        for _ in range(SWEEPS):
            level.sweep()


def solve_kernel(wide, narrow, *refs):
    part_refs, (coef_ref, first_ref, start_ref), refs = refs[:narrow], refs[narrow : narrow + 3], refs[narrow + 3 :]
    pressure_ref, slope_ref = refs[:2]
    level_refs = [refs[2 + 8 * i : 10 + 8 * i] for i in range(3)]
    one_ref, two_ref, coarse_ref, fold_ref, tilt_ref = refs[26:]
    n = lax.axis_index("narrow")
    w = lax.axis_index("wide")
    lanes = pressure_ref.shape[1]
    layers, width_y, width = first_ref.shape
    depth = layers - 2 * REACH
    half, coarse_y = depth // 2, width_y // 2
    levels = [Level(i + 1, level_refs[i]) for i in range(3)]
    top = levels[0]
    middle = width // 2

    part_y = coarse_y // narrow

    def whole(t, z):
        parts = [ref[t, z * part_y : (z + 1) * part_y, :] for ref in part_refs]
        if narrow == 2:
            parts = [jnp.where(n == 0, parts[0], parts[1]), jnp.where(n == 0, parts[1], parts[0])]
        return jnp.concatenate(parts, axis=0)

    def unpack(t):
        for z in range(half):
            low, high = whole(t, z), whole(t + wide // 2, z)
            top.right[t * half + z] = jnp.where(top.first_half, low, pltpu.roll(high, middle, 1))
            top.porous[t * half + z + 1] = jnp.where(top.first_half, pltpu.roll(low, middle, 1), high)

    loop(wide // 2, unpack, half * top.size)
    for upper, lower in ((levels[0], levels[1]), (levels[1], levels[2])):

        def narrow_down(i):
            lower.porous[i + 1] = upper.mean(upper.porous[2 * i + 1] + upper.porous[2 * i + 2])

        loop(lower.layers, narrow_down, upper.size)
    for level in levels:
        level.start()
    coarse_cycle(levels, 0)

    total = top.layers
    spans = layers // 2
    for k in range(spans):
        z = w * half - REACH // 2 + k
        inside = jnp.logical_and(z >= 0, z < 2 * total)
        z = jnp.clip(z, 0, 2 * total - 1)
        upper = z >= total
        value = top.one[jnp.where(upper, z - total, z) + 1]
        value = jnp.where(upper, pltpu.roll(value, middle, 1), value)
        coarse_ref[k * coarse_y : (k + 1) * coarse_y, :] = jnp.where(inside, value, 0.0)
    wider = jnp.dot(coarse_ref[...], spread_matrix(width, width, 0), precision=HIGHEST, preferred_element_type=F32)
    count = spans * coarse_y
    fold_ref[pl.ds(0, count, stride=2), :] = wider
    fold_ref[pl.ds(1, count, stride=2), :] = wider
    for i in range(1, layers - 1):
        k = i // 2
        correction = fold_ref[k * width_y : (k + 1) * width_y, :]
        one_ref[i] = start_ref[i] + correction
    fine_sweep(coef_ref, first_ref, one_ref, two_ref, 2, layers - 2)
    fine_sweep(coef_ref, first_ref, two_ref, one_ref, 3, layers - 3)

    masks = side_masks(width_y, width)
    own = pl.ds(pl.multiple_of(n * lanes, lanes), lanes)
    for z in range(depth):
        i = REACH + z
        here = one_ref[i]
        before_y, after_y, before_x, after_x = sides(here, masks, 1, 1)
        tilt_ref[0, z] = 0.5 * (one_ref[i + 1] - one_ref[i - 1])
        tilt_ref[1, z] = 0.5 * (after_y - before_y)
        tilt_ref[2, z] = 0.5 * (after_x - before_x)
        pressure_ref[z] = one_ref[i, own, :]
        for c in range(3):
            slope_ref[c, z] = tilt_ref[c, z, own, :]


def force_kernel(wide, rows_ref, drag_ref, slope_ref, send_ref):
    w = lax.axis_index("wide")
    _, depth, lanes, _ = slope_ref.shape
    zy, x = cell_rows(rows_ref[1])

    def table(c):
        return lambda row: slope_ref[c, row // lanes, row % lanes : row % lanes + 1, :]

    slopes = gather_cells([table(0), table(1), table(2)], zy, x, depth * lanes)
    forces = [drag_ref[c] - rows_ref[0] * slopes[c] for c in range(3)]
    for g in range(GROUPS):
        target = w - (g - SPREAD)

        @pl.when(jnp.logical_and(target >= 0, target < wide))
        def _():
            for c in range(3):
                for r in range(CAP):
                    at = (c * CAP + r) * 128
                    send_ref[target, :, at : at + 128] = forces[c][g * CAP + r : g * CAP + r + 1]


def finish_kernel(base_ref, pressure_ref, slope_ref, pressure_out_ref, gas_ref):
    pressure_out_ref[...] = pressure_ref[...]
    gas_ref[...] = base_ref[...] - (step_duration / gas_density) * slope_ref[...]


def contact_kernel(wide, chosen, near_ref, count_ref, offset_ref, pos_ref, radius_ref, vel_ref, seat_ref, still_ref, push_ref, across_ref):
    w = lax.axis_index("wide")
    blocks, slots = radius_ref.shape
    neighbours = near_ref.shape[1]
    slot = iota((1, slots), 1)
    reach = [jnp.where(slot < count_ref[b], radius_ref[b : b + 1, :], -100.0) for b in range(blocks)]
    upright = jnp.concatenate([pos_ref[0], pos_ref[1], pos_ref[2]] + reach, axis=0).T
    for q in range(4):
        for b in range(blocks):
            at = q * blocks + b
            across_ref[q, b] = jnp.broadcast_to(upright[:, at : at + 1], (slots, slots))

    offsets, rank = ranks(offset_ref, blocks)
    factor = stiffness / (slots * (neighbours + 1))
    for b in chosen:
        at = b - chosen[0]
        mine = [jnp.broadcast_to(pos_ref[c, b : b + 1, :], (8, slots)) for c in range(3)]
        mine_radius = jnp.broadcast_to(radius_ref[b : b + 1, :], (8, slots))

        def one(k, sums):
            j = jnp.where(k < neighbours, near_ref[b, jnp.minimum(k, neighbours - 1)], b)
            sums = list(sums)
            for row in range(0, slots, 8):
                apart = [mine[c] - across_ref[c, j, row : row + 8, :] for c in range(3)]
                square = apart[0] * apart[0] + apart[1] * apart[1] + (apart[2] * apart[2] + softening * softening)
                inverse = lax.rsqrt(square)
                overlap = jnp.maximum(mine_radius + across_ref[3, j, row : row + 8, :] - square * inverse, 0.0)
                weight = overlap * inverse
                for c in range(3):
                    sums[c] = sums[c] + apart[c] * weight
            return tuple(sums)

        live = jnp.where(slot < count_ref[b], 1.0, 0.0)
        radius = radius_ref[b : b + 1, :]
        inverse = 1.0 / (particle_density * (radius * radius * radius))
        sums = lax.fori_loop(0, neighbours + 1, one, tuple(jnp.zeros((8, slots), F32) for _ in range(3)))
        for c in range(3):
            force = jnp.sum(sums[c], axis=0, keepdims=True) * factor
            push = force * inverse
            if c == 0:
                push = push + gravity
            still_ref[c, at : at + 1, :] = live * (vel_ref[c, b : b + 1, :] + step_duration * push)
        push_ref[at : at + 1, :] = live * (step_duration * inverse)
        seat_ref[0, at] = jnp.clip(w + offsets[b], 0, wide - 1)
        seat_ref[1, at] = rank[b]


def move_kernel(*refs):
    *refs, recv_ref, out_ref = refs
    b = 0
    for seat_ref, still_ref, push_ref in zip(refs[0::3], refs[1::3], refs[2::3]):
        for at in range(push_ref.shape[0]):
            for c in range(3):
                start = pl.multiple_of((c * CAP + seat_ref[1, at]) * 128, 128)
                fluid = recv_ref[seat_ref[0, at], :, pl.ds(start, 128)]
                out_ref[c, b : b + 1, :] = still_ref[c, at : at + 1, :] + push_ref[at : at + 1, :] * fluid
            b += 1


def share(block, narrow):
    if narrow == 2:
        return [block, lax.ppermute(block, "narrow", [(0, 1), (1, 0)])]
    every = lax.all_gather(block, "narrow")
    return [every[i] for i in range(narrow)]


def pairs_of(count, turn):
    lower = range(turn, count - 1, 2)
    return [(i, i + 1) for i in lower] + [(i + 1, i) for i in lower]


def local(
    particle_position,
    particle_velocity,
    radius,
    block_live_count,
    cell_index,
    block_offset,
    neighbours,
    gas_velocity,
    pressure_source,
    void_before,
):
    wide, narrow = lax.axis_size("wide"), lax.axis_size("narrow")
    blocks, slots = radius.shape
    depth, lanes, width = pressure_source.shape
    width_y = lanes * narrow
    voids, layers = depth + 2 * HALO, depth + 2 * REACH
    half, coarse_y = depth // 2, width_y // 2
    slot_rows = -(-GROUPS * CAP // 8) * 8

    send, source, edge, other_edge = call(
        functools.partial(pack_kernel, wide),
        (f32s(wide, SEND_ROWS, width), f32s(depth, lanes, width), f32s(REACH, lanes, width), f32s(REACH, lanes, width)),
        [SMEM, SMEM] + [VMEM] * 5,
        (VMEM,) * 4,
        spare=VMEM_MOST,
    )(block_offset, block_live_count, radius, particle_velocity, cell_index, pressure_source, void_before)
    recv = lax.all_to_all(send, "wide", 0, 0)
    edges = [lax.ppermute(part, "wide", pairs_of(wide, turn)) for turn, part in enumerate((edge, other_edge))]

    def contact(chosen):
        count = len(chosen)
        return call(
            functools.partial(contact_kernel, wide, chosen),
            (jax.ShapeDtypeStruct((2, count), jnp.int32), f32s(3, count, slots), f32s(count, slots)),
            [SMEM, SMEM, SMEM, VMEM, VMEM, VMEM],
            (SMEM, VMEM, VMEM),
            [pltpu.VMEM((4, blocks, slots, slots), F32)],
            flops=28 * 128 * 128 * 20,
        )(neighbours, block_live_count, block_offset, particle_position, radius, particle_velocity)

    early = blocks * 3 // 8
    recv, moved = lax.optimization_barrier((recv, contact(range(early))))
    window, rows = call(
        functools.partial(void_kernel, wide),
        (f32s(voids + layers, lanes, width), f32s(5, slot_rows, slots)),
        [VMEM] * 4,
        (VMEM, VMEM),
    )(recv, *edges, source)
    pieces = share(window, narrow)

    plane = (layers, width_y, width)
    coarse, coefs, first, iterate = call(
        functools.partial(coarsen_kernel, wide),
        (f32s(wide, half * lanes // 2, width), f32s(6, *plane), f32s(*plane), f32s(*plane)),
        [VMEM] * len(pieces),
        (VMEM,) * 4,
        [
            pltpu.VMEM((voids, width_y, width), F32),
            pltpu.VMEM(plane, F32),
            pltpu.VMEM(plane, F32),
            pltpu.VMEM((2, half * width_y, width), F32),
        ],
    )(*pieces)
    gathered = lax.all_to_all(coarse, "wide", 0, 0)

    drag, base = call(
        drag_kernel,
        (f32s(3, slot_rows, slots), f32s(3, depth, lanes, width)),
        [VMEM] * 3,
        (VMEM, VMEM),
        flops=10_000_000,
    )(window, rows, gas_velocity)

    gathered, moved_too = lax.optimization_barrier((gathered, contact(range(early, blocks))))
    parts = share(gathered, narrow)

    level_scratch = []
    for index in range(3):
        count = wide * half // 2 >> index
        body = pltpu.VMEM((count, coarse_y, width), F32)
        edged = pltpu.VMEM((count + 2, coarse_y, width), F32)
        level_scratch += [edged, body, pltpu.VMEM((6, count, coarse_y, width), F32), body, body, body, edged, edged]
    pressure, slope = call(
        functools.partial(solve_kernel, wide, narrow),
        (f32s(depth, lanes, width), f32s(3, depth, lanes, width)),
        [VMEM] * (narrow + 3),
        (VMEM,) * 2,
        level_scratch
        + [pltpu.VMEM(plane, F32), pltpu.VMEM(plane, F32)]
        + [
            pltpu.VMEM((layers // 2 * coarse_y, width), F32),
            pltpu.VMEM((layers // 2 * width_y, width), F32),
            pltpu.VMEM((3, depth, width_y, width), F32),
        ],
    )(*parts, coefs, first, iterate)
    returning = call(
        functools.partial(force_kernel, wide),
        f32s(wide, 1, 3 * CAP * slots),
        [VMEM] * 3,
        VMEM,
    )(rows, drag, slope)
    returned = lax.all_to_all(returning, "wide", 0, 0)
    pressure, gas_next = call(
        finish_kernel,
        (f32s(depth, lanes, width), f32s(3, depth, lanes, width)),
        [VMEM] * 3,
        (VMEM,) * 2,
        flops=5_000_000,
    )(base, pressure, slope)
    returned, pressure, gas_next = lax.optimization_barrier((returned, pressure, gas_next))

    updated = call(
        move_kernel,
        f32s(3, blocks, slots),
        [SMEM, VMEM, VMEM] * 2 + [VMEM],
        VMEM,
    )(*moved, *moved_too, returned)
    return (pressure, gas_next, updated)


def solution(mesh):
    placed = (
        P(None, ("wide", "narrow"), None),
        P(None, ("wide", "narrow"), None),
        P(("wide", "narrow"), None),
        P(("wide", "narrow")),
        P(("wide", "narrow"), None),
        P(("wide", "narrow")),
        P(("wide", "narrow"), None),
        P(None, "wide", "narrow", None),
        P("wide", "narrow", None),
        P("wide", "narrow", None),
    )
    return jax.shard_map(
        local,
        mesh=mesh,
        in_specs=placed,
        out_specs=(
            P("wide", "narrow", None),
            P(None, "wide", "narrow", None),
            P(None, ("wide", "narrow"), None),
        ),
        check_vma=False,
    )
```

```python
import functools
import math

import jax
import jax.numpy as jnp
from jax import lax
from jax.experimental import pallas as pl
from jax.experimental.pallas import tpu as pltpu
from jax.sharding import PartitionSpec as P

SPREAD = 2
SWEEPS = 2
COARSE_SWEEPS = 4
CAP = 3
GROUPS = 2 * SPREAD + 1
HALO = 5
REACH = 4

relax_weight = 0.8
solid_most = 0.6
void_power = 2.65
drag_base = 0.5
drag_slope = 0.5
stiffness = 16.0
softening = 0.1
particle_density = 2.0
gas_density = 1.0
step_duration = 0.25
gravity = -1.0

F32 = jnp.float32
BF16 = jnp.bfloat16
VMEM = pl.BlockSpec(memory_space=pltpu.VMEM)
SMEM = pl.BlockSpec(memory_space=pltpu.SMEM)
HIGHEST = lax.Precision.HIGHEST
VOL_ROW = 0
CELL_ROW = 3 * CAP
VEL_ROW = 6 * CAP
SEND_ROWS = -(-9 * CAP // 8) * 8
UNROLL = 32
VMEM_SPARE = 4 * 1024 * 1024
VMEM_MOST = 60 * 1024 * 1024


def call(kernel, out_shape, in_specs, out_specs, scratch=(), flops=0, spare=VMEM_SPARE):
    def run(*args):
        held = [*args, *jax.tree.leaves(out_shape), *scratch]
        need = sum(4 * math.prod(array.shape) for array in held)
        return pl.pallas_call(
            kernel,
            out_shape=out_shape,
            in_specs=in_specs,
            out_specs=out_specs,
            scratch_shapes=list(scratch),
            compiler_params=pltpu.CompilerParams(vmem_limit_bytes=min(2 * need + spare, VMEM_MOST)),
            cost_estimate=pl.CostEstimate(flops=flops, bytes_accessed=1 << 18, transcendentals=0),
        )(*args)

    return run


def f32s(*shape):
    return jax.ShapeDtypeStruct(shape, F32)


def iota(shape, dim):
    return lax.broadcasted_iota(jnp.int32, shape, dim)


def back(value, step, axis):
    return pltpu.roll(value, step, axis)


def ahead(value, step, axis):
    return pltpu.roll(value, value.shape[axis] - step, axis)


def ranks(offset_ref, count):
    offsets = [offset_ref[i] for i in range(count)]
    found = []
    for i in range(count):
        rank = 0
        for j in range(i):
            rank = rank + jnp.where(offsets[j] == offsets[i], 1, 0)
        found.append(rank)
    return offsets, found


def pack_kernel(wide, offset_ref, count_ref, radius_ref, vel_ref, cell_ref, source_ref, before_ref, send_ref, s_ref, edge_ref, other_edge_ref, slot_ref):
    w = lax.axis_index("wide")
    blocks, slots = radius_ref.shape
    depth, lanes, _ = source_ref.shape
    slot_ref[...] = jnp.zeros(slot_ref.shape, F32)
    for d in range(-SPREAD - 1, SPREAD + 2):
        target = jnp.clip(w + d, 0, wide - 1)
        send_ref[target] = jnp.zeros(send_ref.shape[1:], F32)
    offsets, rank = ranks(offset_ref, blocks)
    slot = iota((1, slots), 1)
    for b in range(blocks):
        radius = radius_ref[b : b + 1, :]
        place = offsets[b] + SPREAD
        vol = jnp.where(slot < count_ref[b], radius * radius * radius, 0.0)
        slot_ref[place, pl.ds(rank[b], 1), :] = vol
        slot_ref[place, pl.ds(CAP + rank[b], 1), :] = cell_ref[b : b + 1, :].astype(F32)
        for c in range(3):
            slot_ref[place, pl.ds((2 + c) * CAP + rank[b], 1), :] = vel_ref[c, b : b + 1, :]
    for d in range(-SPREAD, SPREAD + 1):
        for e in (-1, 0, 1):
            target = w + d - e

            @pl.when(jnp.logical_and(target >= 0, target < wide))
            def _():
                row = (e + 1) * CAP
                send_ref[target, VOL_ROW + row : VOL_ROW + row + CAP, :] = slot_ref[d + SPREAD, :CAP, :]
                send_ref[target, CELL_ROW + row : CELL_ROW + row + CAP, :] = slot_ref[d + SPREAD, CAP : 2 * CAP, :]
                if e == 0:
                    send_ref[target, VEL_ROW : VEL_ROW + 3 * CAP, :] = slot_ref[d + SPREAD, 2 * CAP : 5 * CAP, :]

    for z in range(depth):
        s_ref[z] = source_ref[z] + before_ref[z] * (1.0 / step_duration)

    for turn, ref in enumerate((edge_ref, other_edge_ref)):
        upward = w % 2 == turn
        for z in range(REACH):
            ref[z] = jnp.where(upward, s_ref[depth - REACH + z], s_ref[z])


def cell_rows(cell_row):
    cell = cell_row.astype(jnp.int32)
    return cell >> 7, cell & 127


def pieces_of(value):
    high = value.astype(BF16).astype(F32)
    return high, value - high


def contract(lhs, rhs):
    return lax.dot_general(lhs, rhs, (((1,), (1,)), ((), ())), preferred_element_type=F32)


def solid_of(vols, cells, first, rows):
    total = jnp.zeros((2 * rows, 128), F32)
    place = iota((rows, 128), 0) + first
    column = iota((128, 128), 0)
    for pair in range(0, len(vols), 2):
        left, right = [], []
        for k in range(pair, min(pair + 2, len(vols))):
            zy, x = cell_rows(cells[k])
            here = place == zy
            high, low = pieces_of(vols[k])
            left.append(
                jnp.concatenate([jnp.where(here, high, 0.0), jnp.where(here, low, 0.0)], axis=0).astype(BF16)
            )
            right.append(jnp.where(column == x, 1.0, 0.0).astype(BF16))
        total = total + contract(jnp.concatenate(left, axis=1), jnp.concatenate(right, axis=1))
    return total[:rows] + total[rows:]


def void_kernel(wide, recv_ref, edge_ref, other_edge_ref, s_ref, window_ref, rows_ref):
    w = lax.axis_index("wide")
    depth, lanes, _ = s_ref.shape
    cells = depth * lanes
    rows_ref[...] = jnp.zeros(rows_ref.shape, F32)
    for e in (-1, 0, 1):
        vols, codes = [], []
        for g in range(GROUPS):
            source = w + e - (g - SPREAD)
            inside = jnp.logical_and(source >= 0, source < wide)
            source = jnp.clip(source, 0, wide - 1)
            row = (e + 1) * CAP
            for r in range(CAP):
                k = g * CAP + r
                vol = jnp.where(inside, recv_ref[source, VOL_ROW + row + r : VOL_ROW + row + r + 1, :], 0.0)
                code = recv_ref[source, CELL_ROW + row + r : CELL_ROW + row + r + 1, :]
                vols.append(vol)
                codes.append(code)
                if e == 0:
                    rows_ref[0, k : k + 1, :] = vol
                    rows_ref[1, k : k + 1, :] = code
                    for c in range(3):
                        at = VEL_ROW + c * CAP + r
                        rows_ref[2 + c, k : k + 1, :] = recv_ref[source, at : at + 1, :]
        low = depth - HALO if e < 0 else 0
        layers = depth if e == 0 else HALO
        first = 0 if e >= 0 else (low * lanes) // 16 * 16
        count = cells if e == 0 else -(-(layers * lanes + (low * lanes - first)) // 16) * 16
        solid = solid_of(vols, codes, first, count)
        void = 1.0 - solid_most * solid / (1.0 + solid)
        exists = jnp.logical_and(w + e >= 0, w + e < wide)
        void = jnp.where(exists, void, 0.0)
        base = HALO + (e * HALO if e < 0 else e * depth)
        for z in range(layers):
            start = (low + z) * lanes - first
            window_ref[base + z] = void[start : start + lanes]
    voids = depth + 2 * HALO
    for z in range(depth):
        window_ref[voids + REACH + z] = s_ref[z]
    for e in (-1, 1):
        beside = w + e
        exists = jnp.logical_and(beside >= 0, beside < wide)
        turn = w % 2 == (0 if e > 0 else 1)
        for z in range(REACH):
            part = jnp.where(turn, edge_ref[z], other_edge_ref[z])
            at = voids + (z if e < 0 else REACH + depth + z)
            window_ref[at] = jnp.where(exists, part, 0.0)


def gather_cells(refs, zy, x, rows):
    found = [jnp.zeros(zy.shape, F32) for _ in refs]
    for row in range(rows):
        here = zy == row
        for i, ref in enumerate(refs):
            source = jnp.broadcast_to(ref(row), zy.shape)
            found[i] = jnp.where(here, jnp.take_along_axis(source, x, axis=1), found[i])
    return found


def drag_kernel(window_ref, rows_ref, gas_ref, drag_ref, base_ref):
    _, depth, lanes, _ = gas_ref.shape
    cells = depth * lanes
    vol = rows_ref[0]
    zy, x = cell_rows(rows_ref[1])

    def table(c):
        return lambda row: gas_ref[c, row // lanes, row % lanes : row % lanes + 1, :]

    def voids(row):
        return window_ref[HALO + row // lanes, row % lanes : row % lanes + 1, :]

    gas_z, gas_y, gas_x, void = gather_cells([table(0), table(1), table(2), voids], zy, x, cells)
    slips = [gas_z - rows_ref[2], gas_y - rows_ref[3], gas_x - rows_ref[4]]
    speed = jnp.sqrt(slips[0] * slips[0] + slips[1] * slips[1] + slips[2] * slips[2])
    scale = vol * (drag_base + drag_slope * speed) * jnp.exp(-void_power * jnp.log(void))
    drags = [scale * slip for slip in slips]
    for c in range(3):
        drag_ref[c] = drags[c]
    split = []
    for c in range(3):
        split += list(pieces_of(drags[c]))
    total = jnp.zeros((6 * cells, 128), F32)
    place = iota((cells, 128), 0)
    column = iota((128, 128), 0)
    for pair in range(0, vol.shape[0], 2):
        left, right = [], []
        for k in range(pair, pair + 2):
            here = place == zy[k : k + 1]
            left.append(
                jnp.concatenate([jnp.where(here, part[k : k + 1], 0.0) for part in split], axis=0).astype(BF16)
            )
            right.append(jnp.where(column == x[k : k + 1], 1.0, 0.0).astype(BF16))
        total = total + contract(jnp.concatenate(left, axis=1), jnp.concatenate(right, axis=1))
    for z in range(depth):
        per_void = step_duration / (gas_density * window_ref[HALO + z])
        for c in range(3):
            start = 2 * c * cells + z * lanes
            given = total[start : start + lanes] + total[start + cells : start + cells + lanes]
            base_ref[c, z] = gas_ref[c, z] - per_void * given


def fill_window(pieces, spots, lanes, void_ref, source_ref):
    voids = void_ref.shape[0]
    for piece, spot in zip(pieces, spots):
        at = pl.ds(spot * lanes if isinstance(spot, int) else pl.multiple_of(spot * lanes, lanes), lanes)
        for z in range(voids):
            void_ref[z, at, :] = piece[z]
        for z in range(source_ref.shape[0]):
            source_ref[z, at, :] = piece[voids + z]


def side_masks(lanes, width):
    y, x = iota((lanes, width), 0), iota((lanes, width), 1)
    return (y >= 1, y < lanes - 1, x >= 1, x < width - 1)


def sides(value, masks, step_y, step_x):
    return (
        jnp.where(masks[0], back(value, step_y, 0), 0.0),
        jnp.where(masks[1], ahead(value, step_y, 0), 0.0),
        jnp.where(masks[2], back(value, step_x, 1), 0.0),
        jnp.where(masks[3], ahead(value, step_x, 1), 0.0),
    )


def fine_start(void_ref, source_ref, coef_ref, diag_ref, first_ref):
    layers, lanes, width = source_ref.shape
    masks = side_masks(lanes, width)
    for i in range(layers):
        p = void_ref[i + 1]
        around = (void_ref[i], void_ref[i + 2]) + sides(p, masks, 1, 1)
        sums = [p + q for q in around]
        diag = sums[0] + sums[1] + sums[2] + sums[3] + sums[4] + sums[5]
        inside = p > 0.0
        inverse = jnp.where(inside, relax_weight / jnp.where(inside, diag, 1.0), 0.0)
        for k in range(6):
            coef = sums[k] * inverse
            if k >= 2:
                coef = jnp.where(masks[k - 2], coef, 0.0)
            coef_ref[k, i] = coef
        diag_ref[i] = diag * (0.5 / relax_weight)
        first_ref[i] = (source_ref[i] - p * (1.0 / step_duration)) * inverse * 2.0


def pull(coef_ref, i, below, here, above, step_y=1, step_x=1):
    total = coef_ref[0, i] * below + coef_ref[1, i] * above
    total = total + coef_ref[2, i] * back(here, step_y, 0) + coef_ref[3, i] * ahead(here, step_y, 0)
    return total + coef_ref[4, i] * back(here, step_x, 1) + coef_ref[5, i] * ahead(here, step_x, 1)


def fine_sweep(coef_ref, first_ref, old_ref, new_ref, start, stop):
    for i in range(start, stop):
        here = old_ref[i]
        new_ref[i] = (
            (1.0 - relax_weight) * here
            + first_ref[i]
            + pull(coef_ref, i, old_ref[i - 1], here, old_ref[i + 1])
        )


def spread_matrix(rows, columns, shift):
    return jnp.where(iota((rows, columns), 1) // 2 + shift == iota((rows, columns), 0), 1.0, 0.0)


def mean_matrix(width, shift):
    return jnp.where(iota((width, width), 0) // 2 + shift == iota((width, width), 1), 0.125, 0.0)


def coarsen_kernel(wide, *refs):
    *pieces, send_ref, coef_ref, first_ref, next_ref, void_ref, source_ref, diag_ref, fold_ref = refs
    narrow = len(pieces)
    lanes = pieces[0].shape[1]
    n = lax.axis_index("narrow")
    spots = [n, 1 - n] if narrow == 2 else list(range(narrow))
    fill_window(pieces, spots, lanes, void_ref, source_ref)
    fine_start(void_ref, source_ref, coef_ref, diag_ref, first_ref)
    layers, width_y, width = source_ref.shape
    depth = layers - 2 * REACH
    fine_sweep(coef_ref, first_ref, first_ref, next_ref, 1, layers - 1)
    half = depth // 2
    rows = half * width_y
    for k in range(half):
        total = jnp.zeros((width_y, width), F32)
        for i in (REACH + 2 * k, REACH + 2 * k + 1):
            here = next_ref[i]
            total = total + diag_ref[i] * (
                first_ref[i]
                - relax_weight * here
                + pull(coef_ref, i, next_ref[i - 1], here, next_ref[i + 1])
            )
        fold_ref[0, k * width_y : (k + 1) * width_y, :] = total
        fold_ref[1, k * width_y : (k + 1) * width_y, :] = void_ref[HALO + 2 * k] + void_ref[HALO + 2 * k + 1]
    right = fold_ref[0, pl.ds(0, rows // 2, stride=2), :] + fold_ref[0, pl.ds(1, rows // 2, stride=2), :]
    porous = fold_ref[1, pl.ds(0, rows // 2, stride=2), :] + fold_ref[1, pl.ds(1, rows // 2, stride=2), :]
    coarse = jnp.dot(right, mean_matrix(width, 0), precision=HIGHEST, preferred_element_type=F32)
    coarse = coarse + jnp.dot(porous, mean_matrix(width, width // 2), precision=HIGHEST, preferred_element_type=F32)
    coarse_y, part_y = width_y // 2, lanes // 2
    for k in range(half):
        part = coarse[k * coarse_y : k * coarse_y + part_y]
        for i in range(1, narrow):
            start = k * coarse_y + i * part_y
            part = jnp.where(n == i, coarse[start : start + part_y], part)
        for t in range(wide):
            send_ref[t, k * part_y : (k + 1) * part_y, :] = part


def loop(count, body, size=1):
    unroll = max(1, UNROLL // size)
    if count <= unroll:
        for i in range(count):
            body(i)
        return
    while count % unroll:
        unroll //= 2

    def step(i, _):
        for j in range(unroll):
            body(i * unroll + j)
        return 0

    lax.fori_loop(0, count // unroll, step, 0)


def close_halves(ref, first_half):
    last = ref.shape[0] - 2
    half = ref.shape[2] // 2
    ref[0] = jnp.where(first_half, 0.0, pltpu.roll(ref[last], half, 1))
    ref[last + 1] = jnp.where(first_half, pltpu.roll(ref[1], half, 1), 0.0)


class Level:
    def __init__(self, index, refs):
        self.index = index
        self.step = 2 ** (index - 1)
        self.porous, self.right, self.coef, self.diag, self.scale, self.first, self.one, self.two = refs
        self.layers, lanes, width = self.right.shape
        half = width // 2
        self.size = -(-lanes // 8)
        y, x = iota((lanes, width), 0), iota((lanes, width), 1) % half
        self.first_half = iota((lanes, width), 1) < half
        self.masks = (y >= self.step, y < lanes - self.step, x >= self.step, x < half - self.step)

    def start(self):
        weight = 0.5 * 0.25**self.index
        close_halves(self.porous, self.first_half)

        def body(i):
            p = self.porous[i + 1]
            around = (self.porous[i], self.porous[i + 2]) + sides(p, self.masks, self.step, self.step)
            sums = [p + q for q in around]
            diag = sums[0] + sums[1] + sums[2] + sums[3] + sums[4] + sums[5]
            inverse = relax_weight / diag
            for k in range(6):
                coef = sums[k] * inverse
                if k >= 2:
                    coef = jnp.where(self.masks[k - 2], coef, 0.0)
                self.coef[k, i] = coef
            self.diag[i] = diag * (weight / relax_weight)
            self.scale[i] = inverse * (1.0 / weight)

        loop(self.layers, body, self.size)

    def begin(self):
        def body(i):
            value = self.right[i] * self.scale[i]
            self.first[i] = value
            self.one[i + 1] = value

        loop(self.layers, body, self.size)

    def sweep(self):
        close_halves(self.one, self.first_half)

        def body(i):
            here = self.one[i + 1]
            self.two[i + 1] = (
                (1.0 - relax_weight) * here
                + self.first[i]
                + pull(self.coef, i, self.one[i], here, self.one[i + 2], self.step, self.step)
            )

        loop(self.layers, body, self.size)
        self.one, self.two = self.two, self.one

    def residual(self, i):
        here = self.one[i + 1]
        return self.diag[i] * (
            self.first[i]
            - relax_weight * here
            + pull(self.coef, i, self.one[i], here, self.one[i + 2], self.step, self.step)
        )

    def mean(self, value):
        y, x = iota(value.shape, 0), iota(value.shape, 1)
        value = value + jnp.where(
            (y & self.step) == 0, ahead(value, self.step, 0), back(value, self.step, 0)
        )
        value = value + jnp.where(
            (x & self.step) == 0, ahead(value, self.step, 1), back(value, self.step, 1)
        )
        return value * 0.125


def coarse_cycle(levels, index):
    level = levels[index]
    level.begin()
    last = index == len(levels) - 1
    for _ in range((COARSE_SWEEPS if last else SWEEPS) - 1):
        level.sweep()
    if not last:
        under = levels[index + 1]
        close_halves(level.one, level.first_half)

        def body(i):
            under.right[i] = level.mean(level.residual(2 * i) + level.residual(2 * i + 1))

        loop(under.layers, body, level.size)
        coarse_cycle(levels, index + 1)

        def add(i):
            correction = under.one[i + 1]
            level.one[2 * i + 1] = level.one[2 * i + 1] + correction
            level.one[2 * i + 2] = level.one[2 * i + 2] + correction

        loop(under.layers, add, level.size)
        for _ in range(SWEEPS):
            level.sweep()


def solve_kernel(wide, narrow, *refs):
    part_refs, (coef_ref, first_ref, start_ref), refs = refs[:narrow], refs[narrow : narrow + 3], refs[narrow + 3 :]
    pressure_ref, slope_ref = refs[:2]
    level_refs = [refs[2 + 8 * i : 10 + 8 * i] for i in range(3)]
    one_ref, two_ref, coarse_ref, fold_ref, tilt_ref = refs[26:]
    n = lax.axis_index("narrow")
    w = lax.axis_index("wide")
    lanes = pressure_ref.shape[1]
    layers, width_y, width = first_ref.shape
    depth = layers - 2 * REACH
    half, coarse_y = depth // 2, width_y // 2
    levels = [Level(i + 1, level_refs[i]) for i in range(3)]
    top = levels[0]
    middle = width // 2

    part_y = coarse_y // narrow

    def whole(t, z):
        parts = [ref[t, z * part_y : (z + 1) * part_y, :] for ref in part_refs]
        if narrow == 2:
            parts = [jnp.where(n == 0, parts[0], parts[1]), jnp.where(n == 0, parts[1], parts[0])]
        return jnp.concatenate(parts, axis=0)

    def unpack(t):
        for z in range(half):
            low, high = whole(t, z), whole(t + wide // 2, z)
            top.right[t * half + z] = jnp.where(top.first_half, low, pltpu.roll(high, middle, 1))
            top.porous[t * half + z + 1] = jnp.where(top.first_half, pltpu.roll(low, middle, 1), high)

    loop(wide // 2, unpack, half * top.size)
    for upper, lower in ((levels[0], levels[1]), (levels[1], levels[2])):

        def narrow_down(i):
            lower.porous[i + 1] = upper.mean(upper.porous[2 * i + 1] + upper.porous[2 * i + 2])

        loop(lower.layers, narrow_down, upper.size)
    for level in levels:
        level.start()
    coarse_cycle(levels, 0)

    total = top.layers
    spans = layers // 2
    for k in range(spans):
        z = w * half - REACH // 2 + k
        inside = jnp.logical_and(z >= 0, z < 2 * total)
        z = jnp.clip(z, 0, 2 * total - 1)
        upper = z >= total
        value = top.one[jnp.where(upper, z - total, z) + 1]
        value = jnp.where(upper, pltpu.roll(value, middle, 1), value)
        coarse_ref[k * coarse_y : (k + 1) * coarse_y, :] = jnp.where(inside, value, 0.0)
    wider = jnp.dot(coarse_ref[...], spread_matrix(width, width, 0), precision=HIGHEST, preferred_element_type=F32)
    count = spans * coarse_y
    fold_ref[pl.ds(0, count, stride=2), :] = wider
    fold_ref[pl.ds(1, count, stride=2), :] = wider
    for i in range(1, layers - 1):
        k = i // 2
        correction = fold_ref[k * width_y : (k + 1) * width_y, :]
        one_ref[i] = start_ref[i] + correction
    fine_sweep(coef_ref, first_ref, one_ref, two_ref, 2, layers - 2)
    fine_sweep(coef_ref, first_ref, two_ref, one_ref, 3, layers - 3)

    masks = side_masks(width_y, width)
    own = pl.ds(pl.multiple_of(n * lanes, lanes), lanes)
    for z in range(depth):
        i = REACH + z
        here = one_ref[i]
        before_y, after_y, before_x, after_x = sides(here, masks, 1, 1)
        tilt_ref[0, z] = 0.5 * (one_ref[i + 1] - one_ref[i - 1])
        tilt_ref[1, z] = 0.5 * (after_y - before_y)
        tilt_ref[2, z] = 0.5 * (after_x - before_x)
        pressure_ref[z] = one_ref[i, own, :]
        for c in range(3):
            slope_ref[c, z] = tilt_ref[c, z, own, :]


def force_kernel(wide, rows_ref, drag_ref, slope_ref, send_ref):
    w = lax.axis_index("wide")
    _, depth, lanes, _ = slope_ref.shape
    zy, x = cell_rows(rows_ref[1])

    def table(c):
        return lambda row: slope_ref[c, row // lanes, row % lanes : row % lanes + 1, :]

    slopes = gather_cells([table(0), table(1), table(2)], zy, x, depth * lanes)
    forces = [drag_ref[c] - rows_ref[0] * slopes[c] for c in range(3)]
    for g in range(GROUPS):
        target = w - (g - SPREAD)

        @pl.when(jnp.logical_and(target >= 0, target < wide))
        def _():
            for c in range(3):
                for r in range(CAP):
                    at = (c * CAP + r) * 128
                    send_ref[target, :, at : at + 128] = forces[c][g * CAP + r : g * CAP + r + 1]


def finish_kernel(base_ref, pressure_ref, slope_ref, pressure_out_ref, gas_ref):
    pressure_out_ref[...] = pressure_ref[...]
    gas_ref[...] = base_ref[...] - (step_duration / gas_density) * slope_ref[...]


def contact_kernel(wide, chosen, near_ref, count_ref, offset_ref, pos_ref, radius_ref, vel_ref, seat_ref, still_ref, push_ref, across_ref):
    w = lax.axis_index("wide")
    blocks, slots = radius_ref.shape
    neighbours = near_ref.shape[1]
    slot = iota((1, slots), 1)
    reach = [jnp.where(slot < count_ref[b], radius_ref[b : b + 1, :], -100.0) for b in range(blocks)]
    upright = jnp.concatenate([pos_ref[0], pos_ref[1], pos_ref[2]] + reach, axis=0).T
    for q in range(4):
        for b in range(blocks):
            at = q * blocks + b
            across_ref[q, b] = jnp.broadcast_to(upright[:, at : at + 1], (slots, slots))

    offsets, rank = ranks(offset_ref, blocks)
    factor = stiffness / (slots * (neighbours + 1))
    for b in chosen:
        at = b - chosen[0]
        mine = [jnp.broadcast_to(pos_ref[c, b : b + 1, :], (8, slots)) for c in range(3)]
        mine_radius = jnp.broadcast_to(radius_ref[b : b + 1, :], (8, slots))

        def one(k, sums):
            j = jnp.where(k < neighbours, near_ref[b, jnp.minimum(k, neighbours - 1)], b)
            sums = list(sums)
            for row in range(0, slots, 8):
                apart = [mine[c] - across_ref[c, j, row : row + 8, :] for c in range(3)]
                square = apart[0] * apart[0] + apart[1] * apart[1] + (apart[2] * apart[2] + softening * softening)
                inverse = lax.rsqrt(square)
                overlap = jnp.maximum(mine_radius + across_ref[3, j, row : row + 8, :] - square * inverse, 0.0)
                weight = overlap * inverse
                for c in range(3):
                    sums[c] = sums[c] + apart[c] * weight
            return tuple(sums)

        live = jnp.where(slot < count_ref[b], 1.0, 0.0)
        radius = radius_ref[b : b + 1, :]
        inverse = 1.0 / (particle_density * (radius * radius * radius))
        sums = lax.fori_loop(0, neighbours + 1, one, tuple(jnp.zeros((8, slots), F32) for _ in range(3)))
        for c in range(3):
            force = jnp.sum(sums[c], axis=0, keepdims=True) * factor
            push = force * inverse
            if c == 0:
                push = push + gravity
            still_ref[c, at : at + 1, :] = live * (vel_ref[c, b : b + 1, :] + step_duration * push)
        push_ref[at : at + 1, :] = live * (step_duration * inverse)
        seat_ref[0, at] = jnp.clip(w + offsets[b], 0, wide - 1)
        seat_ref[1, at] = rank[b]


def move_kernel(*refs):
    *refs, recv_ref, out_ref = refs
    b = 0
    for seat_ref, still_ref, push_ref in zip(refs[0::3], refs[1::3], refs[2::3]):
        for at in range(push_ref.shape[0]):
            for c in range(3):
                start = pl.multiple_of((c * CAP + seat_ref[1, at]) * 128, 128)
                fluid = recv_ref[seat_ref[0, at], :, pl.ds(start, 128)]
                out_ref[c, b : b + 1, :] = still_ref[c, at : at + 1, :] + push_ref[at : at + 1, :] * fluid
            b += 1


def share(block, narrow):
    if narrow == 2:
        return [block, lax.ppermute(block, "narrow", [(0, 1), (1, 0)])]
    every = lax.all_gather(block, "narrow")
    return [every[i] for i in range(narrow)]


def pairs_of(count, turn):
    lower = range(turn, count - 1, 2)
    return [(i, i + 1) for i in lower] + [(i + 1, i) for i in lower]


def local(
    particle_position,
    particle_velocity,
    radius,
    block_live_count,
    cell_index,
    block_offset,
    neighbours,
    gas_velocity,
    pressure_source,
    void_before,
):
    wide, narrow = lax.axis_size("wide"), lax.axis_size("narrow")
    blocks, slots = radius.shape
    depth, lanes, width = pressure_source.shape
    width_y = lanes * narrow
    voids, layers = depth + 2 * HALO, depth + 2 * REACH
    half, coarse_y = depth // 2, width_y // 2
    slot_rows = -(-GROUPS * CAP // 8) * 8

    send, source, edge, other_edge = call(
        functools.partial(pack_kernel, wide),
        (f32s(wide, SEND_ROWS, width), f32s(depth, lanes, width), f32s(REACH, lanes, width), f32s(REACH, lanes, width)),
        [SMEM, SMEM] + [VMEM] * 5,
        (VMEM,) * 4,
        [pltpu.VMEM((GROUPS, -(-5 * CAP // 8) * 8, slots), F32)],
        spare=VMEM_MOST,
    )(block_offset, block_live_count, radius, particle_velocity, cell_index, pressure_source, void_before)
    recv = lax.all_to_all(send, "wide", 0, 0)
    edges = [lax.ppermute(part, "wide", pairs_of(wide, turn)) for turn, part in enumerate((edge, other_edge))]

    def contact(chosen):
        count = len(chosen)
        return call(
            functools.partial(contact_kernel, wide, chosen),
            (jax.ShapeDtypeStruct((2, count), jnp.int32), f32s(3, count, slots), f32s(count, slots)),
            [SMEM, SMEM, SMEM, VMEM, VMEM, VMEM],
            (SMEM, VMEM, VMEM),
            [pltpu.VMEM((4, blocks, slots, slots), F32)],
            flops=28 * 128 * 128 * 20,
        )(neighbours, block_live_count, block_offset, particle_position, radius, particle_velocity)

    early = blocks * 3 // 8
    recv, moved = lax.optimization_barrier((recv, contact(range(early))))
    window, rows = call(
        functools.partial(void_kernel, wide),
        (f32s(voids + layers, lanes, width), f32s(5, slot_rows, slots)),
        [VMEM] * 4,
        (VMEM, VMEM),
    )(recv, *edges, source)
    pieces = share(window, narrow)

    plane = (layers, width_y, width)
    coarse, coefs, first, iterate = call(
        functools.partial(coarsen_kernel, wide),
        (f32s(wide, half * lanes // 2, width), f32s(6, *plane), f32s(*plane), f32s(*plane)),
        [VMEM] * len(pieces),
        (VMEM,) * 4,
        [
            pltpu.VMEM((voids, width_y, width), F32),
            pltpu.VMEM(plane, F32),
            pltpu.VMEM(plane, F32),
            pltpu.VMEM((2, half * width_y, width), F32),
        ],
    )(*pieces)
    gathered = lax.all_to_all(coarse, "wide", 0, 0)

    drag, base = call(
        drag_kernel,
        (f32s(3, slot_rows, slots), f32s(3, depth, lanes, width)),
        [VMEM] * 3,
        (VMEM, VMEM),
        flops=10_000_000,
    )(window, rows, gas_velocity)

    gathered, moved_too = lax.optimization_barrier((gathered, contact(range(early, blocks))))
    parts = share(gathered, narrow)

    level_scratch = []
    for index in range(3):
        count = wide * half // 2 >> index
        body = pltpu.VMEM((count, coarse_y, width), F32)
        edged = pltpu.VMEM((count + 2, coarse_y, width), F32)
        level_scratch += [edged, body, pltpu.VMEM((6, count, coarse_y, width), F32), body, body, body, edged, edged]
    pressure, slope = call(
        functools.partial(solve_kernel, wide, narrow),
        (f32s(depth, lanes, width), f32s(3, depth, lanes, width)),
        [VMEM] * (narrow + 3),
        (VMEM,) * 2,
        level_scratch
        + [pltpu.VMEM(plane, F32), pltpu.VMEM(plane, F32)]
        + [
            pltpu.VMEM((layers // 2 * coarse_y, width), F32),
            pltpu.VMEM((layers // 2 * width_y, width), F32),
            pltpu.VMEM((3, depth, width_y, width), F32),
        ],
    )(*parts, coefs, first, iterate)
    returning = call(
        functools.partial(force_kernel, wide),
        f32s(wide, 1, 3 * CAP * slots),
        [VMEM] * 3,
        VMEM,
    )(rows, drag, slope)
    returned = lax.all_to_all(returning, "wide", 0, 0)
    pressure, gas_next = call(
        finish_kernel,
        (f32s(depth, lanes, width), f32s(3, depth, lanes, width)),
        [VMEM] * 3,
        (VMEM,) * 2,
        flops=5_000_000,
    )(base, pressure, slope)
    returned, pressure, gas_next = lax.optimization_barrier((returned, pressure, gas_next))

    updated = call(
        move_kernel,
        f32s(3, blocks, slots),
        [SMEM, VMEM, VMEM] * 2 + [VMEM],
        VMEM,
    )(*moved, *moved_too, returned)
    return (pressure, gas_next, updated)


def solution(mesh):
    placed = (
        P(None, ("wide", "narrow"), None),
        P(None, ("wide", "narrow"), None),
        P(("wide", "narrow"), None),
        P(("wide", "narrow")),
        P(("wide", "narrow"), None),
        P(("wide", "narrow")),
        P(("wide", "narrow"), None),
        P(None, "wide", "narrow", None),
        P("wide", "narrow", None),
        P("wide", "narrow", None),
    )
    return jax.shard_map(
        local,
        mesh=mesh,
        in_specs=placed,
        out_specs=(
            P("wide", "narrow", None),
            P(None, "wide", "narrow", None),
            P(None, ("wide", "narrow"), None),
        ),
        check_vma=False,
    )
```

```python
import functools
import math

import jax
import jax.numpy as jnp
from jax import lax
from jax.experimental import pallas as pl
from jax.experimental.pallas import tpu as pltpu
from jax.sharding import PartitionSpec as P

SPREAD = 2
SWEEPS = 2
COARSE_SWEEPS = 4
CAP = 3
GROUPS = 2 * SPREAD + 1
HALO = 5
REACH = 4

relax_weight = 0.8
solid_most = 0.6
void_power = 2.65
drag_base = 0.5
drag_slope = 0.5
stiffness = 16.0
softening = 0.1
particle_density = 2.0
gas_density = 1.0
step_duration = 0.25
gravity = -1.0

F32 = jnp.float32
BF16 = jnp.bfloat16
VMEM = pl.BlockSpec(memory_space=pltpu.VMEM)
SMEM = pl.BlockSpec(memory_space=pltpu.SMEM)
HIGHEST = lax.Precision.HIGHEST
VOL_ROW = 0
CELL_ROW = 3 * CAP
VEL_ROW = 6 * CAP
SEND_ROWS = -(-9 * CAP // 8) * 8
UNROLL = 32
VMEM_SPARE = 4 * 1024 * 1024
VMEM_MOST = 60 * 1024 * 1024


def call(kernel, out_shape, in_specs, out_specs, scratch=(), flops=0, spare=VMEM_SPARE):
    def run(*args):
        held = [*args, *jax.tree.leaves(out_shape), *scratch]
        need = sum(4 * math.prod(array.shape) for array in held)
        return pl.pallas_call(
            kernel,
            out_shape=out_shape,
            in_specs=in_specs,
            out_specs=out_specs,
            scratch_shapes=list(scratch),
            compiler_params=pltpu.CompilerParams(vmem_limit_bytes=min(2 * need + spare, VMEM_MOST)),
            cost_estimate=pl.CostEstimate(flops=flops, bytes_accessed=1 << 18, transcendentals=0),
        )(*args)

    return run


def f32s(*shape):
    return jax.ShapeDtypeStruct(shape, F32)


def iota(shape, dim):
    return lax.broadcasted_iota(jnp.int32, shape, dim)


def back(value, step, axis):
    return pltpu.roll(value, step, axis)


def ahead(value, step, axis):
    return pltpu.roll(value, value.shape[axis] - step, axis)


def ranks(offset_ref, count):
    offsets = [offset_ref[i] for i in range(count)]
    found = []
    for i in range(count):
        rank = 0
        for j in range(i):
            rank = rank + jnp.where(offsets[j] == offsets[i], 1, 0)
        found.append(rank)
    return offsets, found


def pack_kernel(wide, offset_ref, count_ref, radius_ref, vel_ref, cell_ref, source_ref, before_ref, send_ref, s_ref, edge_ref, other_edge_ref, slot_ref):
    w = lax.axis_index("wide")
    blocks, slots = radius_ref.shape
    depth, lanes, _ = source_ref.shape
    slot_ref[...] = jnp.zeros(slot_ref.shape, F32)
    for d in range(-SPREAD - 1, SPREAD + 2):
        target = jnp.clip(w + d, 0, wide - 1)
        send_ref[target] = jnp.zeros(send_ref.shape[1:], F32)
    offsets, rank = ranks(offset_ref, blocks)
    slot = iota((1, slots), 1)
    for b in range(blocks):
        radius = radius_ref[b : b + 1, :]
        place = offsets[b] + SPREAD
        vol = jnp.where(slot < count_ref[b], radius * radius * radius, 0.0)
        slot_ref[place, pl.ds(rank[b], 1), :] = vol
        slot_ref[place, pl.ds(CAP + rank[b], 1), :] = cell_ref[b : b + 1, :].astype(F32)
        for c in range(3):
            slot_ref[place, pl.ds((2 + c) * CAP + rank[b], 1), :] = vel_ref[c, b : b + 1, :]
    for d in range(-SPREAD, SPREAD + 1):
        for e in (-1, 0, 1):
            target = w + d - e

            @pl.when(jnp.logical_and(target >= 0, target < wide))
            def _():
                row = (e + 1) * CAP
                send_ref[target, VOL_ROW + row : VOL_ROW + row + CAP, :] = slot_ref[d + SPREAD, :CAP, :]
                send_ref[target, CELL_ROW + row : CELL_ROW + row + CAP, :] = slot_ref[d + SPREAD, CAP : 2 * CAP, :]
                if e == 0:
                    send_ref[target, VEL_ROW : VEL_ROW + 3 * CAP, :] = slot_ref[d + SPREAD, 2 * CAP : 5 * CAP, :]

    for z in range(depth):
        s_ref[z] = source_ref[z] + before_ref[z] * (1.0 / step_duration)

    for turn, ref in enumerate((edge_ref, other_edge_ref)):
        upward = w % 2 == turn
        for z in range(REACH):
            ref[z] = jnp.where(upward, s_ref[depth - REACH + z], s_ref[z])


def cell_rows(cell_row):
    cell = cell_row.astype(jnp.int32)
    return cell >> 7, cell & 127


def pieces_of(value):
    high = value.astype(BF16).astype(F32)
    return high, value - high


def contract(lhs, rhs):
    return lax.dot_general(lhs, rhs, (((1,), (1,)), ((), ())), preferred_element_type=F32)


def solid_of(vols, cells, first, rows):
    total = jnp.zeros((2 * rows, 128), F32)
    place = iota((rows, 128), 0) + first
    column = iota((128, 128), 0)
    for pair in range(0, len(vols), 2):
        left, right = [], []
        for k in range(pair, min(pair + 2, len(vols))):
            zy, x = cell_rows(cells[k])
            here = place == zy
            high, low = pieces_of(vols[k])
            left.append(
                jnp.concatenate([jnp.where(here, high, 0.0), jnp.where(here, low, 0.0)], axis=0).astype(BF16)
            )
            right.append(jnp.where(column == x, 1.0, 0.0).astype(BF16))
        total = total + contract(jnp.concatenate(left, axis=1), jnp.concatenate(right, axis=1))
    return total[:rows] + total[rows:]


def void_kernel(wide, recv_ref, edge_ref, other_edge_ref, s_ref, window_ref, rows_ref):
    w = lax.axis_index("wide")
    depth, lanes, _ = s_ref.shape
    cells = depth * lanes
    rows_ref[...] = jnp.zeros(rows_ref.shape, F32)
    for e in (-1, 0, 1):
        vols, codes = [], []
        for g in range(GROUPS):
            source = w + e - (g - SPREAD)
            inside = jnp.logical_and(source >= 0, source < wide)
            source = jnp.clip(source, 0, wide - 1)
            row = (e + 1) * CAP
            for r in range(CAP):
                k = g * CAP + r
                vol = jnp.where(inside, recv_ref[source, VOL_ROW + row + r : VOL_ROW + row + r + 1, :], 0.0)
                code = recv_ref[source, CELL_ROW + row + r : CELL_ROW + row + r + 1, :]
                vols.append(vol)
                codes.append(code)
                if e == 0:
                    rows_ref[0, k : k + 1, :] = vol
                    rows_ref[1, k : k + 1, :] = code
                    for c in range(3):
                        at = VEL_ROW + c * CAP + r
                        rows_ref[2 + c, k : k + 1, :] = recv_ref[source, at : at + 1, :]
        low = depth - HALO if e < 0 else 0
        layers = depth if e == 0 else HALO
        first = 0 if e >= 0 else (low * lanes) // 16 * 16
        count = cells if e == 0 else -(-(layers * lanes + (low * lanes - first)) // 16) * 16
        solid = solid_of(vols, codes, first, count)
        void = 1.0 - solid_most * solid / (1.0 + solid)
        exists = jnp.logical_and(w + e >= 0, w + e < wide)
        void = jnp.where(exists, void, 0.0)
        base = HALO + (e * HALO if e < 0 else e * depth)
        for z in range(layers):
            start = (low + z) * lanes - first
            window_ref[base + z] = void[start : start + lanes]
    voids = depth + 2 * HALO
    for z in range(depth):
        window_ref[voids + REACH + z] = s_ref[z]
    for e in (-1, 1):
        beside = w + e
        exists = jnp.logical_and(beside >= 0, beside < wide)
        turn = w % 2 == (0 if e > 0 else 1)
        for z in range(REACH):
            part = jnp.where(turn, edge_ref[z], other_edge_ref[z])
            at = voids + (z if e < 0 else REACH + depth + z)
            window_ref[at] = jnp.where(exists, part, 0.0)


def gather_cells(refs, zy, x, rows):
    found = [jnp.zeros(zy.shape, F32) for _ in refs]
    for row in range(rows):
        here = zy == row
        for i, ref in enumerate(refs):
            source = jnp.broadcast_to(ref(row), zy.shape)
            found[i] = jnp.where(here, jnp.take_along_axis(source, x, axis=1), found[i])
    return found


def drag_kernel(window_ref, rows_ref, gas_ref, drag_ref, base_ref):
    _, depth, lanes, _ = gas_ref.shape
    cells = depth * lanes
    vol = rows_ref[0]
    zy, x = cell_rows(rows_ref[1])

    def table(c):
        return lambda row: gas_ref[c, row // lanes, row % lanes : row % lanes + 1, :]

    def voids(row):
        return window_ref[HALO + row // lanes, row % lanes : row % lanes + 1, :]

    gas_z, gas_y, gas_x, void = gather_cells([table(0), table(1), table(2), voids], zy, x, cells)
    slips = [gas_z - rows_ref[2], gas_y - rows_ref[3], gas_x - rows_ref[4]]
    speed = jnp.sqrt(slips[0] * slips[0] + slips[1] * slips[1] + slips[2] * slips[2])
    scale = vol * (drag_base + drag_slope * speed) * jnp.exp(-void_power * jnp.log(void))
    drags = [scale * slip for slip in slips]
    for c in range(3):
        drag_ref[c] = drags[c]
    split = []
    for c in range(3):
        split += list(pieces_of(drags[c]))
    total = jnp.zeros((6 * cells, 128), F32)
    place = iota((cells, 128), 0)
    column = iota((128, 128), 0)
    for pair in range(0, vol.shape[0], 2):
        left, right = [], []
        for k in range(pair, pair + 2):
            here = place == zy[k : k + 1]
            left.append(
                jnp.concatenate([jnp.where(here, part[k : k + 1], 0.0) for part in split], axis=0).astype(BF16)
            )
            right.append(jnp.where(column == x[k : k + 1], 1.0, 0.0).astype(BF16))
        total = total + contract(jnp.concatenate(left, axis=1), jnp.concatenate(right, axis=1))
    for z in range(depth):
        per_void = step_duration / (gas_density * window_ref[HALO + z])
        for c in range(3):
            start = 2 * c * cells + z * lanes
            given = total[start : start + lanes] + total[start + cells : start + cells + lanes]
            base_ref[c, z] = gas_ref[c, z] - per_void * given


def fill_window(pieces, spots, lanes, void_ref, source_ref):
    voids = void_ref.shape[0]
    for piece, spot in zip(pieces, spots):
        at = pl.ds(spot * lanes if isinstance(spot, int) else pl.multiple_of(spot * lanes, lanes), lanes)
        for z in range(voids):
            void_ref[z, at, :] = piece[z]
        for z in range(source_ref.shape[0]):
            source_ref[z, at, :] = piece[voids + z]


def side_masks(lanes, width):
    y, x = iota((lanes, width), 0), iota((lanes, width), 1)
    return (y >= 1, y < lanes - 1, x >= 1, x < width - 1)


def sides(value, masks, step_y, step_x):
    return (
        jnp.where(masks[0], back(value, step_y, 0), 0.0),
        jnp.where(masks[1], ahead(value, step_y, 0), 0.0),
        jnp.where(masks[2], back(value, step_x, 1), 0.0),
        jnp.where(masks[3], ahead(value, step_x, 1), 0.0),
    )


def fine_start(void_ref, source_ref, coef_ref, diag_ref, first_ref):
    layers, lanes, width = source_ref.shape
    masks = side_masks(lanes, width)
    for i in range(layers):
        p = void_ref[i + 1]
        around = (void_ref[i], void_ref[i + 2]) + sides(p, masks, 1, 1)
        sums = [p + q for q in around]
        diag = sums[0] + sums[1] + sums[2] + sums[3] + sums[4] + sums[5]
        inside = p > 0.0
        inverse = jnp.where(inside, relax_weight / jnp.where(inside, diag, 1.0), 0.0)
        for k in range(6):
            coef = sums[k] * inverse
            if k >= 2:
                coef = jnp.where(masks[k - 2], coef, 0.0)
            coef_ref[k, i] = coef
        diag_ref[i] = diag * (0.5 / relax_weight)
        first_ref[i] = (source_ref[i] - p * (1.0 / step_duration)) * inverse * 2.0


def pull(coef_ref, i, below, here, above, step_y=1, step_x=1):
    total = coef_ref[0, i] * below + coef_ref[1, i] * above
    total = total + coef_ref[2, i] * back(here, step_y, 0) + coef_ref[3, i] * ahead(here, step_y, 0)
    return total + coef_ref[4, i] * back(here, step_x, 1) + coef_ref[5, i] * ahead(here, step_x, 1)


def fine_sweep(coef_ref, first_ref, old_ref, new_ref, start, stop):
    for i in range(start, stop):
        here = old_ref[i]
        new_ref[i] = (
            (1.0 - relax_weight) * here
            + first_ref[i]
            + pull(coef_ref, i, old_ref[i - 1], here, old_ref[i + 1])
        )


def spread_matrix(rows, columns, shift):
    return jnp.where(iota((rows, columns), 1) // 2 + shift == iota((rows, columns), 0), 1.0, 0.0)


def mean_matrix(width, shift):
    return jnp.where(iota((width, width), 0) // 2 + shift == iota((width, width), 1), 0.125, 0.0)


def coarsen_kernel(wide, *refs):
    *pieces, send_ref, coef_ref, first_ref, next_ref, void_ref, source_ref, diag_ref, fold_ref = refs
    narrow = len(pieces)
    lanes = pieces[0].shape[1]
    n = lax.axis_index("narrow")
    spots = [n, 1 - n] if narrow == 2 else list(range(narrow))
    fill_window(pieces, spots, lanes, void_ref, source_ref)
    fine_start(void_ref, source_ref, coef_ref, diag_ref, first_ref)
    layers, width_y, width = source_ref.shape
    depth = layers - 2 * REACH
    fine_sweep(coef_ref, first_ref, first_ref, next_ref, 1, layers - 1)
    half = depth // 2
    rows = half * width_y
    for k in range(half):
        total = jnp.zeros((width_y, width), F32)
        for i in (REACH + 2 * k, REACH + 2 * k + 1):
            here = next_ref[i]
            total = total + diag_ref[i] * (
                first_ref[i]
                - relax_weight * here
                + pull(coef_ref, i, next_ref[i - 1], here, next_ref[i + 1])
            )
        fold_ref[0, k * width_y : (k + 1) * width_y, :] = total
        fold_ref[1, k * width_y : (k + 1) * width_y, :] = void_ref[HALO + 2 * k] + void_ref[HALO + 2 * k + 1]
    right = fold_ref[0, pl.ds(0, rows // 2, stride=2), :] + fold_ref[0, pl.ds(1, rows // 2, stride=2), :]
    porous = fold_ref[1, pl.ds(0, rows // 2, stride=2), :] + fold_ref[1, pl.ds(1, rows // 2, stride=2), :]
    coarse = jnp.dot(right, mean_matrix(width, 0), precision=HIGHEST, preferred_element_type=F32)
    coarse = coarse + jnp.dot(porous, mean_matrix(width, width // 2), precision=HIGHEST, preferred_element_type=F32)
    coarse_y, part_y = width_y // 2, lanes // 2
    for k in range(half):
        part = coarse[k * coarse_y : k * coarse_y + part_y]
        for i in range(1, narrow):
            start = k * coarse_y + i * part_y
            part = jnp.where(n == i, coarse[start : start + part_y], part)
        for t in range(wide):
            send_ref[t, k * part_y : (k + 1) * part_y, :] = part


def loop(count, body, size=1):
    unroll = max(1, UNROLL // size)
    if count <= unroll:
        for i in range(count):
            body(i)
        return
    while count % unroll:
        unroll //= 2

    def step(i, _):
        for j in range(unroll):
            body(i * unroll + j)
        return 0

    lax.fori_loop(0, count // unroll, step, 0)


def close_halves(ref, first_half):
    last = ref.shape[0] - 2
    half = ref.shape[2] // 2
    ref[0] = jnp.where(first_half, 0.0, pltpu.roll(ref[last], half, 1))
    ref[last + 1] = jnp.where(first_half, pltpu.roll(ref[1], half, 1), 0.0)


class Level:
    def __init__(self, index, refs):
        self.index = index
        self.step = 2 ** (index - 1)
        self.porous, self.right, self.coef, self.diag, self.scale, self.first, self.one, self.two = refs
        self.layers, lanes, width = self.right.shape
        half = width // 2
        self.size = -(-lanes // 8)
        y, x = iota((lanes, width), 0), iota((lanes, width), 1) % half
        self.first_half = iota((lanes, width), 1) < half
        self.masks = (y >= self.step, y < lanes - self.step, x >= self.step, x < half - self.step)

    def start(self):
        weight = 0.5 * 0.25**self.index
        close_halves(self.porous, self.first_half)

        def body(i):
            p = self.porous[i + 1]
            around = (self.porous[i], self.porous[i + 2]) + sides(p, self.masks, self.step, self.step)
            sums = [p + q for q in around]
            diag = sums[0] + sums[1] + sums[2] + sums[3] + sums[4] + sums[5]
            inverse = relax_weight / diag
            for k in range(6):
                coef = sums[k] * inverse
                if k >= 2:
                    coef = jnp.where(self.masks[k - 2], coef, 0.0)
                self.coef[k, i] = coef
            self.diag[i] = diag * (weight / relax_weight)
            self.scale[i] = inverse * (1.0 / weight)

        loop(self.layers, body, self.size)

    def begin(self):
        def body(i):
            value = self.right[i] * self.scale[i]
            self.first[i] = value
            self.one[i + 1] = value

        loop(self.layers, body, self.size)

    def sweep(self):
        close_halves(self.one, self.first_half)

        def body(i):
            here = self.one[i + 1]
            self.two[i + 1] = (
                (1.0 - relax_weight) * here
                + self.first[i]
                + pull(self.coef, i, self.one[i], here, self.one[i + 2], self.step, self.step)
            )

        loop(self.layers, body, self.size)
        self.one, self.two = self.two, self.one

    def residual(self, i):
        here = self.one[i + 1]
        return self.diag[i] * (
            self.first[i]
            - relax_weight * here
            + pull(self.coef, i, self.one[i], here, self.one[i + 2], self.step, self.step)
        )

    def mean(self, value):
        y, x = iota(value.shape, 0), iota(value.shape, 1)
        value = value + jnp.where(
            (y & self.step) == 0, ahead(value, self.step, 0), back(value, self.step, 0)
        )
        value = value + jnp.where(
            (x & self.step) == 0, ahead(value, self.step, 1), back(value, self.step, 1)
        )
        return value * 0.125


def coarse_cycle(levels, index):
    level = levels[index]
    level.begin()
    last = index == len(levels) - 1
    for _ in range((COARSE_SWEEPS if last else SWEEPS) - 1):
        level.sweep()
    if not last:
        under = levels[index + 1]
        close_halves(level.one, level.first_half)

        def body(i):
            under.right[i] = level.mean(level.residual(2 * i) + level.residual(2 * i + 1))

        loop(under.layers, body, level.size)
        coarse_cycle(levels, index + 1)

        def add(i):
            correction = under.one[i + 1]
            level.one[2 * i + 1] = level.one[2 * i + 1] + correction
            level.one[2 * i + 2] = level.one[2 * i + 2] + correction

        loop(under.layers, add, level.size)
        for _ in range(SWEEPS):
            level.sweep()


def solve_kernel(wide, narrow, *refs):
    part_refs, (coef_ref, first_ref, start_ref), refs = refs[:narrow], refs[narrow : narrow + 3], refs[narrow + 3 :]
    pressure_ref, slope_ref = refs[:2]
    level_refs = [refs[2 + 8 * i : 10 + 8 * i] for i in range(3)]
    one_ref, two_ref, coarse_ref, fold_ref, tilt_ref = refs[26:]
    n = lax.axis_index("narrow")
    w = lax.axis_index("wide")
    lanes = pressure_ref.shape[1]
    layers, width_y, width = first_ref.shape
    depth = layers - 2 * REACH
    half, coarse_y = depth // 2, width_y // 2
    levels = [Level(i + 1, level_refs[i]) for i in range(3)]
    top = levels[0]
    middle = width // 2

    part_y = coarse_y // narrow

    def whole(t, z):
        parts = [ref[t, z * part_y : (z + 1) * part_y, :] for ref in part_refs]
        if narrow == 2:
            parts = [jnp.where(n == 0, parts[0], parts[1]), jnp.where(n == 0, parts[1], parts[0])]
        return jnp.concatenate(parts, axis=0)

    def unpack(t):
        for z in range(half):
            low, high = whole(t, z), whole(t + wide // 2, z)
            top.right[t * half + z] = jnp.where(top.first_half, low, pltpu.roll(high, middle, 1))
            top.porous[t * half + z + 1] = jnp.where(top.first_half, pltpu.roll(low, middle, 1), high)

    loop(wide // 2, unpack, half * top.size)
    for upper, lower in ((levels[0], levels[1]), (levels[1], levels[2])):

        def narrow_down(i):
            lower.porous[i + 1] = upper.mean(upper.porous[2 * i + 1] + upper.porous[2 * i + 2])

        loop(lower.layers, narrow_down, upper.size)
    for level in levels:
        level.start()
    coarse_cycle(levels, 0)

    total = top.layers
    spans = layers // 2
    for k in range(spans):
        z = w * half - REACH // 2 + k
        inside = jnp.logical_and(z >= 0, z < 2 * total)
        z = jnp.clip(z, 0, 2 * total - 1)
        upper = z >= total
        value = top.one[jnp.where(upper, z - total, z) + 1]
        value = jnp.where(upper, pltpu.roll(value, middle, 1), value)
        coarse_ref[k * coarse_y : (k + 1) * coarse_y, :] = jnp.where(inside, value, 0.0)
    wider = jnp.dot(coarse_ref[...], spread_matrix(width, width, 0), precision=HIGHEST, preferred_element_type=F32)
    count = spans * coarse_y
    fold_ref[pl.ds(0, count, stride=2), :] = wider
    fold_ref[pl.ds(1, count, stride=2), :] = wider
    for i in range(1, layers - 1):
        k = i // 2
        correction = fold_ref[k * width_y : (k + 1) * width_y, :]
        one_ref[i] = start_ref[i] + correction
    fine_sweep(coef_ref, first_ref, one_ref, two_ref, 2, layers - 2)
    fine_sweep(coef_ref, first_ref, two_ref, one_ref, 3, layers - 3)

    masks = side_masks(width_y, width)
    own = pl.ds(pl.multiple_of(n * lanes, lanes), lanes)
    for z in range(depth):
        i = REACH + z
        here = one_ref[i]
        before_y, after_y, before_x, after_x = sides(here, masks, 1, 1)
        tilt_ref[0, z] = 0.5 * (one_ref[i + 1] - one_ref[i - 1])
        tilt_ref[1, z] = 0.5 * (after_y - before_y)
        tilt_ref[2, z] = 0.5 * (after_x - before_x)
        pressure_ref[z] = one_ref[i, own, :]
        for c in range(3):
            slope_ref[c, z] = tilt_ref[c, z, own, :]


def force_kernel(wide, rows_ref, drag_ref, slope_ref, send_ref):
    w = lax.axis_index("wide")
    _, depth, lanes, _ = slope_ref.shape
    zy, x = cell_rows(rows_ref[1])

    def table(c):
        return lambda row: slope_ref[c, row // lanes, row % lanes : row % lanes + 1, :]

    slopes = gather_cells([table(0), table(1), table(2)], zy, x, depth * lanes)
    forces = [drag_ref[c] - rows_ref[0] * slopes[c] for c in range(3)]
    for g in range(GROUPS):
        target = w - (g - SPREAD)

        @pl.when(jnp.logical_and(target >= 0, target < wide))
        def _():
            for c in range(3):
                for r in range(CAP):
                    at = (c * CAP + r) * 128
                    send_ref[target, :, at : at + 128] = forces[c][g * CAP + r : g * CAP + r + 1]


def finish_kernel(base_ref, pressure_ref, slope_ref, pressure_out_ref, gas_ref):
    pressure_out_ref[...] = pressure_ref[...]
    gas_ref[...] = base_ref[...] - (step_duration / gas_density) * slope_ref[...]


def contact_kernel(wide, chosen, near_ref, count_ref, offset_ref, pos_ref, radius_ref, vel_ref, seat_ref, still_ref, push_ref, across_ref):
    w = lax.axis_index("wide")
    blocks, slots = radius_ref.shape
    neighbours = near_ref.shape[1]
    slot = iota((1, slots), 1)
    reach = [jnp.where(slot < count_ref[b], radius_ref[b : b + 1, :], -100.0) for b in range(blocks)]
    upright = jnp.concatenate([pos_ref[0], pos_ref[1], pos_ref[2]] + reach, axis=0).T
    for q in range(4):
        for b in range(blocks):
            at = q * blocks + b
            across_ref[q, b] = jnp.broadcast_to(upright[:, at : at + 1], (slots, slots))

    offsets, rank = ranks(offset_ref, blocks)
    factor = stiffness / (slots * (neighbours + 1))
    for b in chosen:
        at = b - chosen[0]
        mine = [jnp.broadcast_to(pos_ref[c, b : b + 1, :], (8, slots)) for c in range(3)]
        mine_radius = jnp.broadcast_to(radius_ref[b : b + 1, :], (8, slots))

        def one(k, sums):
            j = jnp.where(k < neighbours, near_ref[b, jnp.minimum(k, neighbours - 1)], b)
            sums = list(sums)
            for row in range(0, slots, 8):
                apart = [mine[c] - across_ref[c, j, row : row + 8, :] for c in range(3)]
                square = apart[0] * apart[0] + apart[1] * apart[1] + (apart[2] * apart[2] + softening * softening)
                inverse = lax.rsqrt(square)
                overlap = jnp.maximum(mine_radius + across_ref[3, j, row : row + 8, :] - square * inverse, 0.0)
                weight = overlap * inverse
                for c in range(3):
                    sums[c] = sums[c] + apart[c] * weight
            return tuple(sums)

        live = jnp.where(slot < count_ref[b], 1.0, 0.0)
        radius = radius_ref[b : b + 1, :]
        inverse = 1.0 / (particle_density * (radius * radius * radius))
        sums = lax.fori_loop(0, neighbours + 1, one, tuple(jnp.zeros((8, slots), F32) for _ in range(3)))
        for c in range(3):
            force = jnp.sum(sums[c], axis=0, keepdims=True) * factor
            push = force * inverse
            if c == 0:
                push = push + gravity
            still_ref[c, at : at + 1, :] = live * (vel_ref[c, b : b + 1, :] + step_duration * push)
        push_ref[at : at + 1, :] = live * (step_duration * inverse)
        seat_ref[0, at] = jnp.clip(w + offsets[b], 0, wide - 1)
        seat_ref[1, at] = rank[b]


def move_kernel(*refs):
    *refs, recv_ref, out_ref = refs
    b = 0
    for seat_ref, still_ref, push_ref in zip(refs[0::3], refs[1::3], refs[2::3]):
        for at in range(push_ref.shape[0]):
            for c in range(3):
                start = pl.multiple_of((c * CAP + seat_ref[1, at]) * 128, 128)
                fluid = recv_ref[seat_ref[0, at], :, pl.ds(start, 128)]
                out_ref[c, b : b + 1, :] = still_ref[c, at : at + 1, :] + push_ref[at : at + 1, :] * fluid
            b += 1


def share(block, narrow):
    if narrow == 2:
        return [block, lax.ppermute(block, "narrow", [(0, 1), (1, 0)])]
    every = lax.all_gather(block, "narrow")
    return [every[i] for i in range(narrow)]


def pairs_of(count, turn):
    lower = range(turn, count - 1, 2)
    return [(i, i + 1) for i in lower] + [(i + 1, i) for i in lower]


def local(
    particle_position,
    particle_velocity,
    radius,
    block_live_count,
    cell_index,
    block_offset,
    neighbours,
    gas_velocity,
    pressure_source,
    void_before,
):
    wide, narrow = lax.axis_size("wide"), lax.axis_size("narrow")
    blocks, slots = radius.shape
    depth, lanes, width = pressure_source.shape
    width_y = lanes * narrow
    voids, layers = depth + 2 * HALO, depth + 2 * REACH
    half, coarse_y = depth // 2, width_y // 2
    slot_rows = -(-GROUPS * CAP // 8) * 8

    send, source, edge, other_edge = call(
        functools.partial(pack_kernel, wide),
        (f32s(wide, SEND_ROWS, width), f32s(depth, lanes, width), f32s(REACH, lanes, width), f32s(REACH, lanes, width)),
        [SMEM, SMEM] + [VMEM] * 5,
        (VMEM,) * 4,
        [pltpu.VMEM((GROUPS, -(-5 * CAP // 8) * 8, slots), F32)],
        spare=VMEM_MOST,
    )(block_offset, block_live_count, radius, particle_velocity, cell_index, pressure_source, void_before)
    recv = lax.all_to_all(send, "wide", 0, 0)
    edges = [lax.ppermute(part, "wide", pairs_of(wide, turn)) for turn, part in enumerate((edge, other_edge))]

    def contact(chosen):
        count = len(chosen)
        return call(
            functools.partial(contact_kernel, wide, chosen),
            (jax.ShapeDtypeStruct((2, count), jnp.int32), f32s(3, count, slots), f32s(count, slots)),
            [SMEM, SMEM, SMEM, VMEM, VMEM, VMEM],
            (SMEM, VMEM, VMEM),
            [pltpu.VMEM((4, blocks, slots, slots), F32)],
            flops=28 * 128 * 128 * 20,
        )(neighbours, block_live_count, block_offset, particle_position, radius, particle_velocity)

    early, late = blocks // 4, blocks * 5 // 8
    recv, moved = lax.optimization_barrier((recv, contact(range(early))))
    window, rows = call(
        functools.partial(void_kernel, wide),
        (f32s(voids + layers, lanes, width), f32s(5, slot_rows, slots)),
        [VMEM] * 4,
        (VMEM, VMEM),
    )(recv, *edges, source)
    pieces = share(window, narrow)

    plane = (layers, width_y, width)
    coarse, coefs, first, iterate = call(
        functools.partial(coarsen_kernel, wide),
        (f32s(wide, half * lanes // 2, width), f32s(6, *plane), f32s(*plane), f32s(*plane)),
        [VMEM] * len(pieces),
        (VMEM,) * 4,
        [
            pltpu.VMEM((voids, width_y, width), F32),
            pltpu.VMEM(plane, F32),
            pltpu.VMEM(plane, F32),
            pltpu.VMEM((2, half * width_y, width), F32),
        ],
    )(*pieces)
    gathered = lax.all_to_all(coarse, "wide", 0, 0)

    drag, base = call(
        drag_kernel,
        (f32s(3, slot_rows, slots), f32s(3, depth, lanes, width)),
        [VMEM] * 3,
        (VMEM, VMEM),
        flops=10_000_000,
    )(window, rows, gas_velocity)

    gathered, moved_too = lax.optimization_barrier((gathered, contact(range(early, late))))
    parts = share(gathered, narrow)

    level_scratch = []
    for index in range(3):
        count = wide * half // 2 >> index
        body = pltpu.VMEM((count, coarse_y, width), F32)
        edged = pltpu.VMEM((count + 2, coarse_y, width), F32)
        level_scratch += [edged, body, pltpu.VMEM((6, count, coarse_y, width), F32), body, body, body, edged, edged]
    pressure, slope = call(
        functools.partial(solve_kernel, wide, narrow),
        (f32s(depth, lanes, width), f32s(3, depth, lanes, width)),
        [VMEM] * (narrow + 3),
        (VMEM,) * 2,
        level_scratch
        + [pltpu.VMEM(plane, F32), pltpu.VMEM(plane, F32)]
        + [
            pltpu.VMEM((layers // 2 * coarse_y, width), F32),
            pltpu.VMEM((layers // 2 * width_y, width), F32),
            pltpu.VMEM((3, depth, width_y, width), F32),
        ],
    )(*parts, coefs, first, iterate)
    returning = call(
        functools.partial(force_kernel, wide),
        f32s(wide, 1, 3 * CAP * slots),
        [VMEM] * 3,
        VMEM,
    )(rows, drag, slope)
    returned = lax.all_to_all(returning, "wide", 0, 0)
    pressure, gas_next = call(
        finish_kernel,
        (f32s(depth, lanes, width), f32s(3, depth, lanes, width)),
        [VMEM] * 3,
        (VMEM,) * 2,
        flops=5_000_000,
    )(base, pressure, slope)
    returned, pressure, gas_next, moved_last = lax.optimization_barrier(
        (returned, pressure, gas_next, contact(range(late, blocks)))
    )

    updated = call(
        move_kernel,
        f32s(3, blocks, slots),
        [SMEM, VMEM, VMEM] * 3 + [VMEM],
        VMEM,
    )(*moved, *moved_too, *moved_last, returned)
    return (pressure, gas_next, updated)


def solution(mesh):
    placed = (
        P(None, ("wide", "narrow"), None),
        P(None, ("wide", "narrow"), None),
        P(("wide", "narrow"), None),
        P(("wide", "narrow")),
        P(("wide", "narrow"), None),
        P(("wide", "narrow")),
        P(("wide", "narrow"), None),
        P(None, "wide", "narrow", None),
        P("wide", "narrow", None),
        P("wide", "narrow", None),
    )
    return jax.shard_map(
        local,
        mesh=mesh,
        in_specs=placed,
        out_specs=(
            P("wide", "narrow", None),
            P(None, "wide", "narrow", None),
            P(None, ("wide", "narrow"), None),
        ),
        check_vma=False,
    )
```
